32 devices in a mesh: grp: 2 (over y), row: 16 (over z, x, core).
Axes of the slice: x: 2, y: 2, z: 4, core: 2. Of those that a mesh axis runs over, the one named last changes fastest.
Arguments:
- pair_acts: bfloat16 [96, 48, 128], P(('grp', 'row')), parts along dimension 0, may hold values from -24 to 24, as said below
- token_count: int32 [2], P('grp'), parts along dimension 0, may hold values from 24 to 48
- input_gain: float32 [128], replicated, may hold values from 0.1 to 1.9
- input_bias: float32 [128], replicated, may hold values from -3 to 3
- project_weight: bfloat16 [128, 64], replicated, may hold values from -0.5 to 0.5
- gate_weight: bfloat16 [128, 128], replicated, may hold values from -0.5 to 0.5
- output_norm_gain: float32 [16], replicated, may hold values from 0.1 to 1.9
- output_shift_bias: float32 [16], replicated, may hold values from -3 to 3
- output_weight: bfloat16 [16, 128], replicated, may hold values from -1.5 to 1.5
- update_grad: bfloat16 [96, 48, 128], P(('grp', 'row')), parts along dimension 0, may hold values from -6 to 6
Outputs:
- update: bfloat16 [96, 48, 128], P(('grp', 'row')), parts along dimension 0
- pair_grad: float32 [96, 48, 128], P(('grp', 'row')), parts along dimension 0
- project_grad: float32 [256, 64], P('grp'), parts along dimension 0
- gate_grad: float32 [256, 128], P('grp'), parts along dimension 0
- output_grad: float32 [32, 128], P('grp'), parts along dimension 0
The draws below stay inside these ranges and needn't reach their ends.
There are 2 independent parts, one for each index of `grp`. The reference program is written for one: setup_inputs(seed, part) draws one part's arguments, and reference() takes and returns one part's arrays. A program takes and returns all parts, laid end to end along the dimension named above; an argument that names none is the same for every part. Nothing has to cross between parts.
Inputs may be any that keep to these rules, and one draw needn't show every extreme that they name: `pair_acts`: pair activations; channel scales differ.
All inputs are finite; a program needn't handle non-finite values.
Results may differ from the reference program's by a relative error of at most 0.0085.
Values may be sent and summed in bfloat16 or wider, within the bound.
No kernel may reach another device: no remote copies, remote signals or barrier semaphores. Data moves between devices by JAX's collectives and lax.ppermute only.
A program may use at most 64 MiB of HBM per device.

```python
import math
import jax
import jax.numpy as jnp
from jax import lax

C_PAIR = 128
N = 48
HID = 16


def draw_pair_acts(key, part):
    key = jax.random.fold_in(key, 11)
    key_base, key_channel, key_site = jax.random.split(key, 3)
    channel_scale = jnp.exp(jax.random.uniform(key_channel, (C_PAIR,), jnp.float32, math.log(0.3), math.log(3.0)))
    site_scale = jnp.exp(jax.random.uniform(key_site, (N, N, 1), jnp.float32, math.log(0.5), math.log(2.0)))
    values = jnp.clip(jax.random.normal(key_base, (N, N, C_PAIR), jnp.float32), -4.0, 4.0)
    return (values * channel_scale * site_scale).astype(jnp.bfloat16)


def steps_of(rng, shape, pieces, low, high):
    def one(position, parts):
        steps = jax.random.uniform(jax.random.fold_in(jax.random.fold_in(rng, 6), position), (parts,), jnp.float32, low / len(pieces), high / len(pieces))
        return jnp.repeat(jnp.exp(steps), shape[position] // parts).reshape((-1,) + (1,) * (len(shape) - position - 1))

    level = one(*pieces[0])
    for cut in pieces[1:]:
        level = level * one(*cut)
    return level


def gaussian(stream_key, dims, deviation, most, pieces=(), kind=jnp.bfloat16):
    drawn = jax.random.normal(stream_key, dims, jnp.float32) * deviation
    if len(pieces) > 0:
        drawn = steps_of(stream_key, dims, pieces, -0.22, 0.18) * drawn
    return jnp.clip(drawn, min=-most, max=most).astype(kind)


def setup_inputs(seed: int = 0, part: int = 0) -> dict:
    splits = jax.random.split(jax.random.key(seed), 11)
    own_keys = jax.random.split(jax.random.fold_in(splits[10], part), 11)
    pair_acts = draw_pair_acts(jax.random.fold_in(jax.random.fold_in(splits[10], part), 71), part)
    token_count = jax.random.randint(own_keys[1], (1,), N // 2, N + 1).astype(jnp.int32)
    input_gain = jnp.clip(1.0 + 0.18 * jax.random.normal(splits[2], (C_PAIR,), jnp.float32), 0.1, 1.9)
    input_bias = gaussian(splits[3], (C_PAIR,), 0.5, 3.0, (), jnp.float32)
    project_weight = gaussian(splits[4], (C_PAIR, 4 * HID), C_PAIR ** -0.5, 0.5)
    gate_weight = gaussian(splits[5], (C_PAIR, C_PAIR), C_PAIR ** -0.5, 0.5)
    output_norm_gain = jnp.clip(1.0 + 0.18 * jax.random.normal(splits[6], (HID,), jnp.float32), 0.1, 1.9)
    output_shift_bias = gaussian(splits[7], (HID,), 0.5, 3.0, (), jnp.float32)
    output_weight = gaussian(splits[8], (HID, C_PAIR), HID ** -0.5, 1.5)
    update_grad = gaussian(own_keys[9], (N, N, C_PAIR), 1.0, 6.0, ((0, 16),))
    return dict(pair_acts=pair_acts, token_count=token_count, input_gain=input_gain, input_bias=input_bias, project_weight=project_weight, gate_weight=gate_weight, output_norm_gain=output_norm_gain, output_shift_bias=output_shift_bias, output_weight=output_weight, update_grad=update_grad)


def cast_to_half_width(values):
    return lax.optimization_barrier(values.astype(jnp.bfloat16))

def layer_normalize(values, norm_gain, norm_bias, reduce_axis):
    average = lax.optimization_barrier(jnp.mean(values, axis=reduce_axis, keepdims=True))
    centered = values - average
    variance = lax.optimization_barrier(jnp.mean(centered * centered, axis=reduce_axis, keepdims=True))
    inv_std = lax.rsqrt(variance + 1e-05)
    normed = centered * inv_std
    return (normed * norm_gain + norm_bias, normed, inv_std)

def norm_backward_pass(upstream, normed, inv_std, norm_gain, reduce_axis):
    scaled = upstream * norm_gain
    first = lax.optimization_barrier(jnp.mean(scaled, axis=reduce_axis, keepdims=True))
    second = lax.optimization_barrier(jnp.mean(scaled * normed, axis=reduce_axis, keepdims=True))
    return inv_std * (scaled - first - normed * second)

def reference(pair_acts, token_count, input_gain, input_bias, project_weight, gate_weight, output_norm_gain, output_shift_bias, output_weight, update_grad):
    single_float_format = jnp.float32
    length = pair_acts.shape[0]
    hidden = output_weight.shape[0]
    live = (jnp.arange(length, dtype=jnp.int32) < token_count[0]).astype(single_float_format)
    live_mask = live[:, None] * live[None, :]
    zn32, zhat, zscale = layer_normalize(pair_acts.astype(single_float_format), input_gain.astype(single_float_format), input_bias.astype(single_float_format), -1)
    normed_pair = cast_to_half_width(zn32)
    normed_wide = normed_pair.astype(single_float_format)
    projected = jnp.einsum('ikd,de->eik', normed_wide, project_weight.astype(single_float_format)).reshape(4, hidden, length, length)
    gate_left = jax.nn.sigmoid(projected[1])
    gate_right = jax.nn.sigmoid(projected[3])
    left_panel = cast_to_half_width(live_mask * gate_left * projected[0]).astype(single_float_format)
    right_panel = cast_to_half_width(live_mask * gate_right * projected[2]).astype(single_float_format)
    triangle_product = cast_to_half_width(jnp.einsum('cik,cjk->cij', left_panel, right_panel)).astype(single_float_format)
    normed_input_single, standardized_input, input_inverse_scale = layer_normalize(triangle_product, output_norm_gain.astype(single_float_format)[:, None, None], output_shift_bias.astype(single_float_format)[:, None, None], 0)
    normed_tri = cast_to_half_width(normed_input_single).astype(single_float_format)
    mixed = jnp.einsum('cij,cd->ijd', normed_tri, output_weight.astype(single_float_format))
    gate_out = jax.nn.sigmoid(jnp.einsum('ikd,de->ike', normed_wide, gate_weight.astype(single_float_format)))
    update = (gate_out * mixed).astype(jnp.bfloat16)
    cotangent = update_grad.astype(single_float_format)
    mixed_grad = cast_to_half_width(cotangent * gate_out).astype(single_float_format)
    gate_logit_grad = cast_to_half_width(cotangent * mixed * gate_out * (1.0 - gate_out)).astype(single_float_format)
    output_grad = jnp.einsum('cij,ijd->cd', normed_tri, mixed_grad) / length
    triangle_normed_gradient = jnp.einsum('ijd,cd->cij', mixed_grad, output_weight.astype(single_float_format))
    triangle_gradient = cast_to_half_width(norm_backward_pass(triangle_normed_gradient, standardized_input, input_inverse_scale, output_norm_gain.astype(single_float_format)[:, None, None], 0)).astype(single_float_format)
    left_grad = cast_to_half_width(jnp.einsum('cij,cjk->cik', triangle_gradient, right_panel)).astype(single_float_format)
    right_grad = cast_to_half_width(jnp.einsum('cij,cik->cjk', triangle_gradient, left_panel)).astype(single_float_format)
    project_terms = jnp.stack([left_grad * live_mask * gate_left, left_grad * live_mask * projected[0] * gate_left * (1.0 - gate_left), right_grad * live_mask * gate_right, right_grad * live_mask * projected[2] * gate_right * (1.0 - gate_right)])
    project_terms = cast_to_half_width(project_terms).astype(single_float_format).reshape(4 * hidden, length, length)
    project_grad = jnp.einsum('ikd,eik->de', normed_wide, project_terms) / length
    gate_grad = jnp.einsum('ikd,ike->de', normed_wide, gate_logit_grad) / length
    normed_grad = jnp.einsum('eik,de->ikd', project_terms, project_weight.astype(single_float_format)) + jnp.einsum('ike,de->ikd', gate_logit_grad, gate_weight.astype(single_float_format))
    pair_grad = norm_backward_pass(normed_grad, zhat, zscale, input_gain.astype(single_float_format), -1)
    return (update, pair_grad, project_grad, gate_grad, output_grad)
```

```python
import functools

import jax
import jax.numpy as jnp
from jax import lax
from jax.experimental import pallas as pl
from jax.experimental.pallas import tpu as pltpu
from jax.sharding import PartitionSpec as P

LANES = 128
WHOLE_BYTES = 4 << 20

NN = (((1,), (0,)), ((), ()))
NT = (((1,), (1,)), ((), ()))
TN = (((0,), (0,)), ((), ()))


def dot(a, b, dims=NN):
    return lax.dot_general(a, b, dims, preferred_element_type=jnp.float32)


def dot_split(a, b):
    high = a.astype(jnp.bfloat16)
    low = (a - high.astype(jnp.float32)).astype(jnp.bfloat16)
    return dot(high, b) + dot(low, b)


def iota(shape, dim):
    return lax.broadcasted_iota(jnp.int32, shape, dim)


def zero_one(condition):
    return jnp.where(condition, 1.0, 0.0).astype(jnp.bfloat16)


def sigmoid(v):
    return 1.0 / (1.0 + jnp.exp(-v))


def normalize(v, axis=-1):
    centered = v - jnp.mean(v, axis=axis, keepdims=True)
    s = lax.rsqrt(jnp.mean(centered * centered, axis=axis, keepdims=True) + 1e-05)
    return centered * s, s


def crop_kernel(
    n,
    hidden,
    mine_ref,
    other_ref,
    own_ref,
    count_ref,
    gain_ref,
    bias_ref,
    project_ref,
    gate_ref,
    out_gain_ref,
    out_bias_ref,
    out_weight_ref,
    update_ref,
    pair_ref,
    project_grad_ref,
    gate_grad_ref,
    out_grad_ref,
    zn_ref,
    ug_ref,
    upd_ref,
    dgo_ref,
    dp_ref,
    dpt_ref,
):
    f32, bf16 = jnp.float32, jnp.bfloat16
    per = LANES // hidden
    groups = n // per
    wide = n * hidden
    me = lax.axis_index("row")
    parity = lax.rem(me, 2)
    blocks = 2 * mine_ref.shape[0]
    rows = n // blocks
    half = rows * n
    count = count_ref[0]
    gain, bias = gain_ref[...], bias_ref[...]

    for block in range(blocks):
        swap = parity != block % 2
        for r in range(rows):
            i = block * rows + r
            g, p = i // per, i % per
            here, there = pl.ds(r * n, n), pl.ds(half + r * n, n)
            v = jnp.where(swap, other_ref[block // 2, here, :], mine_ref[block // 2, here, :])
            zhat, _ = normalize(v.astype(f32))
            zn_ref[p, pl.ds(g * n, n), :] = (zhat * gain + bias).astype(bf16)
            ug_ref[p, pl.ds(g * n, n), :] = jnp.where(
                swap, other_ref[block // 2, there, :], mine_ref[block // 2, there, :]
            )

    kinds = 4 * LANES
    a, b = iota((4 * hidden, kinds), 0), iota((4 * hidden, kinds), 1)
    spread = zero_one((a // hidden == b // LANES) & (a % hidden == b % hidden))
    tiled = dot(project_ref[...], spread).astype(bf16)
    place = (iota((LANES, kinds), 1) % LANES) // hidden
    projected = jnp.zeros((groups * n, kinds), f32)
    for p in range(per):
        projected += dot(zn_ref[p], jnp.where(place == p, tiled, jnp.zeros_like(tiled)))
    row_k = jnp.concatenate([iota((n, LANES), 0)] * groups, axis=0)
    row_g = jnp.concatenate([jnp.full((n, LANES), g * per, jnp.int32) for g in range(groups)], axis=0)
    row_i = row_g + iota((groups * n, LANES), 1) // hidden
    mask = jnp.where((row_i < count) & (row_k < count), 1.0, 0.0)
    value_left, value_right = projected[:, :LANES], projected[:, 2 * LANES : 3 * LANES]
    gate_left = sigmoid(projected[:, LANES : 2 * LANES])
    gate_right = sigmoid(projected[:, 3 * LANES :])
    mask_left, mask_right = mask * gate_left, mask * gate_right

    def lanes(flat):
        return jnp.concatenate([flat[g * n : (g + 1) * n] for g in range(groups)], axis=1)

    def flatten(rowed):
        return jnp.concatenate([rowed[:, g * LANES : (g + 1) * LANES] for g in range(groups)], axis=0)

    left = lanes((mask_left * value_left).astype(bf16))
    right = lanes((mask_right * value_right).astype(bf16))

    same = iota((LANES, wide), 0) % hidden == iota((LANES, wide), 1) % hidden
    pick = zero_one(iota((per, LANES), 0) == iota((per, LANES), 1) // hidden)
    parts = []
    for g in range(groups):
        cross = dot(right[:, g * LANES : (g + 1) * LANES], left, TN).astype(bf16)
        parts.append(dot(pick, jnp.where(same, cross, jnp.zeros_like(cross))))
    x = flatten(jnp.concatenate(parts, axis=0))

    mean = jnp.where(iota((LANES, LANES), 0) // hidden == iota((LANES, LANES), 1) // hidden, 1.0 / hidden, 0.0)
    mean = mean.astype(bf16)
    out_gain = jnp.concatenate([out_gain_ref[...]] * per, axis=1)
    out_bias = jnp.concatenate([out_bias_ref[...]] * per, axis=1)
    centered = x - dot(x.astype(bf16), mean)
    xs = lax.rsqrt(dot_split(centered * centered, mean) + 1e-05)
    xhat = centered * xs
    xn = (xhat * out_gain + out_bias).astype(bf16)

    out_weight = jnp.concatenate([out_weight_ref[...]] * per, axis=0)
    at = iota((LANES, LANES), 0) // hidden
    gate_weight = gate_ref[...]
    gate_grad = jnp.zeros((LANES, LANES), f32)
    out_grad = jnp.zeros((hidden, LANES), f32)
    dxn = jnp.zeros((groups * n, LANES), f32)
    for p in range(per):
        zn = zn_ref[p]
        weight = jnp.where(at == p, out_weight, jnp.zeros_like(out_weight))
        y = dot(xn, weight)
        go = sigmoid(dot(zn, gate_weight))
        upd_ref[p] = (go * y).astype(bf16)
        cotangent = ug_ref[p].astype(f32)
        dy = (cotangent * go).astype(bf16)
        dgo = (cotangent * y * go * (1.0 - go)).astype(bf16)
        dgo_ref[p] = dgo
        gate_grad += dot(zn, dgo, TN)
        out_grad += dot(xn, dy, TN)[p * hidden : (p + 1) * hidden]
        dxn += dot(dy, weight, NT)
    gate_grad_ref[...] = gate_grad / n
    out_grad_ref[...] = out_grad / n

    u = out_gain * dxn
    dx = xs * (u - dot_split(u, mean) - xhat * dot_split(u * xhat, mean))
    dx = lanes(dx.astype(bf16))

    repeat = zero_one(iota((LANES, per), 0) // hidden == iota((LANES, per), 1))
    dleft = jnp.zeros((n, wide), f32)
    dright = []
    for g in range(groups):
        spread_dx = dot(repeat, dx[g * per : (g + 1) * per]).astype(bf16)
        diagonal = jnp.where(same, spread_dx, jnp.zeros_like(spread_dx))
        dleft += dot(right[:, g * LANES : (g + 1) * LANES], diagonal)
        dright.append(dot(left, diagonal, NT))
    dleft = flatten(dleft.astype(bf16)).astype(f32)
    dright = jnp.concatenate(dright, axis=0).astype(bf16).astype(f32)
    dp = [
        dleft * mask_left,
        dleft * mask_left * value_left * (1.0 - gate_left),
        dright * mask_right,
        dright * mask_right * value_right * (1.0 - gate_right),
    ]
    dp = jnp.concatenate([d.astype(bf16) for d in dp], axis=1)
    dp_ref[...] = dp
    dpt_ref[...] = dp.T
    project_grad = jnp.zeros((4 * hidden, LANES), f32)
    for p in range(per):
        at_p = [dpt_ref[pl.ds(kind * LANES + p * hidden, hidden), :] for kind in range(4)]
        project_grad += dot(jnp.concatenate(at_p, axis=0), zn_ref[p])
    project_grad_ref[...] = project_grad.T / n

    place = (iota((n, kinds), 1) % LANES) // hidden
    for r in range(rows):
        i = me * rows + r
        g, p = lax.div(i, per), lax.rem(i, per)
        where = pl.ds(pl.multiple_of(g * n, 16), n)
        update_ref[r] = upd_ref[p, where, :]
        dp_row = dp_ref[where, :]
        dp_row = jnp.where(place == p, dp_row, jnp.zeros_like(dp_row))
        dzn = dot(dp_row, tiled, NT) + dot(dgo_ref[p, where, :], gate_weight, NT)
        zhat, zs = normalize(own_ref[r].astype(f32))
        u = gain * dzn
        first = jnp.mean(u, axis=-1, keepdims=True)
        second = jnp.mean(u * zhat, axis=-1, keepdims=True)
        pair_ref[r] = zs * (u - first - zhat * second)


def body_whole(
    devices,
    pair_acts,
    token_count,
    input_gain,
    input_bias,
    project_weight,
    gate_weight,
    output_norm_gain,
    output_shift_bias,
    output_weight,
    update_grad,
):
    rows, n, channels = pair_acts.shape
    hidden = output_weight.shape[0]
    half = rows * n
    chips = devices // 2
    send = jnp.concatenate(
        [pair_acts.reshape(half, channels), update_grad.reshape(half, channels)], axis=0
    )
    send = jnp.broadcast_to(send[None], (chips,) + send.shape)
    mine = lax.all_to_all(
        send,
        "row",
        split_axis=0,
        concat_axis=0,
        tiled=True,
        axis_index_groups=[[2 * chip + core for chip in range(chips)] for core in range(2)],
    )
    other = lax.ppermute(mine, "row", [(i, i ^ 1) for i in range(devices)])
    per = LANES // hidden
    tall = n // per * n
    f32, bf16 = jnp.float32, jnp.bfloat16
    vmem = pl.BlockSpec(memory_space=pltpu.VMEM)
    return pl.pallas_call(
        functools.partial(crop_kernel, n, hidden),
        out_shape=(
            jax.ShapeDtypeStruct((rows, n, channels), bf16),
            jax.ShapeDtypeStruct((rows, n, channels), f32),
            jax.ShapeDtypeStruct((channels, 4 * hidden), f32),
            jax.ShapeDtypeStruct((channels, channels), f32),
            jax.ShapeDtypeStruct((hidden, channels), f32),
        ),
        in_specs=[vmem] * 3 + [pl.BlockSpec(memory_space=pltpu.SMEM)] + [vmem] * 7,
        out_specs=(vmem,) * 5,
        scratch_shapes=[
            pltpu.VMEM((per, tall, channels), bf16),
            pltpu.VMEM((per, tall, channels), bf16),
            pltpu.VMEM((per, tall, channels), bf16),
            pltpu.VMEM((per, tall, channels), bf16),
            pltpu.VMEM((tall, 4 * LANES), bf16),
            pltpu.VMEM((4 * LANES, tall), bf16),
        ],
        compiler_params=pltpu.CompilerParams(vmem_limit_bytes=32 << 20),
    )(
        mine,
        other,
        pair_acts,
        token_count,
        input_gain[None],
        input_bias[None],
        project_weight,
        gate_weight,
        output_norm_gain[None],
        output_shift_bias[None],
        output_weight,
    )


def layer_normalize(values, norm_gain, norm_bias, reduce_axis):
    average = jnp.mean(values, axis=reduce_axis, keepdims=True)
    centered = values - average
    variance = jnp.mean(centered * centered, axis=reduce_axis, keepdims=True)
    inv_std = lax.rsqrt(variance + 1e-05)
    normed = centered * inv_std
    return (normed * norm_gain + norm_bias, normed, inv_std)


def norm_backward_pass(upstream, normed, inv_std, norm_gain, reduce_axis):
    scaled = upstream * norm_gain
    first = jnp.mean(scaled, axis=reduce_axis, keepdims=True)
    second = jnp.mean(scaled * normed, axis=reduce_axis, keepdims=True)
    return inv_std * (scaled - first - normed * second)


def body(
    pair_acts,
    token_count,
    input_gain,
    input_bias,
    project_weight,
    gate_weight,
    output_norm_gain,
    output_shift_bias,
    output_weight,
    update_grad,
):
    single_float_format = jnp.float32
    brain_float_sixteen = jnp.bfloat16
    row_count, length, channels = pair_acts.shape
    hidden = output_weight.shape[0]
    row_start = lax.axis_index("row") * row_count
    live_limit = token_count[0]
    row_live = (row_start + jnp.arange(row_count, dtype=jnp.int32) < live_limit).astype(
        single_float_format
    )
    col_live = (jnp.arange(length, dtype=jnp.int32) < live_limit).astype(single_float_format)
    live_mask = row_live[:, None] * col_live[None, :]
    zn32, zhat, zscale = layer_normalize(
        pair_acts.astype(single_float_format), input_gain, input_bias, -1
    )
    normed_pair = zn32.astype(brain_float_sixteen)
    projected = jnp.einsum(
        "rkd,de->erk", normed_pair, project_weight, preferred_element_type=single_float_format
    ).reshape(4, hidden, row_count, length)
    gate_left = jax.nn.sigmoid(projected[1])
    gate_right = jax.nn.sigmoid(projected[3])
    left_panel = (live_mask * gate_left * projected[0]).astype(brain_float_sixteen)
    right_panel = (live_mask * gate_right * projected[2]).astype(brain_float_sixteen)
    stacked = jnp.stack([left_panel, right_panel], axis=1)
    columns = lax.all_to_all(stacked, "row", split_axis=0, concat_axis=2, tiled=True)
    left_cols = columns[:, 0]
    right_cols = columns[:, 1]
    products = jnp.einsum(
        "cik,cjk->cij", left_cols, right_cols, preferred_element_type=single_float_format
    ).astype(brain_float_sixteen)
    triangle_product = lax.all_to_all(products, "row", split_axis=1, concat_axis=0, tiled=True)
    normed_input_single, standardized_input, input_inverse_scale = layer_normalize(
        triangle_product.astype(single_float_format),
        output_norm_gain[:, None, None],
        output_shift_bias[:, None, None],
        0,
    )
    normed_tri = normed_input_single.astype(brain_float_sixteen)
    mixed = jnp.einsum(
        "crk,cd->rkd", normed_tri, output_weight, preferred_element_type=single_float_format
    )
    gate_out = jax.nn.sigmoid(
        jnp.einsum(
            "rkd,de->rke", normed_pair, gate_weight, preferred_element_type=single_float_format
        )
    )
    update = (gate_out * mixed).astype(brain_float_sixteen)
    cotangent = update_grad.astype(single_float_format)
    mixed_grad = (cotangent * gate_out).astype(brain_float_sixteen)
    gate_logit_grad = (cotangent * mixed * gate_out * (1.0 - gate_out)).astype(brain_float_sixteen)
    output_terms = jnp.einsum(
        "crk,rkd->cd", normed_tri, mixed_grad, preferred_element_type=single_float_format
    )
    triangle_normed_gradient = jnp.einsum(
        "rkd,cd->crk", mixed_grad, output_weight, preferred_element_type=single_float_format
    )
    triangle_gradient = norm_backward_pass(
        triangle_normed_gradient,
        standardized_input,
        input_inverse_scale,
        output_norm_gain[:, None, None],
        0,
    ).astype(brain_float_sixteen)
    grad_cols = lax.all_to_all(triangle_gradient, "row", split_axis=0, concat_axis=1, tiled=True)
    left_col_grad = jnp.einsum(
        "cij,cjk->cik", grad_cols, right_cols, preferred_element_type=single_float_format
    ).astype(brain_float_sixteen)
    right_col_grad = jnp.einsum(
        "cij,cik->cjk", grad_cols, left_cols, preferred_element_type=single_float_format
    ).astype(brain_float_sixteen)
    returned = lax.all_to_all(
        jnp.stack([left_col_grad, right_col_grad], axis=1),
        "row",
        split_axis=2,
        concat_axis=0,
        tiled=True,
    )
    left_grad = returned[:, 0].astype(single_float_format)
    right_grad = returned[:, 1].astype(single_float_format)
    project_terms = jnp.stack(
        [
            left_grad * live_mask * gate_left,
            left_grad * live_mask * projected[0] * gate_left * (1.0 - gate_left),
            right_grad * live_mask * gate_right,
            right_grad * live_mask * projected[2] * gate_right * (1.0 - gate_right),
        ]
    )
    project_terms = project_terms.astype(brain_float_sixteen).reshape(4 * hidden, row_count, length)
    project_part = jnp.einsum(
        "rkd,erk->de", normed_pair, project_terms, preferred_element_type=single_float_format
    )
    gate_part = jnp.einsum(
        "rkd,rke->de", normed_pair, gate_logit_grad, preferred_element_type=single_float_format
    )
    totals = lax.psum((project_part, gate_part, output_terms), "row")
    project_grad = totals[0] / length
    gate_grad = totals[1] / length
    output_grad = totals[2] / length
    normed_grad = jnp.einsum(
        "erk,de->rkd", project_terms, project_weight, preferred_element_type=single_float_format
    ) + jnp.einsum(
        "rke,de->rkd", gate_logit_grad, gate_weight, preferred_element_type=single_float_format
    )
    pair_grad = norm_backward_pass(normed_grad, zhat, zscale, input_gain, -1)
    return (update, pair_grad, project_grad, gate_grad, output_grad)


def fits_whole(mesh, args):
    pair_acts, output_weight = args[0], args[8]
    devices = mesh.shape["row"]
    length, channels = pair_acts.shape[0] // mesh.shape["grp"], pair_acts.shape[2]
    hidden = output_weight.shape[0]
    return (
        channels == LANES
        and hidden % 16 == 0
        and LANES % hidden == 0
        and length % (LANES // hidden) == 0
        and (LANES // hidden) % 8 == 0
        and length % 16 == 0
        and devices % 2 == 0
        and length % devices == 0
        and 2 * pair_acts.dtype.itemsize * length * length * channels <= WHOLE_BYTES
    )


def solution(mesh):
    in_specs = (
        P(("grp", "row"), None, None),
        P("grp"),
        P(),
        P(),
        P(),
        P(),
        P(),
        P(),
        P(),
        P(("grp", "row"), None, None),
    )
    out_specs = (
        P(("grp", "row"), None, None),
        P(("grp", "row"), None, None),
        P("grp", None),
        P("grp", None),
        P("grp", None),
    )
    devices = mesh.shape["row"]

    def run(*args):
        crop = functools.partial(body_whole, devices) if fits_whole(mesh, args) else body
        return jax.shard_map(crop, mesh=mesh, in_specs=in_specs, out_specs=out_specs, check_vma=False)(*args)

    return run
```

```python
import functools

import jax
import jax.numpy as jnp
from jax import lax
from jax.experimental import pallas as pl
from jax.experimental.pallas import tpu as pltpu
from jax.sharding import PartitionSpec as P

LANES = 128
WHOLE_BYTES = 4 << 20

NN = (((1,), (0,)), ((), ()))
NT = (((1,), (1,)), ((), ()))
TN = (((0,), (0,)), ((), ()))


def dot(a, b, dims=NN):
    return lax.dot_general(a, b, dims, preferred_element_type=jnp.float32)


def dot_split(a, b):
    high = a.astype(jnp.bfloat16)
    low = (a - high.astype(jnp.float32)).astype(jnp.bfloat16)
    return dot(high, b) + dot(low, b)


def iota(shape, dim):
    return lax.broadcasted_iota(jnp.int32, shape, dim)


def zero_one(condition):
    return jnp.where(condition, 1.0, 0.0).astype(jnp.bfloat16)


def sigmoid(v):
    return 1.0 / (1.0 + jnp.exp(-v))


def normalize(v, axis=-1):
    centered = v - jnp.mean(v, axis=axis, keepdims=True)
    s = lax.rsqrt(jnp.mean(centered * centered, axis=axis, keepdims=True) + 1e-05)
    return centered * s, s


def crop_kernel(
    n,
    hidden,
    blocks,
    *refs,
):
    block_refs, refs = refs[:blocks], refs[blocks:]
    count_ref, gain_ref, bias_ref, project_ref, gate_ref = refs[:5]
    out_gain_ref, out_bias_ref, out_weight_ref = refs[5:8]
    update_ref, pair_ref, project_grad_ref, gate_grad_ref, out_grad_ref = refs[8:13]
    zn_ref, ug_ref, upd_ref, dgo_ref, dp_ref, dpt_ref = refs[13:]
    f32, bf16 = jnp.float32, jnp.bfloat16
    per = LANES // hidden
    groups = n // per
    wide = n * hidden
    me = lax.axis_index("row")
    rows = n // blocks
    half = rows * n
    count = count_ref[0]
    gain, bias = gain_ref[...], bias_ref[...]

    for d, block_ref in enumerate(block_refs):
        for r in range(rows):
            i = (me ^ d) * rows + r
            p, where = lax.rem(i, per), pl.ds(pl.multiple_of(lax.div(i, per) * n, 16), n)
            zhat, _ = normalize(block_ref[pl.ds(r * n, n), :].astype(f32))
            zn_ref[p, where, :] = (zhat * gain + bias).astype(bf16)
            ug_ref[p, where, :] = block_ref[pl.ds(half + r * n, n), :]

    kinds = 4 * LANES
    a, b = iota((4 * hidden, kinds), 0), iota((4 * hidden, kinds), 1)
    spread = zero_one((a // hidden == b // LANES) & (a % hidden == b % hidden))
    tiled = dot(project_ref[...], spread).astype(bf16)
    place = (iota((LANES, kinds), 1) % LANES) // hidden
    projected = jnp.zeros((groups * n, kinds), f32)
    for p in range(per):
        projected += dot(zn_ref[p], jnp.where(place == p, tiled, jnp.zeros_like(tiled)))
    row_k = jnp.concatenate([iota((n, LANES), 0)] * groups, axis=0)
    row_g = jnp.concatenate([jnp.full((n, LANES), g * per, jnp.int32) for g in range(groups)], axis=0)
    row_i = row_g + iota((groups * n, LANES), 1) // hidden
    mask = jnp.where((row_i < count) & (row_k < count), 1.0, 0.0)
    value_left, value_right = projected[:, :LANES], projected[:, 2 * LANES : 3 * LANES]
    gate_left = sigmoid(projected[:, LANES : 2 * LANES])
    gate_right = sigmoid(projected[:, 3 * LANES :])
    mask_left, mask_right = mask * gate_left, mask * gate_right

    def lanes(flat):
        return jnp.concatenate([flat[g * n : (g + 1) * n] for g in range(groups)], axis=1)

    def flatten(rowed):
        return jnp.concatenate([rowed[:, g * LANES : (g + 1) * LANES] for g in range(groups)], axis=0)

    left = lanes((mask_left * value_left).astype(bf16))
    right = lanes((mask_right * value_right).astype(bf16))

    same = iota((LANES, wide), 0) % hidden == iota((LANES, wide), 1) % hidden
    pick = zero_one(iota((per, LANES), 0) == iota((per, LANES), 1) // hidden)
    parts = []
    for g in range(groups):
        cross = dot(right[:, g * LANES : (g + 1) * LANES], left, TN).astype(bf16)
        parts.append(dot(pick, jnp.where(same, cross, jnp.zeros_like(cross))))
    x = flatten(jnp.concatenate(parts, axis=0))

    mean = jnp.where(iota((LANES, LANES), 0) // hidden == iota((LANES, LANES), 1) // hidden, 1.0 / hidden, 0.0)
    mean = mean.astype(bf16)
    out_gain = jnp.concatenate([out_gain_ref[...]] * per, axis=1)
    out_bias = jnp.concatenate([out_bias_ref[...]] * per, axis=1)
    centered = x - dot(x.astype(bf16), mean)
    xs = lax.rsqrt(dot_split(centered * centered, mean) + 1e-05)
    xhat = centered * xs
    xn = (xhat * out_gain + out_bias).astype(bf16)

    out_weight = jnp.concatenate([out_weight_ref[...]] * per, axis=0)
    at = iota((LANES, LANES), 0) // hidden
    gate_weight = gate_ref[...]
    gate_grad = jnp.zeros((LANES, LANES), f32)
    out_grad = jnp.zeros((hidden, LANES), f32)
    dxn = jnp.zeros((groups * n, LANES), f32)
    for p in range(per):
        zn = zn_ref[p]
        weight = jnp.where(at == p, out_weight, jnp.zeros_like(out_weight))
        y = dot(xn, weight)
        go = sigmoid(dot(zn, gate_weight))
        upd_ref[p] = (go * y).astype(bf16)
        cotangent = ug_ref[p].astype(f32)
        dy = (cotangent * go).astype(bf16)
        dgo = (cotangent * y * go * (1.0 - go)).astype(bf16)
        dgo_ref[p] = dgo
        gate_grad += dot(zn, dgo, TN)
        out_grad += dot(xn, dy, TN)[p * hidden : (p + 1) * hidden]
        dxn += dot(dy, weight, NT)
    gate_grad_ref[...] = gate_grad / n
    out_grad_ref[...] = out_grad / n

    u = out_gain * dxn
    dx = xs * (u - dot_split(u, mean) - xhat * dot_split(u * xhat, mean))
    dx = lanes(dx.astype(bf16))

    repeat = zero_one(iota((LANES, per), 0) // hidden == iota((LANES, per), 1))
    dleft = jnp.zeros((n, wide), f32)
    dright = []
    for g in range(groups):
        spread_dx = dot(repeat, dx[g * per : (g + 1) * per]).astype(bf16)
        diagonal = jnp.where(same, spread_dx, jnp.zeros_like(spread_dx))
        dleft += dot(right[:, g * LANES : (g + 1) * LANES], diagonal)
        dright.append(dot(left, diagonal, NT))
    dleft = flatten(dleft.astype(bf16)).astype(f32)
    dright = jnp.concatenate(dright, axis=0).astype(bf16).astype(f32)
    dp = [
        dleft * mask_left,
        dleft * mask_left * value_left * (1.0 - gate_left),
        dright * mask_right,
        dright * mask_right * value_right * (1.0 - gate_right),
    ]
    dp = jnp.concatenate([d.astype(bf16) for d in dp], axis=1)
    dp_ref[...] = dp
    dpt_ref[...] = dp.T
    project_grad = jnp.zeros((4 * hidden, LANES), f32)
    for p in range(per):
        at_p = [dpt_ref[pl.ds(kind * LANES + p * hidden, hidden), :] for kind in range(4)]
        project_grad += dot(jnp.concatenate(at_p, axis=0), zn_ref[p])
    project_grad_ref[...] = project_grad.T / n

    place = (iota((n, kinds), 1) % LANES) // hidden
    for r in range(rows):
        i = me * rows + r
        g, p = lax.div(i, per), lax.rem(i, per)
        where = pl.ds(pl.multiple_of(g * n, 16), n)
        update_ref[r] = upd_ref[p, where, :]
        dp_row = dp_ref[where, :]
        dp_row = jnp.where(place == p, dp_row, jnp.zeros_like(dp_row))
        dzn = dot(dp_row, tiled, NT) + dot(dgo_ref[p, where, :], gate_weight, NT)
        zhat, zs = normalize(block_refs[0][pl.ds(r * n, n), :].astype(f32))
        u = gain * dzn
        first = jnp.mean(u, axis=-1, keepdims=True)
        second = jnp.mean(u * zhat, axis=-1, keepdims=True)
        pair_ref[r] = zs * (u - first - zhat * second)


def body_whole(
    devices,
    pair_acts,
    token_count,
    input_gain,
    input_bias,
    project_weight,
    gate_weight,
    output_norm_gain,
    output_shift_bias,
    output_weight,
    update_grad,
):
    rows, n, channels = pair_acts.shape
    hidden = output_weight.shape[0]
    half = rows * n
    send = jnp.concatenate(
        [pair_acts.reshape(half, channels), update_grad.reshape(half, channels)], axis=0
    )
    blocks = {0: send}
    step = devices // 2
    while step:
        pairs = [(i, i ^ step) for i in range(devices)]
        blocks.update({d ^ step: lax.ppermute(blocks[d], "row", pairs) for d in list(blocks)})
        step //= 2
    per = LANES // hidden
    tall = n // per * n
    f32, bf16 = jnp.float32, jnp.bfloat16
    vmem = pl.BlockSpec(memory_space=pltpu.VMEM)
    return pl.pallas_call(
        functools.partial(crop_kernel, n, hidden, devices),
        out_shape=(
            jax.ShapeDtypeStruct((rows, n, channels), bf16),
            jax.ShapeDtypeStruct((rows, n, channels), f32),
            jax.ShapeDtypeStruct((channels, 4 * hidden), f32),
            jax.ShapeDtypeStruct((channels, channels), f32),
            jax.ShapeDtypeStruct((hidden, channels), f32),
        ),
        in_specs=[vmem] * devices + [pl.BlockSpec(memory_space=pltpu.SMEM)] + [vmem] * 7,
        out_specs=(vmem,) * 5,
        scratch_shapes=[
            pltpu.VMEM((per, tall, channels), bf16),
            pltpu.VMEM((per, tall, channels), bf16),
            pltpu.VMEM((per, tall, channels), bf16),
            pltpu.VMEM((per, tall, channels), bf16),
            pltpu.VMEM((tall, 4 * LANES), bf16),
            pltpu.VMEM((4 * LANES, tall), bf16),
        ],
        compiler_params=pltpu.CompilerParams(vmem_limit_bytes=32 << 20),
    )(
        *[blocks[d] for d in range(devices)],
        token_count,
        input_gain[None],
        input_bias[None],
        project_weight,
        gate_weight,
        output_norm_gain[None],
        output_shift_bias[None],
        output_weight,
    )


def layer_normalize(values, norm_gain, norm_bias, reduce_axis):
    average = jnp.mean(values, axis=reduce_axis, keepdims=True)
    centered = values - average
    variance = jnp.mean(centered * centered, axis=reduce_axis, keepdims=True)
    inv_std = lax.rsqrt(variance + 1e-05)
    normed = centered * inv_std
    return (normed * norm_gain + norm_bias, normed, inv_std)


def norm_backward_pass(upstream, normed, inv_std, norm_gain, reduce_axis):
    scaled = upstream * norm_gain
    first = jnp.mean(scaled, axis=reduce_axis, keepdims=True)
    second = jnp.mean(scaled * normed, axis=reduce_axis, keepdims=True)
    return inv_std * (scaled - first - normed * second)


def body(
    pair_acts,
    token_count,
    input_gain,
    input_bias,
    project_weight,
    gate_weight,
    output_norm_gain,
    output_shift_bias,
    output_weight,
    update_grad,
):
    single_float_format = jnp.float32
    brain_float_sixteen = jnp.bfloat16
    row_count, length, channels = pair_acts.shape
    hidden = output_weight.shape[0]
    row_start = lax.axis_index("row") * row_count
    live_limit = token_count[0]
    row_live = (row_start + jnp.arange(row_count, dtype=jnp.int32) < live_limit).astype(
        single_float_format
    )
    col_live = (jnp.arange(length, dtype=jnp.int32) < live_limit).astype(single_float_format)
    live_mask = row_live[:, None] * col_live[None, :]
    zn32, zhat, zscale = layer_normalize(
        pair_acts.astype(single_float_format), input_gain, input_bias, -1
    )
    normed_pair = zn32.astype(brain_float_sixteen)
    projected = jnp.einsum(
        "rkd,de->erk", normed_pair, project_weight, preferred_element_type=single_float_format
    ).reshape(4, hidden, row_count, length)
    gate_left = jax.nn.sigmoid(projected[1])
    gate_right = jax.nn.sigmoid(projected[3])
    left_panel = (live_mask * gate_left * projected[0]).astype(brain_float_sixteen)
    right_panel = (live_mask * gate_right * projected[2]).astype(brain_float_sixteen)
    stacked = jnp.stack([left_panel, right_panel], axis=1)
    columns = lax.all_to_all(stacked, "row", split_axis=0, concat_axis=2, tiled=True)
    left_cols = columns[:, 0]
    right_cols = columns[:, 1]
    products = jnp.einsum(
        "cik,cjk->cij", left_cols, right_cols, preferred_element_type=single_float_format
    ).astype(brain_float_sixteen)
    triangle_product = lax.all_to_all(products, "row", split_axis=1, concat_axis=0, tiled=True)
    normed_input_single, standardized_input, input_inverse_scale = layer_normalize(
        triangle_product.astype(single_float_format),
        output_norm_gain[:, None, None],
        output_shift_bias[:, None, None],
        0,
    )
    normed_tri = normed_input_single.astype(brain_float_sixteen)
    mixed = jnp.einsum(
        "crk,cd->rkd", normed_tri, output_weight, preferred_element_type=single_float_format
    )
    gate_out = jax.nn.sigmoid(
        jnp.einsum(
            "rkd,de->rke", normed_pair, gate_weight, preferred_element_type=single_float_format
        )
    )
    update = (gate_out * mixed).astype(brain_float_sixteen)
    cotangent = update_grad.astype(single_float_format)
    mixed_grad = (cotangent * gate_out).astype(brain_float_sixteen)
    gate_logit_grad = (cotangent * mixed * gate_out * (1.0 - gate_out)).astype(brain_float_sixteen)
    output_terms = jnp.einsum(
        "crk,rkd->cd", normed_tri, mixed_grad, preferred_element_type=single_float_format
    )
    triangle_normed_gradient = jnp.einsum(
        "rkd,cd->crk", mixed_grad, output_weight, preferred_element_type=single_float_format
    )
    triangle_gradient = norm_backward_pass(
        triangle_normed_gradient,
        standardized_input,
        input_inverse_scale,
        output_norm_gain[:, None, None],
        0,
    ).astype(brain_float_sixteen)
    grad_cols = lax.all_to_all(triangle_gradient, "row", split_axis=0, concat_axis=1, tiled=True)
    left_col_grad = jnp.einsum(
        "cij,cjk->cik", grad_cols, right_cols, preferred_element_type=single_float_format
    ).astype(brain_float_sixteen)
    right_col_grad = jnp.einsum(
        "cij,cik->cjk", grad_cols, left_cols, preferred_element_type=single_float_format
    ).astype(brain_float_sixteen)
    returned = lax.all_to_all(
        jnp.stack([left_col_grad, right_col_grad], axis=1),
        "row",
        split_axis=2,
        concat_axis=0,
        tiled=True,
    )
    left_grad = returned[:, 0].astype(single_float_format)
    right_grad = returned[:, 1].astype(single_float_format)
    project_terms = jnp.stack(
        [
            left_grad * live_mask * gate_left,
            left_grad * live_mask * projected[0] * gate_left * (1.0 - gate_left),
            right_grad * live_mask * gate_right,
            right_grad * live_mask * projected[2] * gate_right * (1.0 - gate_right),
        ]
    )
    project_terms = project_terms.astype(brain_float_sixteen).reshape(4 * hidden, row_count, length)
    project_part = jnp.einsum(
        "rkd,erk->de", normed_pair, project_terms, preferred_element_type=single_float_format
    )
    gate_part = jnp.einsum(
        "rkd,rke->de", normed_pair, gate_logit_grad, preferred_element_type=single_float_format
    )
    totals = lax.psum((project_part, gate_part, output_terms), "row")
    project_grad = totals[0] / length
    gate_grad = totals[1] / length
    output_grad = totals[2] / length
    normed_grad = jnp.einsum(
        "erk,de->rkd", project_terms, project_weight, preferred_element_type=single_float_format
    ) + jnp.einsum(
        "rke,de->rkd", gate_logit_grad, gate_weight, preferred_element_type=single_float_format
    )
    pair_grad = norm_backward_pass(normed_grad, zhat, zscale, input_gain, -1)
    return (update, pair_grad, project_grad, gate_grad, output_grad)


def fits_whole(mesh, args):
    pair_acts, output_weight = args[0], args[8]
    devices = mesh.shape["row"]
    length, channels = pair_acts.shape[0] // mesh.shape["grp"], pair_acts.shape[2]
    hidden = output_weight.shape[0]
    return (
        channels == LANES
        and hidden % 16 == 0
        and LANES % hidden == 0
        and length % (LANES // hidden) == 0
        and (LANES // hidden) % 8 == 0
        and length % 16 == 0
        and devices & (devices - 1) == 0
        and length % devices == 0
        and 2 * pair_acts.dtype.itemsize * length * length * channels <= WHOLE_BYTES
    )


def solution(mesh):
    in_specs = (
        P(("grp", "row"), None, None),
        P("grp"),
        P(),
        P(),
        P(),
        P(),
        P(),
        P(),
        P(),
        P(("grp", "row"), None, None),
    )
    out_specs = (
        P(("grp", "row"), None, None),
        P(("grp", "row"), None, None),
        P("grp", None),
        P("grp", None),
        P("grp", None),
    )
    devices = mesh.shape["row"]

    def run(*args):
        crop = functools.partial(body_whole, devices) if fits_whole(mesh, args) else body
        return jax.shard_map(crop, mesh=mesh, in_specs=in_specs, out_specs=out_specs, check_vma=False)(*args)

    return run
```

```python
import functools

import jax
import jax.numpy as jnp
from jax import lax
from jax.experimental import pallas as pl
from jax.experimental.pallas import tpu as pltpu
from jax.sharding import PartitionSpec as P

LANES = 128
KINDS = 4
WHOLE_BYTES = 4 << 20

NN = (((1,), (0,)), ((), ()))
NT = (((1,), (1,)), ((), ()))
TN = (((0,), (0,)), ((), ()))


def dot(a, b, dims=NN):
    return lax.dot_general(a, b, dims, preferred_element_type=jnp.float32)


def dot_split(a, b):
    high = a.astype(jnp.bfloat16)
    low = (a - high.astype(jnp.float32)).astype(jnp.bfloat16)
    return dot(high, b) + dot(low, b)


def iota(shape, dim):
    return lax.broadcasted_iota(jnp.int32, shape, dim)


def zero_one(condition):
    return jnp.where(condition, 1.0, 0.0).astype(jnp.bfloat16)


def sigmoid(v):
    return 0.5 * jnp.tanh(0.5 * v) + 0.5


def normalize(v):
    centered = v - jnp.mean(v, axis=-1, keepdims=True)
    s = lax.rsqrt(jnp.mean(centered * centered, axis=-1, keepdims=True) + 1e-05)
    return centered * s, s


def norm_tiles(n, block_refs, gain, bias, zn_ref):
    per = zn_ref.shape[0]
    rows = block_refs[0].shape[0] // (2 * n)
    for t in range(len(block_refs) * rows):
        v = block_refs[t // rows][pl.ds(t % rows * n, n), :].astype(jnp.float32)
        zn_ref[t % per, pl.ds(t // per * n, n), :] = (normalize(v)[0] * gain + bias).astype(jnp.bfloat16)


def project_tiles(zn_ref, project_t):
    per = zn_ref.shape[0]
    hidden = project_t.shape[0] // KINDS
    columns = []
    for p in range(per):
        parts = []
        for kind in range(KINDS):
            own = project_t[kind * hidden : (kind + 1) * hidden]
            before, after = p * hidden, (per - 1 - p) * hidden
            parts += [jnp.zeros((before, own.shape[1]), own.dtype)] * (before > 0) + [own]
            parts += [jnp.zeros((after, own.shape[1]), own.dtype)] * (after > 0)
        columns.append(jnp.concatenate(parts, axis=0))
    weight = jnp.concatenate(columns, axis=1)
    zn = jnp.concatenate([zn_ref[p] for p in range(per)], axis=1)
    return dot(zn, weight, NT)


def head_kernel(n, *refs):
    *block_refs, gain_ref, bias_ref, project_ref, gate_ref, zn_ref, projected_ref, go_ref = refs
    norm_tiles(n, block_refs, gain_ref[...], bias_ref[...], zn_ref)
    projected_ref[...] = project_tiles(zn_ref, project_ref[...])
    gate_weight = gate_ref[...]
    for p in range(zn_ref.shape[0]):
        go_ref[p] = sigmoid(dot(zn_ref[p], gate_weight))


def tail_kernel(n, hidden, order, *refs):
    blocks = len(order)
    block_refs, refs = refs[:blocks], refs[blocks:]
    zn_head_ref, projected_head_ref, go_head_ref = refs[:3]
    count_ref, gain_ref, bias_ref, project_ref, gate_ref = refs[3:8]
    out_gain_ref, out_bias_ref, out_weight_ref = refs[8:11]
    update_ref, pair_ref, project_grad_ref, gate_grad_ref, out_grad_ref = refs[11:16]
    zn_tail_ref, dpt_ref = refs[16:]
    f32, bf16 = jnp.float32, jnp.bfloat16
    per = LANES // hidden
    groups = n // per
    wide = n * hidden
    rows = n // blocks
    me = lax.axis_index("row")
    count = count_ref[0]
    gain, bias = gain_ref[...], bias_ref[...]
    gate_weight = gate_ref[...]
    project_t = project_ref[...]

    def row_of(t):
        return (me ^ order[t // rows]) * rows + t % rows

    def tiles(p):
        return [(t // rows, t % rows * n) for t in range(p, n, per)]

    norm_tiles(n, block_refs[blocks // 2 :], gain, bias, zn_tail_ref)

    def zn_of(p):
        return jnp.concatenate([zn_head_ref[p], zn_tail_ref[p]], axis=0)

    projected = jnp.concatenate([projected_head_ref[...], project_tiles(zn_tail_ref, project_t)], axis=0)

    place = iota((1, LANES), 1) // hidden
    row_i = []
    for g in range(groups):
        at = jnp.full((1, LANES), row_of(g * per), jnp.int32)
        for p in range(1, per):
            at = jnp.where(place == p, row_of(g * per + p), at)
        row_i.append(at)
    live_k = iota((n, LANES), 0) < count
    mask = jnp.concatenate([jnp.where(live_k & (at < count), 1.0, 0.0) for at in row_i], axis=0)
    value_left, value_right = projected[:, :LANES], projected[:, 2 * LANES : 3 * LANES]
    gate_left = sigmoid(projected[:, LANES : 2 * LANES])
    gate_right = sigmoid(projected[:, 3 * LANES :])
    mask_left, mask_right = mask * gate_left, mask * gate_right

    def lanes(flat):
        return jnp.concatenate([flat[g * n : (g + 1) * n] for g in range(groups)], axis=1)

    def flatten(rowed):
        return jnp.concatenate([rowed[:, g * LANES : (g + 1) * LANES] for g in range(groups)], axis=0)

    left = lanes((mask_left * value_left).astype(bf16))
    right = lanes((mask_right * value_right).astype(bf16))

    same = iota((LANES, wide), 0) % hidden == iota((LANES, wide), 1) % hidden
    x = jnp.zeros((n, wide), f32)
    for g in range(groups):
        cross = dot(right[:, g * LANES : (g + 1) * LANES], left, TN).astype(bf16)
        pick = zero_one(iota((n, LANES), 0) == row_i[g])
        x += dot(pick, jnp.where(same, cross, jnp.zeros_like(cross)))
    x = flatten(x)

    mean = jnp.where(iota((LANES, LANES), 0) // hidden == iota((LANES, LANES), 1) // hidden, 1.0 / hidden, 0.0)
    mean = mean.astype(bf16)
    out_gain = jnp.concatenate([out_gain_ref[...]] * per, axis=1)
    out_bias = jnp.concatenate([out_bias_ref[...]] * per, axis=1)
    centered = x - dot(x.astype(bf16), mean)
    xs = lax.rsqrt(dot_split(centered * centered, mean) + 1e-05)
    xhat = centered * xs
    xn = (xhat * out_gain + out_bias).astype(bf16)

    out_weight = jnp.concatenate([out_weight_ref[...]] * per, axis=0)
    at = iota((LANES, LANES), 0) // hidden
    gate_grad = jnp.zeros((LANES, LANES), f32)
    out_grad = jnp.zeros((hidden, LANES), f32)
    dxn = jnp.zeros((groups * n, LANES), f32)
    own_dgo = []
    for p in range(per):
        zn = zn_of(p)
        weight = jnp.where(at == p, out_weight, jnp.zeros_like(out_weight))
        y = dot(xn, weight)
        go = jnp.concatenate([go_head_ref[p], sigmoid(dot(zn_tail_ref[p], gate_weight))], axis=0)
        ug = [block_refs[b][pl.ds(rows * n + start, n), :] for b, start in tiles(p)]
        cotangent = jnp.concatenate(ug, axis=0).astype(f32)
        dy_wide = cotangent * go
        dy = dy_wide.astype(bf16)
        dgo = (dy_wide * y * (1.0 - go)).astype(bf16)
        if p < rows:
            update_ref[p] = (go[:n] * y[:n]).astype(bf16)
            own_dgo.append(dgo[:n])
        gate_grad += dot(zn, dgo, TN)
        out_grad += dot(xn, dy, TN)[p * hidden : (p + 1) * hidden]
        dxn += dot(dy, weight, NT)
    gate_grad_ref[...] = gate_grad / n
    out_grad_ref[...] = out_grad / n

    u = out_gain * dxn
    dx = xs * (u - dot_split(u, mean) - xhat * dot_split(u * xhat, mean))
    dx = lanes(dx.astype(bf16))

    dleft = jnp.zeros((n, wide), f32)
    dright = []
    for g in range(groups):
        repeat = [zero_one(iota((hidden, n), 1) == row_of(g * per + p)) for p in range(per)]
        spread = dot(jnp.concatenate(repeat, axis=0), dx).astype(bf16)
        diagonal = jnp.where(same, spread, jnp.zeros_like(spread))
        dleft += dot(right[:, g * LANES : (g + 1) * LANES], diagonal)
        dright.append(dot(left, diagonal, NT))
    dleft = flatten(dleft.astype(bf16)).astype(f32)
    dright = jnp.concatenate(dright, axis=0).astype(bf16).astype(f32)
    dleft, dright = dleft * mask_left, dright * mask_right
    dp = [
        dleft,
        dleft * value_left * (1.0 - gate_left),
        dright,
        dright * value_right * (1.0 - gate_right),
    ]
    dp = jnp.concatenate([d.astype(bf16) for d in dp], axis=1)
    dpt_ref[...] = dp.T
    project_grad = jnp.zeros((KINDS * hidden, LANES), f32)
    for p in range(per):
        at_p = [dpt_ref[pl.ds(kind * LANES + p * hidden, hidden), :] for kind in range(KINDS)]
        project_grad += dot(jnp.concatenate(at_p, axis=0), zn_of(p))
    project_grad_ref[...] = project_grad / n

    tiled = [project_t[kind * hidden : (kind + 1) * hidden] for kind in range(KINDS) for _ in range(per)]
    tiled = jnp.concatenate(tiled, axis=0)
    place = iota((n, KINDS * LANES), 1) % LANES // hidden
    for r in range(rows):
        dp_row = jnp.where(place == r, dp[:n], jnp.zeros_like(dp[:n]))
        dzn = dot(dp_row, tiled) + dot(own_dgo[r], gate_weight, NT)
        zhat, zs = normalize(block_refs[0][pl.ds(r * n, n), :].astype(f32))
        u = gain * dzn
        first = jnp.mean(u, axis=-1, keepdims=True)
        second = jnp.mean(u * zhat, axis=-1, keepdims=True)
        pair_ref[r] = zs * (u - first - zhat * second)


def body_whole(
    devices,
    pair_acts,
    token_count,
    input_gain,
    input_bias,
    project_weight,
    gate_weight,
    output_norm_gain,
    output_shift_bias,
    output_weight,
    update_grad,
):
    rows, n, channels = pair_acts.shape
    hidden = output_weight.shape[0]
    f32, bf16 = jnp.float32, jnp.bfloat16
    half = rows * n
    send = jnp.concatenate(
        [pair_acts.reshape(half, channels), update_grad.reshape(half, channels)], axis=0
    )
    blocks = {0: send}
    step = devices // 2
    while step:
        pairs = [(i, i ^ step) for i in range(devices)]
        blocks.update({d ^ step: lax.ppermute(blocks[d], "row", pairs) for d in list(blocks)})
        step //= 2
    order = sorted(blocks, key=lambda d: (d & 2, d))
    ordered = [blocks[d] for d in order]
    per = LANES // hidden
    tall = n // per * n
    vmem = pl.BlockSpec(memory_space=pltpu.VMEM)
    shape = jax.ShapeDtypeStruct
    gain, bias, project_t = input_gain[None], input_bias[None], project_weight.T
    head_blocks = ordered[: devices // 2]
    head = pl.pallas_call(
        functools.partial(head_kernel, n),
        out_shape=(
            shape((per, tall // 2, channels), bf16),
            shape((tall // 2, KINDS * LANES), f32),
            shape((per, tall // 2, channels), f32),
        ),
        in_specs=[vmem] * (len(head_blocks) + 4),
        out_specs=(vmem,) * 3,
        compiler_params=pltpu.CompilerParams(vmem_limit_bytes=16 << 20),
        name="head",
    )(*head_blocks, gain, bias, project_t, gate_weight)
    update, pair_grad, project_grad, gate_grad, output_grad = pl.pallas_call(
        functools.partial(tail_kernel, n, hidden, order),
        out_shape=(
            shape((rows, n, channels), bf16),
            shape((rows, n, channels), f32),
            shape((KINDS * hidden, channels), f32),
            shape((channels, channels), f32),
            shape((hidden, channels), f32),
        ),
        in_specs=[vmem] * (devices + 3) + [pl.BlockSpec(memory_space=pltpu.SMEM)] + [vmem] * 7,
        out_specs=(vmem,) * 5,
        scratch_shapes=[
            pltpu.VMEM((per, tall // 2, channels), bf16),
            pltpu.VMEM((KINDS * LANES, tall), bf16),
        ],
        compiler_params=pltpu.CompilerParams(vmem_limit_bytes=32 << 20),
        name="tail",
    )(
        *ordered,
        *head,
        token_count,
        gain,
        bias,
        project_t,
        gate_weight,
        output_norm_gain[None],
        output_shift_bias[None],
        output_weight,
    )
    return update, pair_grad, project_grad.T, gate_grad, output_grad


def layer_normalize(values, norm_gain, norm_bias, reduce_axis):
    average = jnp.mean(values, axis=reduce_axis, keepdims=True)
    centered = values - average
    variance = jnp.mean(centered * centered, axis=reduce_axis, keepdims=True)
    inv_std = lax.rsqrt(variance + 1e-05)
    normed = centered * inv_std
    return (normed * norm_gain + norm_bias, normed, inv_std)


def norm_backward_pass(upstream, normed, inv_std, norm_gain, reduce_axis):
    scaled = upstream * norm_gain
    first = jnp.mean(scaled, axis=reduce_axis, keepdims=True)
    second = jnp.mean(scaled * normed, axis=reduce_axis, keepdims=True)
    return inv_std * (scaled - first - normed * second)


def body(
    pair_acts,
    token_count,
    input_gain,
    input_bias,
    project_weight,
    gate_weight,
    output_norm_gain,
    output_shift_bias,
    output_weight,
    update_grad,
):
    single_float_format = jnp.float32
    brain_float_sixteen = jnp.bfloat16
    row_count, length, channels = pair_acts.shape
    hidden = output_weight.shape[0]
    row_start = lax.axis_index("row") * row_count
    live_limit = token_count[0]
    row_live = (row_start + jnp.arange(row_count, dtype=jnp.int32) < live_limit).astype(
        single_float_format
    )
    col_live = (jnp.arange(length, dtype=jnp.int32) < live_limit).astype(single_float_format)
    live_mask = row_live[:, None] * col_live[None, :]
    zn32, zhat, zscale = layer_normalize(
        pair_acts.astype(single_float_format), input_gain, input_bias, -1
    )
    normed_pair = zn32.astype(brain_float_sixteen)
    projected = jnp.einsum(
        "rkd,de->erk", normed_pair, project_weight, preferred_element_type=single_float_format
    ).reshape(4, hidden, row_count, length)
    gate_left = jax.nn.sigmoid(projected[1])
    gate_right = jax.nn.sigmoid(projected[3])
    left_panel = (live_mask * gate_left * projected[0]).astype(brain_float_sixteen)
    right_panel = (live_mask * gate_right * projected[2]).astype(brain_float_sixteen)
    stacked = jnp.stack([left_panel, right_panel], axis=1)
    columns = lax.all_to_all(stacked, "row", split_axis=0, concat_axis=2, tiled=True)
    left_cols = columns[:, 0]
    right_cols = columns[:, 1]
    products = jnp.einsum(
        "cik,cjk->cij", left_cols, right_cols, preferred_element_type=single_float_format
    ).astype(brain_float_sixteen)
    triangle_product = lax.all_to_all(products, "row", split_axis=1, concat_axis=0, tiled=True)
    normed_input_single, standardized_input, input_inverse_scale = layer_normalize(
        triangle_product.astype(single_float_format),
        output_norm_gain[:, None, None],
        output_shift_bias[:, None, None],
        0,
    )
    normed_tri = normed_input_single.astype(brain_float_sixteen)
    mixed = jnp.einsum(
        "crk,cd->rkd", normed_tri, output_weight, preferred_element_type=single_float_format
    )
    gate_out = jax.nn.sigmoid(
        jnp.einsum(
            "rkd,de->rke", normed_pair, gate_weight, preferred_element_type=single_float_format
        )
    )
    update = (gate_out * mixed).astype(brain_float_sixteen)
    cotangent = update_grad.astype(single_float_format)
    mixed_grad = (cotangent * gate_out).astype(brain_float_sixteen)
    gate_logit_grad = (cotangent * mixed * gate_out * (1.0 - gate_out)).astype(brain_float_sixteen)
    output_terms = jnp.einsum(
        "crk,rkd->cd", normed_tri, mixed_grad, preferred_element_type=single_float_format
    )
    triangle_normed_gradient = jnp.einsum(
        "rkd,cd->crk", mixed_grad, output_weight, preferred_element_type=single_float_format
    )
    triangle_gradient = norm_backward_pass(
        triangle_normed_gradient,
        standardized_input,
        input_inverse_scale,
        output_norm_gain[:, None, None],
        0,
    ).astype(brain_float_sixteen)
    grad_cols = lax.all_to_all(triangle_gradient, "row", split_axis=0, concat_axis=1, tiled=True)
    left_col_grad = jnp.einsum(
        "cij,cjk->cik", grad_cols, right_cols, preferred_element_type=single_float_format
    ).astype(brain_float_sixteen)
    right_col_grad = jnp.einsum(
        "cij,cik->cjk", grad_cols, left_cols, preferred_element_type=single_float_format
    ).astype(brain_float_sixteen)
    returned = lax.all_to_all(
        jnp.stack([left_col_grad, right_col_grad], axis=1),
        "row",
        split_axis=2,
        concat_axis=0,
        tiled=True,
    )
    left_grad = returned[:, 0].astype(single_float_format)
    right_grad = returned[:, 1].astype(single_float_format)
    project_terms = jnp.stack(
        [
            left_grad * live_mask * gate_left,
            left_grad * live_mask * projected[0] * gate_left * (1.0 - gate_left),
            right_grad * live_mask * gate_right,
            right_grad * live_mask * projected[2] * gate_right * (1.0 - gate_right),
        ]
    )
    project_terms = project_terms.astype(brain_float_sixteen).reshape(4 * hidden, row_count, length)
    project_part = jnp.einsum(
        "rkd,erk->de", normed_pair, project_terms, preferred_element_type=single_float_format
    )
    gate_part = jnp.einsum(
        "rkd,rke->de", normed_pair, gate_logit_grad, preferred_element_type=single_float_format
    )
    totals = lax.psum((project_part, gate_part, output_terms), "row")
    project_grad = totals[0] / length
    gate_grad = totals[1] / length
    output_grad = totals[2] / length
    normed_grad = jnp.einsum(
        "erk,de->rkd", project_terms, project_weight, preferred_element_type=single_float_format
    ) + jnp.einsum(
        "rke,de->rkd", gate_logit_grad, gate_weight, preferred_element_type=single_float_format
    )
    pair_grad = norm_backward_pass(normed_grad, zhat, zscale, input_gain, -1)
    return (update, pair_grad, project_grad, gate_grad, output_grad)


def fits_whole(mesh, args):
    pair_acts, output_weight = args[0], args[8]
    devices = mesh.shape["row"]
    length, channels = pair_acts.shape[0] // mesh.shape["grp"], pair_acts.shape[2]
    hidden = output_weight.shape[0]
    return (
        channels == LANES
        and hidden % 16 == 0
        and LANES % hidden == 0
        and length % (LANES // hidden) == 0
        and (LANES // hidden) % 8 == 0
        and length % 16 == 0
        and devices & (devices - 1) == 0
        and length % devices == 0
        and length // devices <= LANES // hidden
        and devices >= 4
        and length // 2 % (LANES // hidden) == 0
        and 2 * pair_acts.dtype.itemsize * length * length * channels <= WHOLE_BYTES
    )


def solution(mesh):
    in_specs = (
        P(("grp", "row"), None, None),
        P("grp"),
        P(),
        P(),
        P(),
        P(),
        P(),
        P(),
        P(),
        P(("grp", "row"), None, None),
    )
    out_specs = (
        P(("grp", "row"), None, None),
        P(("grp", "row"), None, None),
        P("grp", None),
        P("grp", None),
        P("grp", None),
    )
    devices = mesh.shape["row"]

    def run(*args):
        crop = functools.partial(body_whole, devices) if fits_whole(mesh, args) else body
        return jax.shard_map(crop, mesh=mesh, in_specs=in_specs, out_specs=out_specs, check_vma=False)(*args)

    return run
```

```python
import functools

import jax
import jax.numpy as jnp
from jax import lax
from jax.experimental import pallas as pl
from jax.experimental.pallas import tpu as pltpu
from jax.sharding import PartitionSpec as P

LANES = 128
KINDS = 4
WHOLE_BYTES = 4 << 20

NN = (((1,), (0,)), ((), ()))
NT = (((1,), (1,)), ((), ()))
TN = (((0,), (0,)), ((), ()))


def dot(a, b, dims=NN):
    return lax.dot_general(a, b, dims, preferred_element_type=jnp.float32)


def dot_split(a, b_twice):
    high = a.astype(jnp.bfloat16)
    low = (a - high.astype(jnp.float32)).astype(jnp.bfloat16)
    return dot(jnp.concatenate([high, low], axis=1), b_twice)


def iota(shape, dim):
    return lax.broadcasted_iota(jnp.int32, shape, dim)


def zero_one(condition):
    return jnp.where(condition, 1.0, 0.0).astype(jnp.bfloat16)


def sigmoid(v):
    return 0.5 * jnp.tanh(0.5 * v) + 0.5


def normalize(v):
    centered = v - jnp.mean(v, axis=-1, keepdims=True)
    s = lax.rsqrt(jnp.mean(centered * centered, axis=-1, keepdims=True) + 1e-05)
    return centered * s, s


def norm_tiles(n, block_refs, gain, bias, zn_ref):
    per = zn_ref.shape[0]
    rows = block_refs[0].shape[0] // (2 * n)
    for t in range(len(block_refs) * rows):
        v = block_refs[t // rows][pl.ds(t % rows * n, n), :].astype(jnp.float32)
        zn_ref[t % per, pl.ds(t // per * n, n), :] = (normalize(v)[0] * gain + bias).astype(jnp.bfloat16)


def wide_project(project_t, per):
    hidden, channels = project_t.shape[0] // KINDS, project_t.shape[1]
    columns = []
    for p in range(per):
        parts = []
        for kind in range(KINDS):
            before, after = p * hidden, (per - 1 - p) * hidden
            parts += [jnp.zeros((before, channels), project_t.dtype)] * (before > 0)
            parts += [project_t[kind * hidden : (kind + 1) * hidden]]
            parts += [jnp.zeros((after, channels), project_t.dtype)] * (after > 0)
        columns.append(jnp.concatenate(parts, axis=0))
    return jnp.concatenate(columns, axis=1)


def wide_out(out_weight, per):
    hidden, channels = out_weight.shape
    rows = []
    for p in range(per):
        before, after = p * channels, (per - 1 - p) * channels
        parts = [jnp.zeros((hidden, before), out_weight.dtype)] * (before > 0) + [out_weight]
        rows.append(jnp.concatenate(parts + [jnp.zeros((hidden, after), out_weight.dtype)] * (after > 0), axis=1))
    return jnp.concatenate(rows, axis=0)


def side_by_side(ref):
    return jnp.concatenate([ref[p] for p in range(ref.shape[0])], axis=1)


def load_kernel(*refs):
    count = len(refs) // 2
    sources, targets, sems = refs[:count], refs[count : 2 * count - 1], refs[-1]
    half = sources[0].shape[0]
    targets = [targets[0].at[pl.ds(0, half)], targets[0].at[pl.ds(half, half)], *targets[1:]]
    copies = [pltpu.make_async_copy(a, b, sems.at[k]) for k, (a, b) in enumerate(zip(sources, targets))]
    for copy in copies:
        copy.start()
    for copy in copies:
        copy.wait()


def head_kernel(n, *refs):
    *block_refs, gain_ref, bias_ref, project_ref, gate_ref, out_weight_ref = refs[:-6]
    zn_ref, projected_ref, go_ref, znt_ref, project_wide_ref, out_wide_ref = refs[-6:]
    per = zn_ref.shape[0]
    norm_tiles(n, block_refs, gain_ref[...], bias_ref[...], zn_ref)
    project_wide_ref[...] = wide_project(project_ref[...], per)
    out_wide_ref[...] = wide_out(out_weight_ref[...], per)
    projected_ref[...] = dot(side_by_side(zn_ref), project_wide_ref[...], NT)
    gate_weight = gate_ref[...]
    for p in range(per):
        go_ref[p] = sigmoid(dot(zn_ref[p], gate_weight))
    znt_ref[...] = jnp.concatenate([zn_ref[p] for p in range(per)], axis=0).T


def tail_kernel(n, hidden, order, *refs):
    blocks = len(order)
    block_refs, refs = refs[:blocks], refs[blocks:]
    zn_head_ref, projected_head_ref, go_head_ref, znt_head_ref, project_wide_ref, out_wide_ref = refs[:6]
    count_ref, gain_ref, bias_ref, project_ref, gate_ref, out_gain_ref, out_bias_ref = refs[6:13]
    update_ref, pair_ref, project_grad_ref, gate_grad_ref, out_grad_ref = refs[13:18]
    zn_tail_ref, dpt_ref, square_ref, dgo_head_ref, dgo_tail_ref, dy_ref = refs[18:]
    f32, bf16 = jnp.float32, jnp.bfloat16
    per = LANES // hidden
    groups = n // per
    wide = n * hidden
    rows = n // blocks
    me = lax.axis_index("row")
    count = count_ref[0]
    gain, bias = gain_ref[...], bias_ref[...]
    gate_weight = gate_ref[...]
    project_t = project_ref[...]

    def row_of(t):
        return (me ^ order[t // rows]) * rows + t % rows

    def tiles(p):
        return [(t // rows, t % rows * n) for t in range(p, n, per)]

    norm_tiles(n, block_refs[blocks // 2 :], gain, bias, zn_tail_ref)

    def zn_of(p):
        return jnp.concatenate([zn_head_ref[p], zn_tail_ref[p]], axis=0)

    projected = jnp.concatenate([projected_head_ref[...], dot(side_by_side(zn_tail_ref), project_wide_ref[...], NT)], axis=0)

    place = iota((1, LANES), 1) // hidden
    row_i = []
    for g in range(groups):
        at = jnp.full((1, LANES), row_of(g * per), jnp.int32)
        for p in range(1, per):
            at = jnp.where(place == p, row_of(g * per + p), at)
        row_i.append(at)
    live_k = iota((n, LANES), 0) < count
    mask = jnp.concatenate([jnp.where(live_k & (at < count), 1.0, 0.0) for at in row_i], axis=0)
    value_left, value_right = projected[:, :LANES], projected[:, 2 * LANES : 3 * LANES]
    gate_left = sigmoid(projected[:, LANES : 2 * LANES])
    gate_right = sigmoid(projected[:, 3 * LANES :])
    mask_left, mask_right = mask * gate_left, mask * gate_right

    def lanes(flat):
        return jnp.concatenate([flat[g * n : (g + 1) * n] for g in range(groups)], axis=1)

    def flatten(rowed):
        return jnp.concatenate([rowed[:, g * LANES : (g + 1) * LANES] for g in range(groups)], axis=0)

    left = lanes((mask_left * value_left).astype(bf16))
    right = lanes((mask_right * value_right).astype(bf16))

    same = iota((LANES, wide), 0) % hidden == iota((LANES, wide), 1) % hidden
    for g in range(groups):
        cross = dot(right[:, g * LANES : (g + 1) * LANES], left, TN).astype(bf16)
        square_ref[pl.ds(g * LANES, LANES), :] = jnp.where(same, cross, jnp.zeros_like(cross))
    pick = jnp.concatenate([zero_one(iota((n, LANES), 0) == at) for at in row_i], axis=1)
    x = flatten(dot(pick, square_ref[...]))

    mean = jnp.where(iota((LANES, LANES), 0) // hidden == iota((LANES, LANES), 1) // hidden, 1.0 / hidden, 0.0)
    mean = mean.astype(bf16)
    mean_twice = jnp.concatenate([mean, mean], axis=0)
    out_gain = jnp.concatenate([out_gain_ref[...]] * per, axis=1)
    out_bias = jnp.concatenate([out_bias_ref[...]] * per, axis=1)
    centered = x - dot(x.astype(bf16), mean)
    xs = lax.rsqrt(dot_split(centered * centered, mean_twice) + 1e-05)
    xhat = centered * xs
    xn = (xhat * out_gain + out_bias).astype(bf16)

    out_wide = out_wide_ref[...]
    y_all = dot(xn, out_wide)
    own_dgo = []
    half = groups // 2 * n
    for p in range(per):
        y = y_all[:, p * LANES : (p + 1) * LANES]
        go = jnp.concatenate([go_head_ref[p], sigmoid(dot(zn_tail_ref[p], gate_weight))], axis=0)
        ug = [block_refs[b][pl.ds(rows * n + start, n), :] for b, start in tiles(p)]
        dy = jnp.concatenate(ug, axis=0).astype(f32) * go
        dgo = (dy * y * (1.0 - go)).astype(bf16)
        dy_ref[:, p * LANES : (p + 1) * LANES] = dy.astype(bf16)
        dgo_head_ref[pl.ds(p * half, half), :] = dgo[:half]
        dgo_tail_ref[pl.ds(p * half, half), :] = dgo[half:]
        if p < rows:
            update_ref[p] = (go[:n] * y[:n]).astype(bf16)
            own_dgo.append(dgo[:n])
    dxn = dot(dy_ref[...], out_wide, NT)
    out_grad = dot(xn, dy_ref[...], TN)
    out_grad = [out_grad[p * hidden : (p + 1) * hidden, p * LANES : (p + 1) * LANES] for p in range(per)]
    out_grad_ref[...] = sum(out_grad) / n
    zn_tail = jnp.concatenate([zn_tail_ref[p] for p in range(per)], axis=0)
    gate_grad = dot(znt_head_ref[...], dgo_head_ref[...]) + dot(zn_tail, dgo_tail_ref[...], TN)
    gate_grad_ref[...] = gate_grad / n

    u = out_gain * dxn
    dx = xs * (u - dot_split(u, mean_twice) - xhat * dot_split(u * xhat, mean_twice))
    dx = lanes(dx.astype(bf16))

    for g in range(groups):
        repeat = [zero_one(iota((hidden, n), 1) == row_of(g * per + p)) for p in range(per)]
        spread = dot(jnp.concatenate(repeat, axis=0), dx).astype(bf16)
        square_ref[pl.ds(g * LANES, LANES), :] = jnp.where(same, spread, jnp.zeros_like(spread))
    diagonal = square_ref[...]
    dleft = flatten(dot(right, diagonal).astype(bf16)).astype(f32)
    dright = flatten(dot(left, diagonal, NT).astype(bf16)).astype(f32)
    dleft, dright = dleft * mask_left, dright * mask_right
    dp = [
        dleft,
        dleft * value_left * (1.0 - gate_left),
        dright,
        dright * value_right * (1.0 - gate_right),
    ]
    dp = jnp.concatenate([d.astype(bf16) for d in dp], axis=1)
    dpt_ref[...] = dp.T
    project_grad = jnp.zeros((KINDS * hidden, LANES), f32)
    for p in range(per):
        at_p = [dpt_ref[pl.ds(kind * LANES + p * hidden, hidden), :] for kind in range(KINDS)]
        project_grad += dot(jnp.concatenate(at_p, axis=0), zn_of(p))
    project_grad_ref[...] = project_grad / n

    tiled = [project_t[kind * hidden : (kind + 1) * hidden] for kind in range(KINDS) for _ in range(per)]
    tiled = jnp.concatenate(tiled, axis=0)
    place = iota((n, KINDS * LANES), 1) % LANES // hidden
    for r in range(rows):
        dp_row = jnp.where(place == r, dp[:n], jnp.zeros_like(dp[:n]))
        dzn = dot(dp_row, tiled) + dot(own_dgo[r], gate_weight, NT)
        zhat, zs = normalize(block_refs[0][pl.ds(r * n, n), :].astype(f32))
        u = gain * dzn
        first = jnp.mean(u, axis=-1, keepdims=True)
        second = jnp.mean(u * zhat, axis=-1, keepdims=True)
        pair_ref[r] = zs * (u - first - zhat * second)


def body_whole(
    devices,
    pair_acts,
    token_count,
    input_gain,
    input_bias,
    project_weight,
    gate_weight,
    output_norm_gain,
    output_shift_bias,
    output_weight,
    update_grad,
):
    rows, n, channels = pair_acts.shape
    hidden = output_weight.shape[0]
    f32, bf16 = jnp.float32, jnp.bfloat16
    half = rows * n
    vmem, anywhere = pl.BlockSpec(memory_space=pltpu.VMEM), pl.BlockSpec(memory_space=pl.ANY)
    shape = jax.ShapeDtypeStruct
    sources = [
        pair_acts.reshape(half, channels),
        update_grad.reshape(half, channels),
        input_gain[None],
        input_bias[None],
        project_weight.T,
        gate_weight,
        output_norm_gain[None],
        output_shift_bias[None],
        output_weight,
    ]
    send, gain, bias, project_t, gate_weight, out_gain, out_bias, out_weight = pl.pallas_call(
        load_kernel,
        out_shape=[pltpu.VMEM((2 * half, channels), bf16)] + [pltpu.VMEM(v.shape, v.dtype) for v in sources[2:]],
        in_specs=[anywhere] * len(sources),
        out_specs=[vmem] * (len(sources) - 1),
        scratch_shapes=[pltpu.SemaphoreType.DMA((len(sources),))],
        name="load",
    )(*sources)
    blocks = {0: send}
    step = devices // 2
    while step:
        pairs = [(i, i ^ step) for i in range(devices)]
        blocks.update({d ^ step: lax.ppermute(blocks[d], "row", pairs) for d in list(blocks)})
        step //= 2
    order = sorted(blocks, key=lambda d: (2 * (d >> 1).bit_count() + (d & 1), -d))
    ordered = [blocks[d] for d in order]
    per = LANES // hidden
    tall = n // per * n
    head_blocks = ordered[: devices // 2]
    head_out = (
        pltpu.VMEM((per, tall // 2, channels), bf16),
        pltpu.VMEM((tall // 2, KINDS * LANES), f32),
        pltpu.VMEM((per, tall // 2, channels), f32),
        pltpu.VMEM((channels, per * tall // 2), bf16),
        pltpu.VMEM((KINDS * LANES, per * channels), bf16),
        pltpu.VMEM((LANES, per * channels), bf16),
    )
    head = pl.pallas_call(
        functools.partial(head_kernel, n),
        out_shape=head_out,
        in_specs=[vmem] * (len(head_blocks) + 5),
        out_specs=(vmem,) * len(head_out),
        compiler_params=pltpu.CompilerParams(vmem_limit_bytes=16 << 20),
        name="head",
    )(*head_blocks, gain, bias, project_t, gate_weight, out_weight)
    update, pair_grad, project_grad, gate_grad, output_grad = pl.pallas_call(
        functools.partial(tail_kernel, n, hidden, order),
        out_shape=(
            shape((rows, n, channels), bf16),
            shape((rows, n, channels), f32),
            shape((KINDS * hidden, channels), f32),
            shape((channels, channels), f32),
            shape((hidden, channels), f32),
        ),
        in_specs=[vmem] * (devices + len(head_out)) + [pl.BlockSpec(memory_space=pltpu.SMEM)] + [vmem] * 6,
        out_specs=(vmem,) * 5,
        scratch_shapes=[
            pltpu.VMEM((per, tall // 2, channels), bf16),
            pltpu.VMEM((KINDS * LANES, tall), bf16),
            pltpu.VMEM((n * hidden, n * hidden), bf16),
            pltpu.VMEM((per * tall // 2, channels), bf16),
            pltpu.VMEM((per * tall // 2, channels), bf16),
            pltpu.VMEM((tall, per * channels), bf16),
        ],
        compiler_params=pltpu.CompilerParams(vmem_limit_bytes=32 << 20),
        name="tail",
    )(*ordered, *head, token_count, gain, bias, project_t, gate_weight, out_gain, out_bias)
    return update, pair_grad, project_grad.T, gate_grad, output_grad


def layer_normalize(values, norm_gain, norm_bias, reduce_axis):
    average = jnp.mean(values, axis=reduce_axis, keepdims=True)
    centered = values - average
    variance = jnp.mean(centered * centered, axis=reduce_axis, keepdims=True)
    inv_std = lax.rsqrt(variance + 1e-05)
    normed = centered * inv_std
    return (normed * norm_gain + norm_bias, normed, inv_std)


def norm_backward_pass(upstream, normed, inv_std, norm_gain, reduce_axis):
    scaled = upstream * norm_gain
    first = jnp.mean(scaled, axis=reduce_axis, keepdims=True)
    second = jnp.mean(scaled * normed, axis=reduce_axis, keepdims=True)
    return inv_std * (scaled - first - normed * second)


def body(
    pair_acts,
    token_count,
    input_gain,
    input_bias,
    project_weight,
    gate_weight,
    output_norm_gain,
    output_shift_bias,
    output_weight,
    update_grad,
):
    single_float_format = jnp.float32
    brain_float_sixteen = jnp.bfloat16
    row_count, length, channels = pair_acts.shape
    hidden = output_weight.shape[0]
    row_start = lax.axis_index("row") * row_count
    live_limit = token_count[0]
    row_live = (row_start + jnp.arange(row_count, dtype=jnp.int32) < live_limit).astype(
        single_float_format
    )
    col_live = (jnp.arange(length, dtype=jnp.int32) < live_limit).astype(single_float_format)
    live_mask = row_live[:, None] * col_live[None, :]
    zn32, zhat, zscale = layer_normalize(
        pair_acts.astype(single_float_format), input_gain, input_bias, -1
    )
    normed_pair = zn32.astype(brain_float_sixteen)
    projected = jnp.einsum(
        "rkd,de->erk", normed_pair, project_weight, preferred_element_type=single_float_format
    ).reshape(4, hidden, row_count, length)
    gate_left = jax.nn.sigmoid(projected[1])
    gate_right = jax.nn.sigmoid(projected[3])
    left_panel = (live_mask * gate_left * projected[0]).astype(brain_float_sixteen)
    right_panel = (live_mask * gate_right * projected[2]).astype(brain_float_sixteen)
    stacked = jnp.stack([left_panel, right_panel], axis=1)
    columns = lax.all_to_all(stacked, "row", split_axis=0, concat_axis=2, tiled=True)
    left_cols = columns[:, 0]
    right_cols = columns[:, 1]
    products = jnp.einsum(
        "cik,cjk->cij", left_cols, right_cols, preferred_element_type=single_float_format
    ).astype(brain_float_sixteen)
    triangle_product = lax.all_to_all(products, "row", split_axis=1, concat_axis=0, tiled=True)
    normed_input_single, standardized_input, input_inverse_scale = layer_normalize(
        triangle_product.astype(single_float_format),
        output_norm_gain[:, None, None],
        output_shift_bias[:, None, None],
        0,
    )
    normed_tri = normed_input_single.astype(brain_float_sixteen)
    mixed = jnp.einsum(
        "crk,cd->rkd", normed_tri, output_weight, preferred_element_type=single_float_format
    )
    gate_out = jax.nn.sigmoid(
        jnp.einsum(
            "rkd,de->rke", normed_pair, gate_weight, preferred_element_type=single_float_format
        )
    )
    update = (gate_out * mixed).astype(brain_float_sixteen)
    cotangent = update_grad.astype(single_float_format)
    mixed_grad = (cotangent * gate_out).astype(brain_float_sixteen)
    gate_logit_grad = (cotangent * mixed * gate_out * (1.0 - gate_out)).astype(brain_float_sixteen)
    output_terms = jnp.einsum(
        "crk,rkd->cd", normed_tri, mixed_grad, preferred_element_type=single_float_format
    )
    triangle_normed_gradient = jnp.einsum(
        "rkd,cd->crk", mixed_grad, output_weight, preferred_element_type=single_float_format
    )
    triangle_gradient = norm_backward_pass(
        triangle_normed_gradient,
        standardized_input,
        input_inverse_scale,
        output_norm_gain[:, None, None],
        0,
    ).astype(brain_float_sixteen)
    grad_cols = lax.all_to_all(triangle_gradient, "row", split_axis=0, concat_axis=1, tiled=True)
    left_col_grad = jnp.einsum(
        "cij,cjk->cik", grad_cols, right_cols, preferred_element_type=single_float_format
    ).astype(brain_float_sixteen)
    right_col_grad = jnp.einsum(
        "cij,cik->cjk", grad_cols, left_cols, preferred_element_type=single_float_format
    ).astype(brain_float_sixteen)
    returned = lax.all_to_all(
        jnp.stack([left_col_grad, right_col_grad], axis=1),
        "row",
        split_axis=2,
        concat_axis=0,
        tiled=True,
    )
    left_grad = returned[:, 0].astype(single_float_format)
    right_grad = returned[:, 1].astype(single_float_format)
    project_terms = jnp.stack(
        [
            left_grad * live_mask * gate_left,
            left_grad * live_mask * projected[0] * gate_left * (1.0 - gate_left),
            right_grad * live_mask * gate_right,
            right_grad * live_mask * projected[2] * gate_right * (1.0 - gate_right),
        ]
    )
    project_terms = project_terms.astype(brain_float_sixteen).reshape(4 * hidden, row_count, length)
    project_part = jnp.einsum(
        "rkd,erk->de", normed_pair, project_terms, preferred_element_type=single_float_format
    )
    gate_part = jnp.einsum(
        "rkd,rke->de", normed_pair, gate_logit_grad, preferred_element_type=single_float_format
    )
    totals = lax.psum((project_part, gate_part, output_terms), "row")
    project_grad = totals[0] / length
    gate_grad = totals[1] / length
    output_grad = totals[2] / length
    normed_grad = jnp.einsum(
        "erk,de->rkd", project_terms, project_weight, preferred_element_type=single_float_format
    ) + jnp.einsum(
        "rke,de->rkd", gate_logit_grad, gate_weight, preferred_element_type=single_float_format
    )
    pair_grad = norm_backward_pass(normed_grad, zhat, zscale, input_gain, -1)
    return (update, pair_grad, project_grad, gate_grad, output_grad)


def fits_whole(mesh, args):
    pair_acts, output_weight = args[0], args[8]
    devices = mesh.shape["row"]
    length, channels = pair_acts.shape[0] // mesh.shape["grp"], pair_acts.shape[2]
    hidden = output_weight.shape[0]
    return (
        channels == LANES
        and hidden % 16 == 0
        and LANES % hidden == 0
        and length % (LANES // hidden) == 0
        and (LANES // hidden) % 8 == 0
        and length % 16 == 0
        and devices & (devices - 1) == 0
        and length % devices == 0
        and length // devices <= LANES // hidden
        and devices >= 4
        and length // 2 % (LANES // hidden) == 0
        and 2 * pair_acts.dtype.itemsize * length * length * channels <= WHOLE_BYTES
    )


def solution(mesh):
    in_specs = (
        P(("grp", "row"), None, None),
        P("grp"),
        P(),
        P(),
        P(),
        P(),
        P(),
        P(),
        P(),
        P(("grp", "row"), None, None),
    )
    out_specs = (
        P(("grp", "row"), None, None),
        P(("grp", "row"), None, None),
        P("grp", None),
        P("grp", None),
        P("grp", None),
    )
    devices = mesh.shape["row"]

    def run(*args):
        crop = functools.partial(body_whole, devices) if fits_whole(mesh, args) else body
        return jax.shard_map(crop, mesh=mesh, in_specs=in_specs, out_specs=out_specs, check_vma=False)(*args)

    return run
```

```python
import functools

import jax
import jax.numpy as jnp
from jax import lax
from jax.experimental import pallas as pl
from jax.experimental.pallas import tpu as pltpu
from jax.sharding import PartitionSpec as P

LANES = 128
KINDS = 4
WHOLE_BYTES = 4 << 20

NN = (((1,), (0,)), ((), ()))
NT = (((1,), (1,)), ((), ()))
TN = (((0,), (0,)), ((), ()))


def dot(a, b, dims=NN):
    return lax.dot_general(a, b, dims, preferred_element_type=jnp.float32)


def dot_split(a, b_twice):
    high = a.astype(jnp.bfloat16)
    low = (a - high.astype(jnp.float32)).astype(jnp.bfloat16)
    return dot(jnp.concatenate([high, low], axis=1), b_twice)


def iota(shape, dim):
    return lax.broadcasted_iota(jnp.int32, shape, dim)


def zero_one(condition):
    return jnp.where(condition, 1.0, 0.0).astype(jnp.bfloat16)


def sigmoid(v):
    return 0.5 * jnp.tanh(0.5 * v) + 0.5


def normalize(v):
    centered = v - jnp.mean(v, axis=-1, keepdims=True)
    s = lax.rsqrt(jnp.mean(centered * centered, axis=-1, keepdims=True) + 1e-05)
    return centered * s, s


def row_of(order, rows, t):
    return (lax.axis_index("row") ^ order[t // rows]) * rows + t % rows


def rows_of_lanes(order, rows, hidden, group):
    per = LANES // hidden
    place = iota((1, LANES), 1) // hidden
    at = jnp.full((1, LANES), row_of(order, rows, group * per), jnp.int32)
    for p in range(1, per):
        at = jnp.where(place == p, row_of(order, rows, group * per + p), at)
    return at


def stage(n, hidden, order, first, block_refs, count, gain, bias, project_wide, out_wide, gate_weight, refs):
    left_ref, right_ref, mask_ref, slope_ref, dy_ref, dgo_part_ref, dxn_ref, znt_ref = refs
    f32, bf16 = jnp.float32, jnp.bfloat16
    per = LANES // hidden
    rows = n // len(order)
    tall = left_ref.shape[0]
    start = first * per
    zn, cotangent = {}, {}
    for t in range(start, start + per * (tall // n)):
        block, at = block_refs[t // rows - start // rows], t % rows * n
        zn[t] = (normalize(block[pl.ds(at, n), :].astype(f32))[0] * gain + bias).astype(bf16)
        cotangent[t] = block[pl.ds((rows + t % rows) * n, n), :]

    def place(tiles, p):
        return jnp.concatenate([tiles[t] for t in range(start + p, start + per * (tall // n), per)], axis=0)

    zn = [place(zn, p) for p in range(per)]
    projected = dot(jnp.concatenate(zn, axis=1), project_wide, NT)
    live_k = iota((n, LANES), 0) < count
    mask = [
        jnp.where(live_k & (rows_of_lanes(order, rows, hidden, first + g) < count), 1.0, 0.0) for g in range(tall // n)
    ]
    mask = jnp.concatenate(mask, axis=0)
    for side, ref in enumerate((left_ref, right_ref)):
        value = projected[:, 2 * side * LANES : (2 * side + 1) * LANES]
        gate = sigmoid(projected[:, (2 * side + 1) * LANES : (2 * side + 2) * LANES])
        ref[...] = (mask * gate * value).astype(bf16)
        mask_ref[side] = mask * gate
        slope_ref[side] = value * (1.0 - gate)
    own = []
    zn_tall = jnp.concatenate(zn, axis=0)
    gates = sigmoid(dot(zn_tall, gate_weight))
    for p in range(per):
        go = gates[p * tall : (p + 1) * tall]
        dy = place(cotangent, p).astype(f32) * go
        dy_ref[:, p * LANES : (p + 1) * LANES] = dy.astype(bf16)
        dgo_part_ref[p] = dy * (1.0 - go)
        own.append(go[:n])
    dxn_ref[...] = dot(dy_ref[...], out_wide, NT)
    half = per // 2 * tall
    znt_ref[0] = zn_tall[:half].T
    znt_ref[1] = zn_tall[half:].T
    return own


def wide_project(project_t, per):
    hidden, channels = project_t.shape[0] // KINDS, project_t.shape[1]
    columns = []
    for p in range(per):
        parts = []
        for kind in range(KINDS):
            before, after = p * hidden, (per - 1 - p) * hidden
            parts += [jnp.zeros((before, channels), project_t.dtype)] * (before > 0)
            parts += [project_t[kind * hidden : (kind + 1) * hidden]]
            parts += [jnp.zeros((after, channels), project_t.dtype)] * (after > 0)
        columns.append(jnp.concatenate(parts, axis=0))
    return jnp.concatenate(columns, axis=1)


def wide_out(out_weight, per):
    hidden, channels = out_weight.shape
    rows = []
    for p in range(per):
        before, after = p * channels, (per - 1 - p) * channels
        parts = [jnp.zeros((hidden, before), out_weight.dtype)] * (before > 0) + [out_weight]
        rows.append(jnp.concatenate(parts + [jnp.zeros((hidden, after), out_weight.dtype)] * (after > 0), axis=1))
    return jnp.concatenate(rows, axis=0)


def pick_place(per, hidden):
    half, width = per // 2, KINDS * hidden
    a, b = iota((KINDS * LANES, LANES), 0), iota((KINDS * LANES, LANES), 1)
    own = (a // LANES == b % width // hidden) & (a % hidden == b % hidden)
    place = a % LANES // hidden
    return jnp.concatenate([zero_one(own & (place == b // width * half + q)) for q in range(half)], axis=1)


def load_kernel(*refs):
    count = len(refs) // 2
    sources, targets, sems = refs[:count], refs[count : 2 * count - 1], refs[-1]
    half = sources[0].shape[0]
    targets = [targets[0].at[pl.ds(0, half)], targets[0].at[pl.ds(half, half)], *targets[1:]]
    copies = [pltpu.make_async_copy(a, b, sems.at[k]) for k, (a, b) in enumerate(zip(sources, targets))]
    for copy in copies:
        copy.start()
    for copy in copies:
        copy.wait()


def head_kernel(n, hidden, order, *refs):
    *block_refs, count_ref, gain_ref, bias_ref, project_ref, gate_ref, out_weight_ref = refs[:-12]
    *stage_refs, project_wide_ref, out_wide_ref, pick_ref, own_ref = refs[-12:]
    per = LANES // hidden
    project_wide_ref[...] = wide_project(project_ref[...], per)
    out_wide_ref[...] = wide_out(out_weight_ref[...], per)
    pick_ref[...] = pick_place(per, hidden)
    weights = [ref[...] for ref in (gain_ref, bias_ref, project_wide_ref, out_wide_ref, gate_ref)]
    own = stage(n, hidden, order, 0, block_refs, count_ref[0], *weights, stage_refs)
    for r in range(own_ref.shape[0]):
        own_ref[r] = own[r]


def middle_kernel(n, hidden, order, first, *refs):
    *block_refs, count_ref, gain_ref, bias_ref, project_wide_ref, out_wide_ref, gate_ref = refs[:-8]
    weights = [ref[...] for ref in (gain_ref, bias_ref, project_wide_ref, out_wide_ref, gate_ref)]
    stage(n, hidden, order, first, block_refs, count_ref[0], *weights, refs[-8:])


def tail_kernel(n, hidden, order, cuts, *refs):
    blocks = len(order)
    block_refs, refs = refs[:blocks], refs[blocks:]
    head_refs, (project_wide_ref, out_wide_ref, pick_ref, own_ref), middle_refs = refs[:8], refs[8:12], refs[12:20]
    count_ref, gain_ref, bias_ref, project_ref, gate_ref, out_gain_ref, out_bias_ref = refs[20:27]
    update_ref, pair_ref, project_grad_ref, gate_grad_ref, out_grad_ref = refs[27:32]
    tail_refs, (square_ref, dgo_ref, dp_ref, dx_ref) = refs[32:40], refs[40:]
    stages = (head_refs, middle_refs, tail_refs)
    f32, bf16 = jnp.float32, jnp.bfloat16
    per = LANES // hidden
    groups = n // per
    wide = n * hidden
    rows = n // blocks
    gain, gate_weight, project_t = gain_ref[...], gate_ref[...], project_ref[...]
    weights = gain, bias_ref[...], project_wide_ref[...], out_wide_ref[...], gate_weight
    stage(n, hidden, order, cuts[1], block_refs[cuts[1] * per // rows :], count_ref[0], *weights, tail_refs)

    spans = [(low * n, high * n) for low, high in zip((0, *cuts), (*cuts, groups))]
    half = per // 2

    def put(ref, q, column, value):
        for low, high in spans:
            ref[pl.ds(low * half + q * (high - low), high - low), pl.ds(column, LANES)] = value[low:high]

    def sum_pairs(ref):
        znt = [refs[7][...].reshape(2 * LANES, half * (high - low)) for refs, (low, high) in zip(stages, spans)]
        rows_of = [ref[pl.ds(low * half, (high - low) * half), :] for low, high in spans]
        return sum(dot(a, b) for a, b in zip(znt, rows_of))

    def all_rows(k):
        return jnp.concatenate([refs[k][...] for refs in stages], axis=0)

    row_i = [rows_of_lanes(order, rows, hidden, g) for g in range(groups)]

    def lanes(flat):
        return jnp.concatenate([flat[g * n : (g + 1) * n] for g in range(groups)], axis=1)

    def flatten(rowed):
        return jnp.concatenate([rowed[:, g * LANES : (g + 1) * LANES] for g in range(groups)], axis=0)

    left, right = lanes(all_rows(0)), lanes(all_rows(1))

    same = iota((LANES, wide), 0) % hidden == iota((LANES, wide), 1) % hidden

    def keep_same(square):
        for g in range(groups):
            part = square[g * LANES : (g + 1) * LANES].astype(bf16)
            square_ref[pl.ds(g * LANES, LANES), :] = jnp.where(same, part, jnp.zeros_like(part))

    keep_same(dot(right, left, TN))
    pick = jnp.concatenate([zero_one(iota((n, LANES), 0) == at) for at in row_i], axis=1)
    x = flatten(dot(pick, square_ref[...]))

    mean = jnp.where(iota((LANES, LANES), 0) // hidden == iota((LANES, LANES), 1) // hidden, 1.0 / hidden, 0.0)
    mean = mean.astype(bf16)
    mean_twice = jnp.concatenate([mean, mean], axis=0)
    out_gain = jnp.concatenate([out_gain_ref[...]] * per, axis=1)
    out_bias = jnp.concatenate([out_bias_ref[...]] * per, axis=1)
    centered = x - dot(x.astype(bf16), mean)
    xs = lax.rsqrt(dot_split(centered * centered, mean_twice) + 1e-05)
    xhat = centered * xs
    xn = (xhat * out_gain + out_bias).astype(bf16)

    y_all = dot(xn, out_wide_ref[...])
    own_dgo = []
    for p in range(per):
        y = y_all[:, p * LANES : (p + 1) * LANES]
        dgo = (jnp.concatenate([refs[5][p] for refs in stages], axis=0) * y).astype(bf16)
        put(dgo_ref, p % half, p // half * LANES, dgo)
        if p < rows:
            update_ref[p] = (own_ref[p] * y[:n]).astype(bf16)
            own_dgo.append(dgo[:n])
    out_grad = dot(xn, all_rows(4), TN)
    out_grad = [out_grad[p * hidden : (p + 1) * hidden, p * LANES : (p + 1) * LANES] for p in range(per)]
    out_grad_ref[...] = sum(out_grad) / n
    gate_grad = sum_pairs(dgo_ref)
    gate_grad_ref[...] = (gate_grad[:LANES, :LANES] + gate_grad[LANES:, LANES:]) / n

    u = out_gain * all_rows(6)
    dx = xs * (u - dot_split(u, mean_twice) - xhat * dot_split(u * xhat, mean_twice))
    dx_ref[...] = lanes(dx.astype(bf16)).astype(f32)

    for t in range(n):
        row = dx_ref[pl.ds(row_of(order, rows, t), 1), :]
        row = jnp.broadcast_to(row, (hidden, wide)).astype(bf16)
        square_ref[pl.ds(t * hidden, hidden), :] = jnp.where(same[:hidden], row, jnp.zeros_like(row))
    diagonal = square_ref[...]
    dleft = flatten(dot(right, diagonal).astype(bf16)).astype(f32)
    dright = flatten(dot(left, diagonal, NT).astype(bf16)).astype(f32)
    dp = []
    for side, grad in enumerate((dleft, dright)):
        masked = grad * jnp.concatenate([refs[2][side] for refs in stages], axis=0)
        dp += [masked, masked * jnp.concatenate([refs[3][side] for refs in stages], axis=0)]
    dp = jnp.concatenate([d.astype(bf16) for d in dp], axis=1)
    by_place = dot(dp, pick_ref[...]).astype(bf16)
    for q in range(half):
        put(dp_ref, q, 0, by_place[:, q * LANES : (q + 1) * LANES])
    project_grad = sum_pairs(dp_ref).T
    width = KINDS * hidden
    project_grad_ref[...] = (project_grad[:width, :LANES] + project_grad[width:, LANES:]) / n

    tiled = [project_t[kind * hidden : (kind + 1) * hidden] for kind in range(KINDS) for _ in range(per)]
    place = iota((n, KINDS * LANES), 1) % LANES // hidden
    dp_rows = [jnp.where(place == r, dp[:n], jnp.zeros_like(dp[:n])) for r in range(rows)]
    dzn = dot(jnp.concatenate(dp_rows, axis=0), jnp.concatenate(tiled, axis=0))
    dzn += dot(jnp.concatenate(own_dgo, axis=0), gate_weight, NT)
    zhat, zs = normalize(block_refs[0][pl.ds(0, rows * n), :].astype(f32))
    u = gain * dzn
    first = jnp.mean(u, axis=-1, keepdims=True)
    second = jnp.mean(u * zhat, axis=-1, keepdims=True)
    pair_grad = zs * (u - first - zhat * second)
    for r in range(rows):
        pair_ref[r] = pair_grad[r * n : (r + 1) * n]


def body_whole(
    devices,
    pair_acts,
    token_count,
    input_gain,
    input_bias,
    project_weight,
    gate_weight,
    output_norm_gain,
    output_shift_bias,
    output_weight,
    update_grad,
):
    rows, n, channels = pair_acts.shape
    hidden = output_weight.shape[0]
    f32, bf16 = jnp.float32, jnp.bfloat16
    half = rows * n
    vmem, anywhere = pl.BlockSpec(memory_space=pltpu.VMEM), pl.BlockSpec(memory_space=pl.ANY)
    shape = jax.ShapeDtypeStruct
    sources = [
        pair_acts.reshape(half, channels),
        update_grad.reshape(half, channels),
        input_gain[None],
        input_bias[None],
        project_weight.T,
        gate_weight,
        output_norm_gain[None],
        output_shift_bias[None],
        output_weight,
    ]
    send, gain, bias, project_t, gate_weight, out_gain, out_bias, out_weight = pl.pallas_call(
        load_kernel,
        out_shape=[pltpu.VMEM((2 * half, channels), bf16)] + [pltpu.VMEM(v.shape, v.dtype) for v in sources[2:]],
        in_specs=[anywhere] * len(sources),
        out_specs=[vmem] * (len(sources) - 1),
        scratch_shapes=[pltpu.SemaphoreType.DMA((len(sources),))],
        name="load",
    )(*sources)
    blocks = {0: send}
    core, x, *z = [1 << bit for bit in range(devices.bit_length() - 1)]

    def hop(step, sources):
        pairs = [(i, i ^ step) for i in range(devices)]
        for d in sources:
            blocks[d ^ step] = lax.ppermute(blocks[d], "row", pairs)

    for step in reversed(z):
        hop(step, [0])
    hop(x, [0])
    for k, step in enumerate(z[:-1]):
        hop(step, [x])
        hop(step, [d for d in list(blocks) if 0 < d and d % (2 * step) == 0])
    hop(x, [d for d in list(blocks) if not d & x and d ^ x not in blocks])
    hop(core, [d for d in list(blocks) if d != devices - 2])
    order = sorted(range(devices), key=lambda d: (2 * d.bit_count() + (d & x) / x, -(d & core), -d))
    blocks[devices - 1] = None
    ordered = [blocks[d] for d in order]
    per = LANES // hidden
    groups = n // per
    cuts = (groups // 2, groups - 1)

    def stage_out(count):
        tall = count * n
        return (
            pltpu.VMEM((tall, LANES), bf16),
            pltpu.VMEM((tall, LANES), bf16),
            pltpu.VMEM((2, tall, LANES), f32),
            pltpu.VMEM((2, tall, LANES), f32),
            pltpu.VMEM((tall, per * channels), bf16),
            pltpu.VMEM((per, tall, channels), f32),
            pltpu.VMEM((tall, LANES), f32),
            pltpu.VMEM((2, channels, per // 2 * tall), bf16),
        )

    def span(first, last):
        return ordered[first * per // rows : -(-last * per // rows)]

    head_in = [*span(0, cuts[0]), token_count, gain, bias, project_t, gate_weight, out_weight]
    smem = pl.BlockSpec(memory_space=pltpu.SMEM)
    head_out = (
        *stage_out(cuts[0]),
        pltpu.VMEM((KINDS * LANES, per * channels), bf16),
        pltpu.VMEM((LANES, per * channels), bf16),
        pltpu.VMEM((KINDS * LANES, per // 2 * LANES), bf16),
        pltpu.VMEM((rows, n, channels), f32),
    )
    head = pl.pallas_call(
        functools.partial(head_kernel, n, hidden, order),
        out_shape=head_out,
        in_specs=[vmem] * (len(head_in) - 6) + [smem] + [vmem] * 5,
        out_specs=(vmem,) * len(head_out),
        compiler_params=pltpu.CompilerParams(vmem_limit_bytes=16 << 20),
        name="head",
    )(*head_in)
    blocks[devices - 2], head = lax.optimization_barrier((blocks[devices - 2], head))
    hop(core, [devices - 2])
    ordered = [blocks[d] for d in order]
    middle_in = [*span(*cuts), token_count, gain, bias, head[8], head[9], gate_weight]
    middle_out = stage_out(cuts[1] - cuts[0])
    middle = pl.pallas_call(
        functools.partial(middle_kernel, n, hidden, order, cuts[0]),
        out_shape=middle_out,
        in_specs=[vmem] * (len(middle_in) - 6) + [smem] + [vmem] * 5,
        out_specs=(vmem,) * len(middle_out),
        compiler_params=pltpu.CompilerParams(vmem_limit_bytes=16 << 20),
        name="middle",
    )(*middle_in)
    tall = groups * n
    update, pair_grad, project_grad, gate_grad, output_grad = pl.pallas_call(
        functools.partial(tail_kernel, n, hidden, order, cuts),
        out_shape=(
            shape((rows, n, channels), bf16),
            shape((rows, n, channels), f32),
            shape((KINDS * hidden, channels), f32),
            shape((channels, channels), f32),
            shape((hidden, channels), f32),
        ),
        in_specs=[vmem] * (devices + len(head) + len(middle)) + [smem] + [vmem] * 6,
        out_specs=(vmem,) * 5,
        scratch_shapes=[
            *stage_out(groups - cuts[1]),
            pltpu.VMEM((n * hidden, n * hidden), bf16),
            pltpu.VMEM((per // 2 * tall, 2 * channels), bf16),
            pltpu.VMEM((per // 2 * tall, LANES), bf16),
            pltpu.VMEM((n, n * hidden), f32),
        ],
        compiler_params=pltpu.CompilerParams(vmem_limit_bytes=32 << 20),
        name="tail",
    )(*ordered, *head, *middle, token_count, gain, bias, project_t, gate_weight, out_gain, out_bias)
    return update, pair_grad, project_grad.T, gate_grad, output_grad


def layer_normalize(values, norm_gain, norm_bias, reduce_axis):
    average = jnp.mean(values, axis=reduce_axis, keepdims=True)
    centered = values - average
    variance = jnp.mean(centered * centered, axis=reduce_axis, keepdims=True)
    inv_std = lax.rsqrt(variance + 1e-05)
    normed = centered * inv_std
    return (normed * norm_gain + norm_bias, normed, inv_std)


def norm_backward_pass(upstream, normed, inv_std, norm_gain, reduce_axis):
    scaled = upstream * norm_gain
    first = jnp.mean(scaled, axis=reduce_axis, keepdims=True)
    second = jnp.mean(scaled * normed, axis=reduce_axis, keepdims=True)
    return inv_std * (scaled - first - normed * second)


def body(
    pair_acts,
    token_count,
    input_gain,
    input_bias,
    project_weight,
    gate_weight,
    output_norm_gain,
    output_shift_bias,
    output_weight,
    update_grad,
):
    single_float_format = jnp.float32
    brain_float_sixteen = jnp.bfloat16
    row_count, length, channels = pair_acts.shape
    hidden = output_weight.shape[0]
    row_start = lax.axis_index("row") * row_count
    live_limit = token_count[0]
    row_live = (row_start + jnp.arange(row_count, dtype=jnp.int32) < live_limit).astype(
        single_float_format
    )
    col_live = (jnp.arange(length, dtype=jnp.int32) < live_limit).astype(single_float_format)
    live_mask = row_live[:, None] * col_live[None, :]
    zn32, zhat, zscale = layer_normalize(
        pair_acts.astype(single_float_format), input_gain, input_bias, -1
    )
    normed_pair = zn32.astype(brain_float_sixteen)
    projected = jnp.einsum(
        "rkd,de->erk", normed_pair, project_weight, preferred_element_type=single_float_format
    ).reshape(4, hidden, row_count, length)
    gate_left = jax.nn.sigmoid(projected[1])
    gate_right = jax.nn.sigmoid(projected[3])
    left_panel = (live_mask * gate_left * projected[0]).astype(brain_float_sixteen)
    right_panel = (live_mask * gate_right * projected[2]).astype(brain_float_sixteen)
    stacked = jnp.stack([left_panel, right_panel], axis=1)
    columns = lax.all_to_all(stacked, "row", split_axis=0, concat_axis=2, tiled=True)
    left_cols = columns[:, 0]
    right_cols = columns[:, 1]
    products = jnp.einsum(
        "cik,cjk->cij", left_cols, right_cols, preferred_element_type=single_float_format
    ).astype(brain_float_sixteen)
    triangle_product = lax.all_to_all(products, "row", split_axis=1, concat_axis=0, tiled=True)
    normed_input_single, standardized_input, input_inverse_scale = layer_normalize(
        triangle_product.astype(single_float_format),
        output_norm_gain[:, None, None],
        output_shift_bias[:, None, None],
        0,
    )
    normed_tri = normed_input_single.astype(brain_float_sixteen)
    mixed = jnp.einsum(
        "crk,cd->rkd", normed_tri, output_weight, preferred_element_type=single_float_format
    )
    gate_out = jax.nn.sigmoid(
        jnp.einsum(
            "rkd,de->rke", normed_pair, gate_weight, preferred_element_type=single_float_format
        )
    )
    update = (gate_out * mixed).astype(brain_float_sixteen)
    cotangent = update_grad.astype(single_float_format)
    mixed_grad = (cotangent * gate_out).astype(brain_float_sixteen)
    gate_logit_grad = (cotangent * mixed * gate_out * (1.0 - gate_out)).astype(brain_float_sixteen)
    output_terms = jnp.einsum(
        "crk,rkd->cd", normed_tri, mixed_grad, preferred_element_type=single_float_format
    )
    triangle_normed_gradient = jnp.einsum(
        "rkd,cd->crk", mixed_grad, output_weight, preferred_element_type=single_float_format
    )
    triangle_gradient = norm_backward_pass(
        triangle_normed_gradient,
        standardized_input,
        input_inverse_scale,
        output_norm_gain[:, None, None],
        0,
    ).astype(brain_float_sixteen)
    grad_cols = lax.all_to_all(triangle_gradient, "row", split_axis=0, concat_axis=1, tiled=True)
    left_col_grad = jnp.einsum(
        "cij,cjk->cik", grad_cols, right_cols, preferred_element_type=single_float_format
    ).astype(brain_float_sixteen)
    right_col_grad = jnp.einsum(
        "cij,cik->cjk", grad_cols, left_cols, preferred_element_type=single_float_format
    ).astype(brain_float_sixteen)
    returned = lax.all_to_all(
        jnp.stack([left_col_grad, right_col_grad], axis=1),
        "row",
        split_axis=2,
        concat_axis=0,
        tiled=True,
    )
    left_grad = returned[:, 0].astype(single_float_format)
    right_grad = returned[:, 1].astype(single_float_format)
    project_terms = jnp.stack(
        [
            left_grad * live_mask * gate_left,
            left_grad * live_mask * projected[0] * gate_left * (1.0 - gate_left),
            right_grad * live_mask * gate_right,
            right_grad * live_mask * projected[2] * gate_right * (1.0 - gate_right),
        ]
    )
    project_terms = project_terms.astype(brain_float_sixteen).reshape(4 * hidden, row_count, length)
    project_part = jnp.einsum(
        "rkd,erk->de", normed_pair, project_terms, preferred_element_type=single_float_format
    )
    gate_part = jnp.einsum(
        "rkd,rke->de", normed_pair, gate_logit_grad, preferred_element_type=single_float_format
    )
    totals = lax.psum((project_part, gate_part, output_terms), "row")
    project_grad = totals[0] / length
    gate_grad = totals[1] / length
    output_grad = totals[2] / length
    normed_grad = jnp.einsum(
        "erk,de->rkd", project_terms, project_weight, preferred_element_type=single_float_format
    ) + jnp.einsum(
        "rke,de->rkd", gate_logit_grad, gate_weight, preferred_element_type=single_float_format
    )
    pair_grad = norm_backward_pass(normed_grad, zhat, zscale, input_gain, -1)
    return (update, pair_grad, project_grad, gate_grad, output_grad)


def fits_whole(mesh, args):
    pair_acts, output_weight = args[0], args[8]
    devices = mesh.shape["row"]
    length, channels = pair_acts.shape[0] // mesh.shape["grp"], pair_acts.shape[2]
    hidden = output_weight.shape[0]
    return (
        channels == LANES
        and hidden % 16 == 0
        and LANES % hidden == 0
        and length % (LANES // hidden) == 0
        and (LANES // hidden) % 8 == 0
        and length % 16 == 0
        and devices & (devices - 1) == 0
        and length % devices == 0
        and length // devices <= LANES // hidden
        and devices >= 4
        and length // 2 % (LANES // hidden) == 0
        and 2 * pair_acts.dtype.itemsize * length * length * channels <= WHOLE_BYTES
    )


def solution(mesh):
    in_specs = (
        P(("grp", "row"), None, None),
        P("grp"),
        P(),
        P(),
        P(),
        P(),
        P(),
        P(),
        P(),
        P(("grp", "row"), None, None),
    )
    out_specs = (
        P(("grp", "row"), None, None),
        P(("grp", "row"), None, None),
        P("grp", None),
        P("grp", None),
        P("grp", None),
    )
    devices = mesh.shape["row"]

    def run(*args):
        crop = functools.partial(body_whole, devices) if fits_whole(mesh, args) else body
        return jax.shard_map(crop, mesh=mesh, in_specs=in_specs, out_specs=out_specs, check_vma=False)(*args)

    return run
```

```python
import functools

import jax
import jax.numpy as jnp
from jax import lax
from jax.experimental import pallas as pl
from jax.experimental.pallas import tpu as pltpu
from jax.sharding import PartitionSpec as P

LANES = 128
KINDS = 4
WHOLE_BYTES = 4 << 20

NN = (((1,), (0,)), ((), ()))
NT = (((1,), (1,)), ((), ()))
TN = (((0,), (0,)), ((), ()))


def dot(a, b, dims=NN):
    return lax.dot_general(a, b, dims, preferred_element_type=jnp.float32)


def dot_split(a, b_twice):
    high = a.astype(jnp.bfloat16)
    low = (a - high.astype(jnp.float32)).astype(jnp.bfloat16)
    return dot(jnp.concatenate([high, low], axis=1), b_twice)


def iota(shape, dim):
    return lax.broadcasted_iota(jnp.int32, shape, dim)


def zero_one(condition):
    return jnp.where(condition, 1.0, 0.0).astype(jnp.bfloat16)


def sigmoid(v):
    return 0.5 * jnp.tanh(0.5 * v) + 0.5


def normalize(v):
    centered = v - jnp.mean(v, axis=-1, keepdims=True)
    s = lax.rsqrt(jnp.mean(centered * centered, axis=-1, keepdims=True) + 1e-05)
    return centered * s, s


def row_of(order, rows, t):
    return (lax.axis_index("row") ^ order[t // rows]) * rows + t % rows


def rows_of_lanes(order, rows, hidden, group):
    per = LANES // hidden
    place = iota((1, LANES), 1) // hidden
    at = jnp.full((1, LANES), row_of(order, rows, group * per), jnp.int32)
    for p in range(1, per):
        at = jnp.where(place == p, row_of(order, rows, group * per + p), at)
    return at


def stage(n, hidden, order, first, block_refs, count, gain, bias, project_wide, out_wide, gate_weight, refs):
    left_ref, right_ref, mask_ref, slope_ref, dy_ref, dgo_part_ref, dxn_ref, znt_ref = refs
    f32, bf16 = jnp.float32, jnp.bfloat16
    per = LANES // hidden
    rows = n // len(order)
    tall = left_ref.shape[0]
    start = first * per
    zn, cotangent = {}, {}
    for t in range(start, start + per * (tall // n)):
        block, at = block_refs[t // rows - start // rows], t % rows * n
        zn[t] = (normalize(block[pl.ds(at, n), :].astype(f32))[0] * gain + bias).astype(bf16)
        cotangent[t] = block[pl.ds((rows + t % rows) * n, n), :]

    def place(tiles, p):
        return jnp.concatenate([tiles[t] for t in range(start + p, start + per * (tall // n), per)], axis=0)

    zn = [place(zn, p) for p in range(per)]
    projected = dot(jnp.concatenate(zn, axis=1), project_wide, NT)
    live_k = iota((n, LANES), 0) < count
    mask = [
        jnp.where(live_k & (rows_of_lanes(order, rows, hidden, first + g) < count), 1.0, 0.0) for g in range(tall // n)
    ]
    mask = jnp.concatenate(mask, axis=0)
    for side, ref in enumerate((left_ref, right_ref)):
        value = projected[:, 2 * side * LANES : (2 * side + 1) * LANES]
        gate = sigmoid(projected[:, (2 * side + 1) * LANES : (2 * side + 2) * LANES])
        ref[...] = (mask * gate * value).astype(bf16)
        mask_ref[side] = mask * gate
        slope_ref[side] = value * (1.0 - gate)
    own = []
    zn_tall = jnp.concatenate(zn, axis=0)
    gates = sigmoid(dot(zn_tall, gate_weight))
    for p in range(per):
        go = gates[p * tall : (p + 1) * tall]
        dy = place(cotangent, p).astype(f32) * go
        dy_ref[:, p * LANES : (p + 1) * LANES] = dy.astype(bf16)
        dgo_part_ref[p] = dy * (1.0 - go)
        own.append(go[:n])
    dxn_ref[...] = dot(dy_ref[...], out_wide, NT)
    half = per // 2 * tall
    znt_ref[0] = zn_tall[:half].T
    znt_ref[1] = zn_tall[half:].T
    return own


def wide_project(project_t, per):
    hidden, channels = project_t.shape[0] // KINDS, project_t.shape[1]
    columns = []
    for p in range(per):
        parts = []
        for kind in range(KINDS):
            before, after = p * hidden, (per - 1 - p) * hidden
            parts += [jnp.zeros((before, channels), project_t.dtype)] * (before > 0)
            parts += [project_t[kind * hidden : (kind + 1) * hidden]]
            parts += [jnp.zeros((after, channels), project_t.dtype)] * (after > 0)
        columns.append(jnp.concatenate(parts, axis=0))
    return jnp.concatenate(columns, axis=1)


def wide_out(out_weight, per):
    hidden, channels = out_weight.shape
    rows = []
    for p in range(per):
        before, after = p * channels, (per - 1 - p) * channels
        parts = [jnp.zeros((hidden, before), out_weight.dtype)] * (before > 0) + [out_weight]
        rows.append(jnp.concatenate(parts + [jnp.zeros((hidden, after), out_weight.dtype)] * (after > 0), axis=1))
    return jnp.concatenate(rows, axis=0)


def pick_place(per, hidden):
    half = per // 2
    rows = []
    for kind in range(KINDS):
        for p in range(per):
            column = (p // half * KINDS + kind) * hidden
            own = zero_one(iota((hidden, LANES), 1) == iota((hidden, LANES), 0) + column)
            before, after = p % half * LANES, (half - 1 - p % half) * LANES
            parts = [jnp.zeros((hidden, before), own.dtype)] * (before > 0) + [own]
            rows.append(jnp.concatenate(parts + [jnp.zeros((hidden, after), own.dtype)] * (after > 0), axis=1))
    return jnp.concatenate(rows, axis=0)


def load_kernel(*refs):
    count = len(refs) // 2
    sources, targets, sems = refs[:count], refs[count : 2 * count - 1], refs[-1]
    half = sources[0].shape[0]
    targets = [targets[0].at[pl.ds(0, half)], targets[0].at[pl.ds(half, half)], *targets[1:]]
    copies = [pltpu.make_async_copy(a, b, sems.at[k]) for k, (a, b) in enumerate(zip(sources, targets))]
    for copy in copies:
        copy.start()
    for copy in copies:
        copy.wait()


def cross(n, hidden, order, lefts, rights, first, store):
    wide = lefts.shape[1]
    same = iota((hidden, wide), 0) == iota((hidden, wide), 1) % hidden
    product = dot(rights, lefts, TN)
    for t in range(rights.shape[1] // hidden):
        own = jnp.where(same, product[t * hidden : (t + 1) * hidden], 0.0)
        store(pl.ds(row_of(order, n // len(order), first + t), 1), jnp.sum(own, axis=0, keepdims=True))


def side_by_side(ref, n):
    return jnp.concatenate([ref[pl.ds(g * n, n), :] for g in range(ref.shape[0] // n)], axis=1)


def head_kernel(n, hidden, order, *refs):
    *block_refs, count_ref, gain_ref, bias_ref, project_ref, gate_ref, out_weight_ref = refs[:-12]
    *stage_refs, project_wide_ref, out_wide_ref, pick_ref, own_ref = refs[-12:]
    per = LANES // hidden
    project_wide_ref[...] = wide_project(project_ref[...], per)
    out_wide_ref[...] = wide_out(out_weight_ref[...], per)
    pick_ref[...] = pick_place(per, hidden)
    weights = [ref[...] for ref in (gain_ref, bias_ref, project_wide_ref, out_wide_ref, gate_ref)]
    own = stage(n, hidden, order, 0, block_refs, count_ref[0], *weights, stage_refs)
    for r in range(own_ref.shape[0]):
        own_ref[r] = own[r]


def middle_kernel(n, hidden, order, first, *refs):
    left_head_ref, right_head_ref, *block_refs = refs[:-15]
    count_ref, gain_ref, bias_ref, project_wide_ref, out_wide_ref, gate_ref = refs[-15:-9]
    *stage_refs, x_ref = refs[-9:]
    weights = [ref[...] for ref in (gain_ref, bias_ref, project_wide_ref, out_wide_ref, gate_ref)]
    stage(n, hidden, order, first, block_refs, count_ref[0], *weights, stage_refs)
    left = jnp.concatenate([side_by_side(left_head_ref, n), side_by_side(stage_refs[0], n)], axis=1)
    right = jnp.concatenate([side_by_side(right_head_ref, n), side_by_side(stage_refs[1], n)], axis=1)
    x_ref[...] = jnp.zeros_like(x_ref)

    def store(row, value):
        x_ref[row, :] = value

    cross(n, hidden, order, left, right, 0, store)


def tail_kernel(n, hidden, order, cuts, *refs):
    blocks = len(order)
    block_refs, refs = refs[:blocks], refs[blocks:]
    head_refs, (project_wide_ref, out_wide_ref, pick_ref, own_ref), middle_refs = refs[:8], refs[8:12], refs[12:20]
    x_early_ref, *refs = refs[20:]
    count_ref, gain_ref, bias_ref, project_ref, gate_ref, out_gain_ref, out_bias_ref = refs[:7]
    update_ref, pair_ref, project_grad_ref, gate_grad_ref, out_grad_ref = refs[7:12]
    tail_refs, (square_ref, dgo_ref, dp_ref, x_ref, x_late_ref, dx_ref) = refs[12:20], refs[20:]
    stages = (head_refs, middle_refs, tail_refs)
    f32, bf16 = jnp.float32, jnp.bfloat16
    per = LANES // hidden
    groups = n // per
    wide = n * hidden
    rows = n // blocks
    gain, gate_weight, project_t = gain_ref[...], gate_ref[...], project_ref[...]
    weights = gain, bias_ref[...], project_wide_ref[...], out_wide_ref[...], gate_weight
    stage(n, hidden, order, cuts[1], block_refs[cuts[1] * per // rows :], count_ref[0], *weights, tail_refs)

    spans = [(low * n, high * n) for low, high in zip((0, *cuts), (*cuts, groups))]
    half = per // 2

    def put(ref, q, column, value):
        for low, high in spans:
            ref[pl.ds(low * half + q * (high - low), high - low), pl.ds(column, LANES)] = value[low:high]

    def sum_pairs(ref):
        znt = [refs[7][...].reshape(2 * LANES, half * (high - low)) for refs, (low, high) in zip(stages, spans)]
        rows_of = [ref[pl.ds(low * half, (high - low) * half), :] for low, high in spans]
        return sum(dot(a, b) for a, b in zip(znt, rows_of))

    def all_rows(k):
        return jnp.concatenate([refs[k][...] for refs in stages], axis=0)


    def lanes(flat):
        return jnp.concatenate([flat[g * n : (g + 1) * n] for g in range(groups)], axis=1)

    def flatten(rowed):
        return jnp.concatenate([rowed[:, g * LANES : (g + 1) * LANES] for g in range(groups)], axis=0)

    left, right = lanes(all_rows(0)), lanes(all_rows(1))

    split = cuts[1] * LANES
    x_ref[...] = jnp.zeros_like(x_ref)

    def store_late(row, value):
        x_late_ref[row, :] = value

    def store_both(row, value):
        x_ref[row, :] = value[:, :split]
        x_late_ref[row, :] = value[:, split:]

    cross(n, hidden, order, left[:, split:], right[:, :split], 0, store_late)
    cross(n, hidden, order, left, right[:, split:], split // hidden, store_both)
    x = jnp.concatenate([x_early_ref[...] + x_ref[...], x_late_ref[...]], axis=1)
    x = flatten(x.astype(bf16).astype(f32))

    mean = jnp.where(iota((LANES, LANES), 0) // hidden == iota((LANES, LANES), 1) // hidden, 1.0 / hidden, 0.0)
    mean = mean.astype(bf16)
    mean_twice = jnp.concatenate([mean, mean], axis=0)
    out_gain = jnp.concatenate([out_gain_ref[...]] * per, axis=1)
    out_bias = jnp.concatenate([out_bias_ref[...]] * per, axis=1)
    centered = x - dot(x.astype(bf16), mean)
    xs = lax.rsqrt(dot_split(centered * centered, mean_twice) + 1e-05)
    xhat = centered * xs
    xn = (xhat * out_gain + out_bias).astype(bf16)

    u = out_gain * all_rows(6)
    dx = xs * (u - dot_split(u, mean_twice) - xhat * dot_split(u * xhat, mean_twice))
    dx_ref[...] = lanes(dx.astype(bf16)).astype(f32)

    same = iota((hidden, wide), 0) == iota((hidden, wide), 1) % hidden
    for t in range(n):
        row = dx_ref[pl.ds(row_of(order, rows, t), 1), :]
        row = jnp.broadcast_to(row, (hidden, wide)).astype(bf16)
        square_ref[pl.ds(t * hidden, hidden), :] = jnp.where(same, row, jnp.zeros_like(row))
    y_all = dot(xn, out_wide_ref[...])
    own_dgo = []
    for p in range(per):
        y = y_all[:, p * LANES : (p + 1) * LANES]
        dgo = (jnp.concatenate([refs[5][p] for refs in stages], axis=0) * y).astype(bf16)
        put(dgo_ref, p % half, p // half * LANES, dgo)
        if p < rows:
            update_ref[p] = (own_ref[p] * y[:n]).astype(bf16)
            own_dgo.append(dgo[:n])
    diagonal = square_ref[...]
    dleft = flatten(dot(right, diagonal).astype(bf16)).astype(f32)
    dright = flatten(dot(left, diagonal, NT).astype(bf16)).astype(f32)
    xnt, dy = xn.T, all_rows(4)
    out_grad = [dot(xnt[p * hidden : (p + 1) * hidden], dy[:, p * LANES : (p + 1) * LANES]) for p in range(per)]
    out_grad_ref[...] = sum(out_grad) / n
    gate_grad = sum_pairs(dgo_ref)
    gate_grad_ref[...] = (gate_grad[:LANES, :LANES] + gate_grad[LANES:, LANES:]) / n

    dp = []
    for side, grad in enumerate((dleft, dright)):
        masked = grad * jnp.concatenate([refs[2][side] for refs in stages], axis=0)
        dp += [masked, masked * jnp.concatenate([refs[3][side] for refs in stages], axis=0)]
    dp = jnp.concatenate([d.astype(bf16) for d in dp], axis=1)
    by_place = dot(dp, pick_ref[...]).astype(bf16)
    for q in range(half):
        put(dp_ref, q, 0, by_place[:, q * LANES : (q + 1) * LANES])
    project_grad = sum_pairs(dp_ref).T
    width = KINDS * hidden
    project_grad_ref[...] = (project_grad[:width, :LANES] + project_grad[width:, LANES:]) / n

    tiled = [project_t[kind * hidden : (kind + 1) * hidden] for kind in range(KINDS) for _ in range(per)]
    place = iota((n, KINDS * LANES), 1) % LANES // hidden
    dp_rows = [jnp.where(place == r, dp[:n], jnp.zeros_like(dp[:n])) for r in range(rows)]
    dzn = dot(jnp.concatenate(dp_rows, axis=0), jnp.concatenate(tiled, axis=0))
    dzn += dot(jnp.concatenate(own_dgo, axis=0), gate_weight, NT)
    zhat, zs = normalize(block_refs[0][pl.ds(0, rows * n), :].astype(f32))
    u = gain * dzn
    first = jnp.mean(u, axis=-1, keepdims=True)
    second = jnp.mean(u * zhat, axis=-1, keepdims=True)
    pair_grad = zs * (u - first - zhat * second)
    for r in range(rows):
        pair_ref[r] = pair_grad[r * n : (r + 1) * n]


def body_whole(
    devices,
    pair_acts,
    token_count,
    input_gain,
    input_bias,
    project_weight,
    gate_weight,
    output_norm_gain,
    output_shift_bias,
    output_weight,
    update_grad,
):
    rows, n, channels = pair_acts.shape
    hidden = output_weight.shape[0]
    f32, bf16 = jnp.float32, jnp.bfloat16
    half = rows * n
    vmem, anywhere = pl.BlockSpec(memory_space=pltpu.VMEM), pl.BlockSpec(memory_space=pl.ANY)
    shape = jax.ShapeDtypeStruct
    sources = [
        pair_acts.reshape(half, channels),
        update_grad.reshape(half, channels),
        input_gain[None],
        input_bias[None],
        project_weight.T,
        gate_weight,
        output_norm_gain[None],
        output_shift_bias[None],
        output_weight,
    ]
    send, gain, bias, project_t, gate_weight, out_gain, out_bias, out_weight = pl.pallas_call(
        load_kernel,
        out_shape=[pltpu.VMEM((2 * half, channels), bf16)] + [pltpu.VMEM(v.shape, v.dtype) for v in sources[2:]],
        in_specs=[anywhere] * len(sources),
        out_specs=[vmem] * (len(sources) - 1),
        scratch_shapes=[pltpu.SemaphoreType.DMA((len(sources),))],
        name="load",
    )(*sources)
    blocks = {0: send}
    core, x, *z = [1 << bit for bit in range(devices.bit_length() - 1)]

    def hop(step, sources):
        pairs = [(i, i ^ step) for i in range(devices)]
        for d in sources:
            blocks[d ^ step] = lax.ppermute(blocks[d], "row", pairs)

    for step in reversed(z):
        hop(step, [0])
        if step == z[-1]:
            hop(x, [0])
    for k, step in enumerate(z[:-1]):
        hop(step, [x])
        hop(step, [d for d in list(blocks) if 0 < d and d % (2 * step) == 0])
    hop(x, [d for d in list(blocks) if not d & x and d ^ x not in blocks])
    hop(core, [d for d in list(blocks) if d not in [14]])
    order = sorted(range(devices), key=lambda d: (2 * d.bit_count() + (d & x) / x, -(d & core), -d))
    blocks[15] = None
    ordered = [blocks[d] for d in order]
    per = LANES // hidden
    groups = n // per
    cuts = (groups // 2, groups - 1)

    def stage_out(count):
        tall = count * n
        return (
            pltpu.VMEM((tall, LANES), bf16),
            pltpu.VMEM((tall, LANES), bf16),
            pltpu.VMEM((2, tall, LANES), f32),
            pltpu.VMEM((2, tall, LANES), f32),
            pltpu.VMEM((tall, per * channels), bf16),
            pltpu.VMEM((per, tall, channels), f32),
            pltpu.VMEM((tall, LANES), f32),
            pltpu.VMEM((2, channels, per // 2 * tall), bf16),
        )

    def span(first, last):
        return ordered[first * per // rows : -(-last * per // rows)]

    head_in = [*span(0, cuts[0]), token_count, gain, bias, project_t, gate_weight, out_weight]
    smem = pl.BlockSpec(memory_space=pltpu.SMEM)
    head_out = (
        *stage_out(cuts[0]),
        pltpu.VMEM((KINDS * LANES, per * channels), bf16),
        pltpu.VMEM((LANES, per * channels), bf16),
        pltpu.VMEM((KINDS * LANES, per // 2 * LANES), bf16),
        pltpu.VMEM((rows, n, channels), f32),
    )
    head = pl.pallas_call(
        functools.partial(head_kernel, n, hidden, order),
        out_shape=head_out,
        in_specs=[vmem] * (len(head_in) - 6) + [smem] + [vmem] * 5,
        out_specs=(vmem,) * len(head_out),
        compiler_params=pltpu.CompilerParams(vmem_limit_bytes=16 << 20),
        name="head",
    )(*head_in)
    held = [blocks[d] for d in [14]]
    held, head = lax.optimization_barrier((held, head))
    for d, block in zip([14], held):
        blocks[d] = block
    hop(core, [14])
    ordered = [blocks[d] for d in order]
    middle_in = [head[0], head[1], *span(*cuts), token_count, gain, bias, head[8], head[9], gate_weight]
    middle_out = (*stage_out(cuts[1] - cuts[0]), pltpu.VMEM((n, cuts[1] * LANES), f32))
    middle = pl.pallas_call(
        functools.partial(middle_kernel, n, hidden, order, cuts[0]),
        out_shape=middle_out,
        in_specs=[vmem] * (len(middle_in) - 6) + [smem] + [vmem] * 5,
        out_specs=(vmem,) * len(middle_out),
        compiler_params=pltpu.CompilerParams(vmem_limit_bytes=16 << 20),
        name="middle",
    )(*middle_in)
    tall = groups * n
    update, pair_grad, project_grad, gate_grad, output_grad = pl.pallas_call(
        functools.partial(tail_kernel, n, hidden, order, cuts),
        out_shape=(
            shape((rows, n, channels), bf16),
            shape((rows, n, channels), f32),
            shape((KINDS * hidden, channels), f32),
            shape((channels, channels), f32),
            shape((hidden, channels), f32),
        ),
        in_specs=[vmem] * (devices + len(head) + len(middle)) + [smem] + [vmem] * 6,
        out_specs=(vmem,) * 5,
        scratch_shapes=[
            *stage_out(groups - cuts[1]),
            pltpu.VMEM((n * hidden, n * hidden), bf16),
            pltpu.VMEM((per // 2 * tall, 2 * channels), bf16),
            pltpu.VMEM((per // 2 * tall, LANES), bf16),
            pltpu.VMEM((n, cuts[1] * LANES), f32),
            pltpu.VMEM((n, (groups - cuts[1]) * LANES), f32),
            pltpu.VMEM((n, n * hidden), f32),
        ],
        compiler_params=pltpu.CompilerParams(vmem_limit_bytes=32 << 20),
        name="tail",
    )(*ordered, *head, *middle, token_count, gain, bias, project_t, gate_weight, out_gain, out_bias)
    return update, pair_grad, project_grad.T, gate_grad, output_grad


def layer_normalize(values, norm_gain, norm_bias, reduce_axis):
    average = jnp.mean(values, axis=reduce_axis, keepdims=True)
    centered = values - average
    variance = jnp.mean(centered * centered, axis=reduce_axis, keepdims=True)
    inv_std = lax.rsqrt(variance + 1e-05)
    normed = centered * inv_std
    return (normed * norm_gain + norm_bias, normed, inv_std)


def norm_backward_pass(upstream, normed, inv_std, norm_gain, reduce_axis):
    scaled = upstream * norm_gain
    first = jnp.mean(scaled, axis=reduce_axis, keepdims=True)
    second = jnp.mean(scaled * normed, axis=reduce_axis, keepdims=True)
    return inv_std * (scaled - first - normed * second)


def body(
    pair_acts,
    token_count,
    input_gain,
    input_bias,
    project_weight,
    gate_weight,
    output_norm_gain,
    output_shift_bias,
    output_weight,
    update_grad,
):
    single_float_format = jnp.float32
    brain_float_sixteen = jnp.bfloat16
    row_count, length, channels = pair_acts.shape
    hidden = output_weight.shape[0]
    row_start = lax.axis_index("row") * row_count
    live_limit = token_count[0]
    row_live = (row_start + jnp.arange(row_count, dtype=jnp.int32) < live_limit).astype(
        single_float_format
    )
    col_live = (jnp.arange(length, dtype=jnp.int32) < live_limit).astype(single_float_format)
    live_mask = row_live[:, None] * col_live[None, :]
    zn32, zhat, zscale = layer_normalize(
        pair_acts.astype(single_float_format), input_gain, input_bias, -1
    )
    normed_pair = zn32.astype(brain_float_sixteen)
    projected = jnp.einsum(
        "rkd,de->erk", normed_pair, project_weight, preferred_element_type=single_float_format
    ).reshape(4, hidden, row_count, length)
    gate_left = jax.nn.sigmoid(projected[1])
    gate_right = jax.nn.sigmoid(projected[3])
    left_panel = (live_mask * gate_left * projected[0]).astype(brain_float_sixteen)
    right_panel = (live_mask * gate_right * projected[2]).astype(brain_float_sixteen)
    stacked = jnp.stack([left_panel, right_panel], axis=1)
    columns = lax.all_to_all(stacked, "row", split_axis=0, concat_axis=2, tiled=True)
    left_cols = columns[:, 0]
    right_cols = columns[:, 1]
    products = jnp.einsum(
        "cik,cjk->cij", left_cols, right_cols, preferred_element_type=single_float_format
    ).astype(brain_float_sixteen)
    triangle_product = lax.all_to_all(products, "row", split_axis=1, concat_axis=0, tiled=True)
    normed_input_single, standardized_input, input_inverse_scale = layer_normalize(
        triangle_product.astype(single_float_format),
        output_norm_gain[:, None, None],
        output_shift_bias[:, None, None],
        0,
    )
    normed_tri = normed_input_single.astype(brain_float_sixteen)
    mixed = jnp.einsum(
        "crk,cd->rkd", normed_tri, output_weight, preferred_element_type=single_float_format
    )
    gate_out = jax.nn.sigmoid(
        jnp.einsum(
            "rkd,de->rke", normed_pair, gate_weight, preferred_element_type=single_float_format
        )
    )
    update = (gate_out * mixed).astype(brain_float_sixteen)
    cotangent = update_grad.astype(single_float_format)
    mixed_grad = (cotangent * gate_out).astype(brain_float_sixteen)
    gate_logit_grad = (cotangent * mixed * gate_out * (1.0 - gate_out)).astype(brain_float_sixteen)
    output_terms = jnp.einsum(
        "crk,rkd->cd", normed_tri, mixed_grad, preferred_element_type=single_float_format
    )
    triangle_normed_gradient = jnp.einsum(
        "rkd,cd->crk", mixed_grad, output_weight, preferred_element_type=single_float_format
    )
    triangle_gradient = norm_backward_pass(
        triangle_normed_gradient,
        standardized_input,
        input_inverse_scale,
        output_norm_gain[:, None, None],
        0,
    ).astype(brain_float_sixteen)
    grad_cols = lax.all_to_all(triangle_gradient, "row", split_axis=0, concat_axis=1, tiled=True)
    left_col_grad = jnp.einsum(
        "cij,cjk->cik", grad_cols, right_cols, preferred_element_type=single_float_format
    ).astype(brain_float_sixteen)
    right_col_grad = jnp.einsum(
        "cij,cik->cjk", grad_cols, left_cols, preferred_element_type=single_float_format
    ).astype(brain_float_sixteen)
    returned = lax.all_to_all(
        jnp.stack([left_col_grad, right_col_grad], axis=1),
        "row",
        split_axis=2,
        concat_axis=0,
        tiled=True,
    )
    left_grad = returned[:, 0].astype(single_float_format)
    right_grad = returned[:, 1].astype(single_float_format)
    project_terms = jnp.stack(
        [
            left_grad * live_mask * gate_left,
            left_grad * live_mask * projected[0] * gate_left * (1.0 - gate_left),
            right_grad * live_mask * gate_right,
            right_grad * live_mask * projected[2] * gate_right * (1.0 - gate_right),
        ]
    )
    project_terms = project_terms.astype(brain_float_sixteen).reshape(4 * hidden, row_count, length)
    project_part = jnp.einsum(
        "rkd,erk->de", normed_pair, project_terms, preferred_element_type=single_float_format
    )
    gate_part = jnp.einsum(
        "rkd,rke->de", normed_pair, gate_logit_grad, preferred_element_type=single_float_format
    )
    totals = lax.psum((project_part, gate_part, output_terms), "row")
    project_grad = totals[0] / length
    gate_grad = totals[1] / length
    output_grad = totals[2] / length
    normed_grad = jnp.einsum(
        "erk,de->rkd", project_terms, project_weight, preferred_element_type=single_float_format
    ) + jnp.einsum(
        "rke,de->rkd", gate_logit_grad, gate_weight, preferred_element_type=single_float_format
    )
    pair_grad = norm_backward_pass(normed_grad, zhat, zscale, input_gain, -1)
    return (update, pair_grad, project_grad, gate_grad, output_grad)


def fits_whole(mesh, args):
    pair_acts, output_weight = args[0], args[8]
    devices = mesh.shape["row"]
    length, channels = pair_acts.shape[0] // mesh.shape["grp"], pair_acts.shape[2]
    hidden = output_weight.shape[0]
    return (
        channels == LANES
        and hidden % 16 == 0
        and LANES % hidden == 0
        and length % (LANES // hidden) == 0
        and (LANES // hidden) % 8 == 0
        and length % 16 == 0
        and devices & (devices - 1) == 0
        and length % devices == 0
        and length // devices <= LANES // hidden
        and devices >= 4
        and length // 2 % (LANES // hidden) == 0
        and 2 * pair_acts.dtype.itemsize * length * length * channels <= WHOLE_BYTES
    )


def solution(mesh):
    in_specs = (
        P(("grp", "row"), None, None),
        P("grp"),
        P(),
        P(),
        P(),
        P(),
        P(),
        P(),
        P(),
        P(("grp", "row"), None, None),
    )
    out_specs = (
        P(("grp", "row"), None, None),
        P(("grp", "row"), None, None),
        P("grp", None),
        P("grp", None),
        P("grp", None),
    )
    devices = mesh.shape["row"]

    def run(*args):
        crop = functools.partial(body_whole, devices) if fits_whole(mesh, args) else body
        return jax.shard_map(crop, mesh=mesh, in_specs=in_specs, out_specs=out_specs, check_vma=False)(*args)

    return run
```

```python
import functools

import jax
import jax.numpy as jnp
from jax import lax
from jax.experimental import pallas as pl
from jax.experimental.pallas import tpu as pltpu
from jax.sharding import PartitionSpec as P

LANES = 128
KINDS = 4
WHOLE_BYTES = 4 << 20

NN = (((1,), (0,)), ((), ()))
NT = (((1,), (1,)), ((), ()))
TN = (((0,), (0,)), ((), ()))


def dot(a, b, dims=NN):
    return lax.dot_general(a, b, dims, preferred_element_type=jnp.float32)


def dot_split(a, b_twice):
    high = a.astype(jnp.bfloat16)
    low = (a - high.astype(jnp.float32)).astype(jnp.bfloat16)
    return dot(jnp.concatenate([high, low], axis=1), b_twice)


def iota(shape, dim):
    return lax.broadcasted_iota(jnp.int32, shape, dim)


def zero_one(condition):
    return jnp.where(condition, 1.0, 0.0).astype(jnp.bfloat16)


def sigmoid(v):
    return 1.0 / (1.0 + jnp.exp(-v))


def normalize(v):
    centered = v - jnp.mean(v, axis=-1, keepdims=True)
    s = lax.rsqrt(jnp.mean(centered * centered, axis=-1, keepdims=True) + 1e-05)
    return centered * s, s


def row_of(order, rows, t):
    return (lax.axis_index("row") ^ order[t // rows]) * rows + t % rows


def rows_of_lanes(order, rows, hidden, group):
    per = LANES // hidden
    place = iota((1, LANES), 1) // hidden
    at = jnp.full((1, LANES), row_of(order, rows, group * per), jnp.int32)
    for p in range(1, per):
        at = jnp.where(place == p, row_of(order, rows, group * per + p), at)
    return at


def stage(n, hidden, order, first, block_refs, count, gain, bias, project_wide, out_wide, gate_weight, refs):
    left_ref, right_ref, mask_ref, slope_ref, dy_ref, dgo_part_ref, dxn_ref, znt_ref = refs
    f32, bf16 = jnp.float32, jnp.bfloat16
    per = LANES // hidden
    rows = n // len(order)
    tall = left_ref.shape[0]
    start = first * per
    zn, cotangent = {}, {}
    for t in range(start, start + per * (tall // n)):
        block, at = block_refs[t // rows - start // rows], t % rows * n
        zn[t] = (normalize(block[pl.ds(at, n), :].astype(f32))[0] * gain + bias).astype(bf16)
        cotangent[t] = block[pl.ds((rows + t % rows) * n, n), :]

    def place(tiles, p):
        return jnp.concatenate([tiles[t] for t in range(start + p, start + per * (tall // n), per)], axis=0)

    zn = [place(zn, p) for p in range(per)]
    projected = dot(jnp.concatenate(zn, axis=1), project_wide, NT)
    live_k = iota((n, LANES), 0) < count
    mask = [
        jnp.where(live_k & (rows_of_lanes(order, rows, hidden, first + g) < count), 1.0, 0.0) for g in range(tall // n)
    ]
    mask = jnp.concatenate(mask, axis=0)
    for side, ref in enumerate((left_ref, right_ref)):
        value = projected[:, 2 * side * LANES : (2 * side + 1) * LANES]
        gate = sigmoid(projected[:, (2 * side + 1) * LANES : (2 * side + 2) * LANES])
        ref[...] = (mask * gate * value).astype(bf16)
        mask_ref[side] = mask * gate
        slope_ref[side] = value * (1.0 - gate)
    own = []
    zn_tall = jnp.concatenate(zn, axis=0)
    gates = sigmoid(dot(zn_tall, gate_weight))
    for p in range(per):
        go = gates[p * tall : (p + 1) * tall]
        dy = place(cotangent, p).astype(f32) * go
        dy_ref[:, p * LANES : (p + 1) * LANES] = dy.astype(bf16)
        dgo_part_ref[p] = dy * (1.0 - go)
        own.append(go[:n])
    dxn_ref[...] = dot(dy_ref[...], out_wide, NT)
    half = per // 2 * tall
    znt_ref[0] = zn_tall[:half].T
    znt_ref[1] = zn_tall[half:].T
    return own


def wide_project(project_t, per):
    hidden, channels = project_t.shape[0] // KINDS, project_t.shape[1]
    columns = []
    for p in range(per):
        parts = []
        for kind in range(KINDS):
            before, after = p * hidden, (per - 1 - p) * hidden
            parts += [jnp.zeros((before, channels), project_t.dtype)] * (before > 0)
            parts += [project_t[kind * hidden : (kind + 1) * hidden]]
            parts += [jnp.zeros((after, channels), project_t.dtype)] * (after > 0)
        columns.append(jnp.concatenate(parts, axis=0))
    return jnp.concatenate(columns, axis=1)


def wide_out(out_weight, per):
    hidden, channels = out_weight.shape
    rows = []
    for p in range(per):
        before, after = p * channels, (per - 1 - p) * channels
        parts = [jnp.zeros((hidden, before), out_weight.dtype)] * (before > 0) + [out_weight]
        rows.append(jnp.concatenate(parts + [jnp.zeros((hidden, after), out_weight.dtype)] * (after > 0), axis=1))
    return jnp.concatenate(rows, axis=0)


def pick_place(per, hidden):
    half = per // 2
    rows = []
    for kind in range(KINDS):
        for p in range(per):
            column = (p // half * KINDS + kind) * hidden
            own = zero_one(iota((hidden, LANES), 1) == iota((hidden, LANES), 0) + column)
            before, after = p % half * LANES, (half - 1 - p % half) * LANES
            parts = [jnp.zeros((hidden, before), own.dtype)] * (before > 0) + [own]
            rows.append(jnp.concatenate(parts + [jnp.zeros((hidden, after), own.dtype)] * (after > 0), axis=1))
    return jnp.concatenate(rows, axis=0)


def load_kernel(*refs):
    count = len(refs) // 2
    sources, targets, sems = refs[:count], refs[count : 2 * count - 1], refs[-1]
    half = sources[0].shape[0]
    targets = [targets[0].at[pl.ds(0, half)], targets[0].at[pl.ds(half, half)], *targets[1:]]
    copies = [pltpu.make_async_copy(a, b, sems.at[k]) for k, (a, b) in enumerate(zip(sources, targets))]
    for copy in copies:
        copy.start()
    for copy in copies:
        copy.wait()


def cross(n, hidden, order, lefts, rights, first, store):
    wide = lefts.shape[1]
    same = iota((hidden, wide), 0) == iota((hidden, wide), 1) % hidden
    product = dot(rights, lefts, TN)
    for t in range(rights.shape[1] // hidden):
        own = jnp.where(same, product[t * hidden : (t + 1) * hidden], 0.0)
        store(pl.ds(row_of(order, n // len(order), first + t), 1), jnp.sum(own, axis=0, keepdims=True))


def side_by_side(ref, n):
    return jnp.concatenate([ref[pl.ds(g * n, n), :] for g in range(ref.shape[0] // n)], axis=1)


def head_kernel(n, hidden, order, *refs):
    *block_refs, count_ref, gain_ref, bias_ref, project_ref, gate_ref, out_weight_ref = refs[:-12]
    *stage_refs, project_wide_ref, out_wide_ref, pick_ref, own_ref = refs[-12:]
    per = LANES // hidden
    project_wide_ref[...] = wide_project(project_ref[...], per)
    out_wide_ref[...] = wide_out(out_weight_ref[...], per)
    pick_ref[...] = pick_place(per, hidden)
    weights = [ref[...] for ref in (gain_ref, bias_ref, project_wide_ref, out_wide_ref, gate_ref)]
    own = stage(n, hidden, order, 0, block_refs, count_ref[0], *weights, stage_refs)
    for r in range(own_ref.shape[0]):
        own_ref[r] = own[r]


def middle_kernel(n, hidden, order, first, *refs):
    left_head_ref, right_head_ref, *block_refs = refs[:-15]
    count_ref, gain_ref, bias_ref, project_wide_ref, out_wide_ref, gate_ref = refs[-15:-9]
    *stage_refs, x_ref = refs[-9:]
    weights = [ref[...] for ref in (gain_ref, bias_ref, project_wide_ref, out_wide_ref, gate_ref)]
    stage(n, hidden, order, first, block_refs, count_ref[0], *weights, stage_refs)
    left = jnp.concatenate([side_by_side(left_head_ref, n), side_by_side(stage_refs[0], n)], axis=1)
    right = jnp.concatenate([side_by_side(right_head_ref, n), side_by_side(stage_refs[1], n)], axis=1)
    x_ref[...] = jnp.zeros_like(x_ref)

    def store(row, value):
        x_ref[row, :] = value

    cross(n, hidden, order, left, right, 0, store)


def tail_kernel(n, hidden, order, cuts, *refs):
    blocks = len(order)
    block_refs, refs = refs[:blocks], refs[blocks:]
    head_refs, (project_wide_ref, out_wide_ref, pick_ref, own_ref), middle_refs = refs[:8], refs[8:12], refs[12:20]
    x_early_ref, *refs = refs[20:]
    count_ref, gain_ref, bias_ref, project_ref, gate_ref, out_gain_ref, out_bias_ref = refs[:7]
    update_ref, pair_ref, project_grad_ref, gate_grad_ref, out_grad_ref = refs[7:12]
    tail_refs, (square_ref, dgo_ref, dp_ref, x_ref, x_late_ref, dx_ref) = refs[12:20], refs[20:]
    stages = (head_refs, middle_refs, tail_refs)
    f32, bf16 = jnp.float32, jnp.bfloat16
    per = LANES // hidden
    groups = n // per
    wide = n * hidden
    rows = n // blocks
    gain, gate_weight, project_t = gain_ref[...], gate_ref[...], project_ref[...]
    weights = gain, bias_ref[...], project_wide_ref[...], out_wide_ref[...], gate_weight
    stage(n, hidden, order, cuts[1], block_refs[cuts[1] * per // rows :], count_ref[0], *weights, tail_refs)

    spans = [(low * n, high * n) for low, high in zip((0, *cuts), (*cuts, groups))]
    half = per // 2

    def put(ref, q, column, value):
        for low, high in spans:
            ref[pl.ds(low * half + q * (high - low), high - low), pl.ds(column, LANES)] = value[low:high]

    def sum_pairs(ref):
        znt = [refs[7][...].reshape(2 * LANES, half * (high - low)) for refs, (low, high) in zip(stages, spans)]
        rows_of = [ref[pl.ds(low * half, (high - low) * half), :] for low, high in spans]
        return sum(dot(a, b) for a, b in zip(znt, rows_of))

    def all_rows(k):
        return jnp.concatenate([refs[k][...] for refs in stages], axis=0)


    def lanes(flat):
        return jnp.concatenate([flat[g * n : (g + 1) * n] for g in range(groups)], axis=1)

    def flatten(rowed):
        return jnp.concatenate([rowed[:, g * LANES : (g + 1) * LANES] for g in range(groups)], axis=0)

    left, right = lanes(all_rows(0)), lanes(all_rows(1))

    split = cuts[1] * LANES
    x_ref[...] = jnp.zeros_like(x_ref)

    def store_late(row, value):
        x_late_ref[row, :] = value

    def store_both(row, value):
        x_ref[row, :] = value[:, :split]
        x_late_ref[row, :] = value[:, split:]

    cross(n, hidden, order, left[:, split:], right[:, :split], 0, store_late)
    cross(n, hidden, order, left, right[:, split:], split // hidden, store_both)
    x = jnp.concatenate([x_early_ref[...] + x_ref[...], x_late_ref[...]], axis=1)
    x = flatten(x.astype(bf16).astype(f32))

    mean = jnp.where(iota((LANES, LANES), 0) // hidden == iota((LANES, LANES), 1) // hidden, 1.0 / hidden, 0.0)
    mean = mean.astype(bf16)
    mean_twice = jnp.concatenate([mean, mean], axis=0)
    out_gain = jnp.concatenate([out_gain_ref[...]] * per, axis=1)
    out_bias = jnp.concatenate([out_bias_ref[...]] * per, axis=1)
    centered = x - dot(x.astype(bf16), mean)
    xs = lax.rsqrt(dot_split(centered * centered, mean_twice) + 1e-05)
    xhat = centered * xs
    xn = (xhat * out_gain + out_bias).astype(bf16)

    u = out_gain * all_rows(6)
    dx = xs * (u - dot_split(u, mean_twice) - xhat * dot_split(u * xhat, mean_twice))
    dx_ref[...] = lanes(dx.astype(bf16)).astype(f32)

    same = iota((hidden, wide), 0) == iota((hidden, wide), 1) % hidden
    for t in range(n):
        row = dx_ref[pl.ds(row_of(order, rows, t), 1), :]
        row = jnp.broadcast_to(row, (hidden, wide)).astype(bf16)
        square_ref[pl.ds(t * hidden, hidden), :] = jnp.where(same, row, jnp.zeros_like(row))
    y_all = dot(xn, out_wide_ref[...])
    own_dgo = []
    for p in range(per):
        y = y_all[:, p * LANES : (p + 1) * LANES]
        dgo = (jnp.concatenate([refs[5][p] for refs in stages], axis=0) * y).astype(bf16)
        put(dgo_ref, p % half, p // half * LANES, dgo)
        if p < rows:
            update_ref[p] = (own_ref[p] * y[:n]).astype(bf16)
            own_dgo.append(dgo[:n])
    diagonal = square_ref[...]
    dleft = flatten(dot(right, diagonal).astype(bf16)).astype(f32)
    dright = flatten(dot(left, diagonal, NT).astype(bf16)).astype(f32)
    xnt, dy = xn.T, all_rows(4)
    out_grad = [dot(xnt[p * hidden : (p + 1) * hidden], dy[:, p * LANES : (p + 1) * LANES]) for p in range(per)]
    out_grad_ref[...] = sum(out_grad) / n
    gate_grad = sum_pairs(dgo_ref)
    gate_grad_ref[...] = (gate_grad[:LANES, :LANES] + gate_grad[LANES:, LANES:]) / n

    dp = []
    for side, grad in enumerate((dleft, dright)):
        masked = grad * jnp.concatenate([refs[2][side] for refs in stages], axis=0)
        dp += [masked, masked * jnp.concatenate([refs[3][side] for refs in stages], axis=0)]
    dp = jnp.concatenate([d.astype(bf16) for d in dp], axis=1)
    by_place = dot(dp, pick_ref[...]).astype(bf16)
    for q in range(half):
        put(dp_ref, q, 0, by_place[:, q * LANES : (q + 1) * LANES])
    project_grad = sum_pairs(dp_ref).T
    width = KINDS * hidden
    project_grad_ref[...] = (project_grad[:width, :LANES] + project_grad[width:, LANES:]) / n

    tiled = [project_t[kind * hidden : (kind + 1) * hidden] for kind in range(KINDS) for _ in range(per)]
    place = iota((n, KINDS * LANES), 1) % LANES // hidden
    dp_rows = [jnp.where(place == r, dp[:n], jnp.zeros_like(dp[:n])) for r in range(rows)]
    dzn = dot(jnp.concatenate(dp_rows, axis=0), jnp.concatenate(tiled, axis=0))
    dzn += dot(jnp.concatenate(own_dgo, axis=0), gate_weight, NT)
    zhat, zs = normalize(block_refs[0][pl.ds(0, rows * n), :].astype(f32))
    u = gain * dzn
    first = jnp.mean(u, axis=-1, keepdims=True)
    second = jnp.mean(u * zhat, axis=-1, keepdims=True)
    pair_grad = zs * (u - first - zhat * second)
    for r in range(rows):
        pair_ref[r] = pair_grad[r * n : (r + 1) * n]


def body_whole(
    devices,
    pair_acts,
    token_count,
    input_gain,
    input_bias,
    project_weight,
    gate_weight,
    output_norm_gain,
    output_shift_bias,
    output_weight,
    update_grad,
):
    rows, n, channels = pair_acts.shape
    hidden = output_weight.shape[0]
    f32, bf16 = jnp.float32, jnp.bfloat16
    half = rows * n
    vmem, anywhere = pl.BlockSpec(memory_space=pltpu.VMEM), pl.BlockSpec(memory_space=pl.ANY)
    shape = jax.ShapeDtypeStruct
    sources = [
        pair_acts.reshape(half, channels),
        update_grad.reshape(half, channels),
        input_gain[None],
        input_bias[None],
        project_weight.T,
        gate_weight,
        output_norm_gain[None],
        output_shift_bias[None],
        output_weight,
    ]
    send, gain, bias, project_t, gate_weight, out_gain, out_bias, out_weight = pl.pallas_call(
        load_kernel,
        out_shape=[pltpu.VMEM((2 * half, channels), bf16)] + [pltpu.VMEM(v.shape, v.dtype) for v in sources[2:]],
        in_specs=[anywhere] * len(sources),
        out_specs=[vmem] * (len(sources) - 1),
        scratch_shapes=[pltpu.SemaphoreType.DMA((len(sources),))],
        name="load",
    )(*sources)
    blocks = {0: send}
    core, x, *z = [1 << bit for bit in range(devices.bit_length() - 1)]

    def hop(step, sources):
        pairs = [(i, i ^ step) for i in range(devices)]
        for d in sources:
            blocks[d ^ step] = lax.ppermute(blocks[d], "row", pairs)

    for step in reversed(z):
        hop(step, [0])
        if step == z[-1]:
            hop(x, [0])
    for k, step in enumerate(z[:-1]):
        hop(step, [x])
        hop(step, [d for d in list(blocks) if 0 < d and d % (2 * step) == 0])
    hop(x, [d for d in list(blocks) if not d & x and d ^ x not in blocks])
    last = devices - 1 - core
    hop(core, [d for d in list(blocks) if d != last])
    order = sorted(range(devices), key=lambda d: (2 * d.bit_count() + (d & x) / x, -(d & core), -d))
    ordered = [blocks.get(d) for d in order]
    per = LANES // hidden
    groups = n // per
    cuts = (groups // 2, groups - 1)

    def stage_out(count):
        tall = count * n
        return (
            pltpu.VMEM((tall, LANES), bf16),
            pltpu.VMEM((tall, LANES), bf16),
            pltpu.VMEM((2, tall, LANES), f32),
            pltpu.VMEM((2, tall, LANES), f32),
            pltpu.VMEM((tall, per * channels), bf16),
            pltpu.VMEM((per, tall, channels), f32),
            pltpu.VMEM((tall, LANES), f32),
            pltpu.VMEM((2, channels, per // 2 * tall), bf16),
        )

    def span(first, last):
        return ordered[first * per // rows : -(-last * per // rows)]

    head_in = [*span(0, cuts[0]), token_count, gain, bias, project_t, gate_weight, out_weight]
    smem = pl.BlockSpec(memory_space=pltpu.SMEM)
    head_out = (
        *stage_out(cuts[0]),
        pltpu.VMEM((KINDS * LANES, per * channels), bf16),
        pltpu.VMEM((LANES, per * channels), bf16),
        pltpu.VMEM((KINDS * LANES, per // 2 * LANES), bf16),
        pltpu.VMEM((rows, n, channels), f32),
    )
    head = pl.pallas_call(
        functools.partial(head_kernel, n, hidden, order),
        out_shape=head_out,
        in_specs=[vmem] * (len(head_in) - 6) + [smem] + [vmem] * 5,
        out_specs=(vmem,) * len(head_out),
        compiler_params=pltpu.CompilerParams(vmem_limit_bytes=16 << 20),
        name="head",
    )(*head_in)
    blocks[last], head = lax.optimization_barrier((blocks[last], head))
    hop(core, [last])
    ordered = [blocks[d] for d in order]
    middle_in = [head[0], head[1], *span(*cuts), token_count, gain, bias, head[8], head[9], gate_weight]
    middle_out = (*stage_out(cuts[1] - cuts[0]), pltpu.VMEM((n, cuts[1] * LANES), f32))
    middle = pl.pallas_call(
        functools.partial(middle_kernel, n, hidden, order, cuts[0]),
        out_shape=middle_out,
        in_specs=[vmem] * (len(middle_in) - 6) + [smem] + [vmem] * 5,
        out_specs=(vmem,) * len(middle_out),
        compiler_params=pltpu.CompilerParams(vmem_limit_bytes=16 << 20),
        name="middle",
    )(*middle_in)
    tall = groups * n
    update, pair_grad, project_grad, gate_grad, output_grad = pl.pallas_call(
        functools.partial(tail_kernel, n, hidden, order, cuts),
        out_shape=(
            shape((rows, n, channels), bf16),
            shape((rows, n, channels), f32),
            shape((KINDS * hidden, channels), f32),
            shape((channels, channels), f32),
            shape((hidden, channels), f32),
        ),
        in_specs=[vmem] * (devices + len(head) + len(middle)) + [smem] + [vmem] * 6,
        out_specs=(vmem,) * 5,
        scratch_shapes=[
            *stage_out(groups - cuts[1]),
            pltpu.VMEM((n * hidden, n * hidden), bf16),
            pltpu.VMEM((per // 2 * tall, 2 * channels), bf16),
            pltpu.VMEM((per // 2 * tall, LANES), bf16),
            pltpu.VMEM((n, cuts[1] * LANES), f32),
            pltpu.VMEM((n, (groups - cuts[1]) * LANES), f32),
            pltpu.VMEM((n, n * hidden), f32),
        ],
        compiler_params=pltpu.CompilerParams(vmem_limit_bytes=32 << 20),
        name="tail",
    )(*ordered, *head, *middle, token_count, gain, bias, project_t, gate_weight, out_gain, out_bias)
    return update, pair_grad, project_grad.T, gate_grad, output_grad


def layer_normalize(values, norm_gain, norm_bias, reduce_axis):
    average = jnp.mean(values, axis=reduce_axis, keepdims=True)
    centered = values - average
    variance = jnp.mean(centered * centered, axis=reduce_axis, keepdims=True)
    inv_std = lax.rsqrt(variance + 1e-05)
    normed = centered * inv_std
    return (normed * norm_gain + norm_bias, normed, inv_std)


def norm_backward_pass(upstream, normed, inv_std, norm_gain, reduce_axis):
    scaled = upstream * norm_gain
    first = jnp.mean(scaled, axis=reduce_axis, keepdims=True)
    second = jnp.mean(scaled * normed, axis=reduce_axis, keepdims=True)
    return inv_std * (scaled - first - normed * second)


def body(
    pair_acts,
    token_count,
    input_gain,
    input_bias,
    project_weight,
    gate_weight,
    output_norm_gain,
    output_shift_bias,
    output_weight,
    update_grad,
):
    single_float_format = jnp.float32
    brain_float_sixteen = jnp.bfloat16
    row_count, length, channels = pair_acts.shape
    hidden = output_weight.shape[0]
    row_start = lax.axis_index("row") * row_count
    live_limit = token_count[0]
    row_live = (row_start + jnp.arange(row_count, dtype=jnp.int32) < live_limit).astype(
        single_float_format
    )
    col_live = (jnp.arange(length, dtype=jnp.int32) < live_limit).astype(single_float_format)
    live_mask = row_live[:, None] * col_live[None, :]
    zn32, zhat, zscale = layer_normalize(
        pair_acts.astype(single_float_format), input_gain, input_bias, -1
    )
    normed_pair = zn32.astype(brain_float_sixteen)
    projected = jnp.einsum(
        "rkd,de->erk", normed_pair, project_weight, preferred_element_type=single_float_format
    ).reshape(4, hidden, row_count, length)
    gate_left = jax.nn.sigmoid(projected[1])
    gate_right = jax.nn.sigmoid(projected[3])
    left_panel = (live_mask * gate_left * projected[0]).astype(brain_float_sixteen)
    right_panel = (live_mask * gate_right * projected[2]).astype(brain_float_sixteen)
    stacked = jnp.stack([left_panel, right_panel], axis=1)
    columns = lax.all_to_all(stacked, "row", split_axis=0, concat_axis=2, tiled=True)
    left_cols = columns[:, 0]
    right_cols = columns[:, 1]
    products = jnp.einsum(
        "cik,cjk->cij", left_cols, right_cols, preferred_element_type=single_float_format
    ).astype(brain_float_sixteen)
    triangle_product = lax.all_to_all(products, "row", split_axis=1, concat_axis=0, tiled=True)
    normed_input_single, standardized_input, input_inverse_scale = layer_normalize(
        triangle_product.astype(single_float_format),
        output_norm_gain[:, None, None],
        output_shift_bias[:, None, None],
        0,
    )
    normed_tri = normed_input_single.astype(brain_float_sixteen)
    mixed = jnp.einsum(
        "crk,cd->rkd", normed_tri, output_weight, preferred_element_type=single_float_format
    )
    gate_out = jax.nn.sigmoid(
        jnp.einsum(
            "rkd,de->rke", normed_pair, gate_weight, preferred_element_type=single_float_format
        )
    )
    update = (gate_out * mixed).astype(brain_float_sixteen)
    cotangent = update_grad.astype(single_float_format)
    mixed_grad = (cotangent * gate_out).astype(brain_float_sixteen)
    gate_logit_grad = (cotangent * mixed * gate_out * (1.0 - gate_out)).astype(brain_float_sixteen)
    output_terms = jnp.einsum(
        "crk,rkd->cd", normed_tri, mixed_grad, preferred_element_type=single_float_format
    )
    triangle_normed_gradient = jnp.einsum(
        "rkd,cd->crk", mixed_grad, output_weight, preferred_element_type=single_float_format
    )
    triangle_gradient = norm_backward_pass(
        triangle_normed_gradient,
        standardized_input,
        input_inverse_scale,
        output_norm_gain[:, None, None],
        0,
    ).astype(brain_float_sixteen)
    grad_cols = lax.all_to_all(triangle_gradient, "row", split_axis=0, concat_axis=1, tiled=True)
    left_col_grad = jnp.einsum(
        "cij,cjk->cik", grad_cols, right_cols, preferred_element_type=single_float_format
    ).astype(brain_float_sixteen)
    right_col_grad = jnp.einsum(
        "cij,cik->cjk", grad_cols, left_cols, preferred_element_type=single_float_format
    ).astype(brain_float_sixteen)
    returned = lax.all_to_all(
        jnp.stack([left_col_grad, right_col_grad], axis=1),
        "row",
        split_axis=2,
        concat_axis=0,
        tiled=True,
    )
    left_grad = returned[:, 0].astype(single_float_format)
    right_grad = returned[:, 1].astype(single_float_format)
    project_terms = jnp.stack(
        [
            left_grad * live_mask * gate_left,
            left_grad * live_mask * projected[0] * gate_left * (1.0 - gate_left),
            right_grad * live_mask * gate_right,
            right_grad * live_mask * projected[2] * gate_right * (1.0 - gate_right),
        ]
    )
    project_terms = project_terms.astype(brain_float_sixteen).reshape(4 * hidden, row_count, length)
    project_part = jnp.einsum(
        "rkd,erk->de", normed_pair, project_terms, preferred_element_type=single_float_format
    )
    gate_part = jnp.einsum(
        "rkd,rke->de", normed_pair, gate_logit_grad, preferred_element_type=single_float_format
    )
    totals = lax.psum((project_part, gate_part, output_terms), "row")
    project_grad = totals[0] / length
    gate_grad = totals[1] / length
    output_grad = totals[2] / length
    normed_grad = jnp.einsum(
        "erk,de->rkd", project_terms, project_weight, preferred_element_type=single_float_format
    ) + jnp.einsum(
        "rke,de->rkd", gate_logit_grad, gate_weight, preferred_element_type=single_float_format
    )
    pair_grad = norm_backward_pass(normed_grad, zhat, zscale, input_gain, -1)
    return (update, pair_grad, project_grad, gate_grad, output_grad)


def fits_whole(mesh, args):
    pair_acts, output_weight = args[0], args[8]
    devices = mesh.shape["row"]
    length, channels = pair_acts.shape[0] // mesh.shape["grp"], pair_acts.shape[2]
    hidden = output_weight.shape[0]
    return (
        channels == LANES
        and hidden % 16 == 0
        and LANES % hidden == 0
        and length % (LANES // hidden) == 0
        and (LANES // hidden) % 8 == 0
        and length % 16 == 0
        and length % devices == 0
        and length // devices <= LANES // hidden
        and devices in (8, 16)
        and 2 * KINDS * hidden == LANES
        and length // (LANES // hidden) >= 4
        and length // 2 % (LANES // hidden) == 0
        and 2 * pair_acts.dtype.itemsize * length * length * channels <= WHOLE_BYTES
    )


def solution(mesh):
    in_specs = (
        P(("grp", "row"), None, None),
        P("grp"),
        P(),
        P(),
        P(),
        P(),
        P(),
        P(),
        P(),
        P(("grp", "row"), None, None),
    )
    out_specs = (
        P(("grp", "row"), None, None),
        P(("grp", "row"), None, None),
        P("grp", None),
        P("grp", None),
        P("grp", None),
    )
    devices = mesh.shape["row"]

    def run(*args):
        crop = functools.partial(body_whole, devices) if fits_whole(mesh, args) else body
        return jax.shard_map(crop, mesh=mesh, in_specs=in_specs, out_specs=out_specs, check_vma=False)(*args)

    return run
```

```python
import functools

import jax
import jax.numpy as jnp
from jax import lax
from jax.experimental import pallas as pl
from jax.experimental.pallas import tpu as pltpu
from jax.sharding import PartitionSpec as P

LANES = 128
KINDS = 4
WHOLE_BYTES = 4 << 20

NN = (((1,), (0,)), ((), ()))
NT = (((1,), (1,)), ((), ()))
TN = (((0,), (0,)), ((), ()))


def dot(a, b, dims=NN):
    return lax.dot_general(a, b, dims, preferred_element_type=jnp.float32)


def dot_split(a, b_twice):
    high = a.astype(jnp.bfloat16)
    low = (a - high.astype(jnp.float32)).astype(jnp.bfloat16)
    return dot(jnp.concatenate([high, low], axis=1), b_twice)


def iota(shape, dim):
    return lax.broadcasted_iota(jnp.int32, shape, dim)


def zero_one(condition):
    return jnp.where(condition, 1.0, 0.0).astype(jnp.bfloat16)


def sigmoid(v):
    return 1.0 / (1.0 + jnp.exp(-v))


def normalize(v):
    centered = v - jnp.mean(v, axis=-1, keepdims=True)
    s = lax.rsqrt(jnp.mean(centered * centered, axis=-1, keepdims=True) + 1e-05)
    return centered * s, s


def row_of(order, rows, t):
    return (lax.axis_index("row") ^ order[t // rows]) * rows + t % rows


def rows_of_lanes(order, rows, hidden, group):
    per = LANES // hidden
    place = iota((1, LANES), 1) // hidden
    at = jnp.full((1, LANES), row_of(order, rows, group * per), jnp.int32)
    for p in range(1, per):
        at = jnp.where(place == p, row_of(order, rows, group * per + p), at)
    return at


def stage(n, hidden, order, first, block_refs, count, gain, bias, project_wide, out_wide, gate_weight, refs):
    left_ref, right_ref, mask_ref, slope_ref, dy_ref, dgo_part_ref, dxn_ref, znt_ref = refs
    f32, bf16 = jnp.float32, jnp.bfloat16
    per = LANES // hidden
    rows = n // len(order)
    tall = left_ref.shape[0]
    start = first * per
    zn, cotangent = {}, {}
    for t in range(start, start + per * (tall // n)):
        block, at = block_refs[t // rows - start // rows], t % rows * n
        zn[t] = (normalize(block[pl.ds(at, n), :].astype(f32))[0] * gain + bias).astype(bf16)
        cotangent[t] = block[pl.ds((rows + t % rows) * n, n), :]

    def place(tiles, p):
        return jnp.concatenate([tiles[t] for t in range(start + p, start + per * (tall // n), per)], axis=0)

    zn = [place(zn, p) for p in range(per)]
    projected = dot(jnp.concatenate(zn, axis=1), project_wide, NT)
    live_k = iota((n, LANES), 0) < count
    mask = [
        jnp.where(live_k & (rows_of_lanes(order, rows, hidden, first + g) < count), 1.0, 0.0) for g in range(tall // n)
    ]
    mask = jnp.concatenate(mask, axis=0)
    for side, ref in enumerate((left_ref, right_ref)):
        value = projected[:, 2 * side * LANES : (2 * side + 1) * LANES]
        gate = sigmoid(projected[:, (2 * side + 1) * LANES : (2 * side + 2) * LANES])
        ref[...] = (mask * gate * value).astype(bf16)
        mask_ref[side] = mask * gate
        slope_ref[side] = value * (1.0 - gate)
    own = []
    zn_tall = jnp.concatenate(zn, axis=0)
    gates = sigmoid(dot(zn_tall, gate_weight))
    for p in range(per):
        go = gates[p * tall : (p + 1) * tall]
        dy = place(cotangent, p).astype(f32) * go
        dy_ref[:, p * LANES : (p + 1) * LANES] = dy.astype(bf16)
        dgo_part_ref[p] = dy * (1.0 - go)
        own.append(go[:n])
    dxn_ref[...] = dot(dy_ref[...], out_wide, NT)
    half = per // 2 * tall
    znt_ref[0] = zn_tall[:half].T
    znt_ref[1] = zn_tall[half:].T
    return own


def wide_project(project_t, per):
    hidden, channels = project_t.shape[0] // KINDS, project_t.shape[1]
    columns = []
    for p in range(per):
        parts = []
        for kind in range(KINDS):
            before, after = p * hidden, (per - 1 - p) * hidden
            parts += [jnp.zeros((before, channels), project_t.dtype)] * (before > 0)
            parts += [project_t[kind * hidden : (kind + 1) * hidden]]
            parts += [jnp.zeros((after, channels), project_t.dtype)] * (after > 0)
        columns.append(jnp.concatenate(parts, axis=0))
    return jnp.concatenate(columns, axis=1)


def wide_out(out_weight, per):
    hidden, channels = out_weight.shape
    rows = []
    for p in range(per):
        before, after = p * channels, (per - 1 - p) * channels
        parts = [jnp.zeros((hidden, before), out_weight.dtype)] * (before > 0) + [out_weight]
        rows.append(jnp.concatenate(parts + [jnp.zeros((hidden, after), out_weight.dtype)] * (after > 0), axis=1))
    return jnp.concatenate(rows, axis=0)


def pick_place(per, hidden):
    half = per // 2
    rows = []
    for kind in range(KINDS):
        for p in range(per):
            column = (p // half * KINDS + kind) * hidden
            own = zero_one(iota((hidden, LANES), 1) == iota((hidden, LANES), 0) + column)
            before, after = p % half * LANES, (half - 1 - p % half) * LANES
            parts = [jnp.zeros((hidden, before), own.dtype)] * (before > 0) + [own]
            rows.append(jnp.concatenate(parts + [jnp.zeros((hidden, after), own.dtype)] * (after > 0), axis=1))
    return jnp.concatenate(rows, axis=0)


def load_kernel(*refs):
    count = len(refs) // 2
    sources, targets, sems = refs[:count], refs[count : 2 * count - 1], refs[-1]
    half = sources[0].shape[0]
    targets = [targets[0].at[pl.ds(0, half)], targets[0].at[pl.ds(half, half)], *targets[1:]]
    copies = [pltpu.make_async_copy(a, b, sems.at[k]) for k, (a, b) in enumerate(zip(sources, targets))]
    for copy in copies:
        copy.start()
    for copy in copies:
        copy.wait()


def cross(n, hidden, order, lefts, rights, first, store):
    wide = lefts.shape[1]
    same = iota((hidden, wide), 0) == iota((hidden, wide), 1) % hidden
    product = dot(rights, lefts, TN)
    for t in range(rights.shape[1] // hidden):
        own = jnp.where(same, product[t * hidden : (t + 1) * hidden], 0.0)
        store(pl.ds(row_of(order, n // len(order), first + t), 1), jnp.sum(own, axis=0, keepdims=True))


def side_by_side(ref, n):
    return jnp.concatenate([ref[pl.ds(g * n, n), :] for g in range(ref.shape[0] // n)], axis=1)


def head_kernel(n, hidden, order, *refs):
    *block_refs, count_ref, gain_ref, bias_ref, project_ref, gate_ref, out_weight_ref = refs[:-12]
    *stage_refs, project_wide_ref, out_wide_ref, pick_ref, own_ref = refs[-12:]
    per = LANES // hidden
    project_wide_ref[...] = wide_project(project_ref[...], per)
    out_wide_ref[...] = wide_out(out_weight_ref[...], per)
    pick_ref[...] = pick_place(per, hidden)
    weights = [ref[...] for ref in (gain_ref, bias_ref, project_wide_ref, out_wide_ref, gate_ref)]
    own = stage(n, hidden, order, 0, block_refs, count_ref[0], *weights, stage_refs)
    for r in range(own_ref.shape[0]):
        own_ref[r] = own[r]


def middle_kernel(n, hidden, order, first, *refs):
    left_head_ref, right_head_ref, *block_refs = refs[:-15]
    count_ref, gain_ref, bias_ref, project_wide_ref, out_wide_ref, gate_ref = refs[-15:-9]
    *stage_refs, x_ref = refs[-9:]
    weights = [ref[...] for ref in (gain_ref, bias_ref, project_wide_ref, out_wide_ref, gate_ref)]
    stage(n, hidden, order, first, block_refs, count_ref[0], *weights, stage_refs)
    left = jnp.concatenate([side_by_side(left_head_ref, n), side_by_side(stage_refs[0], n)], axis=1)
    right = jnp.concatenate([side_by_side(right_head_ref, n), side_by_side(stage_refs[1], n)], axis=1)
    x_ref[...] = jnp.zeros_like(x_ref)

    def store(row, value):
        x_ref[row, :] = value

    cross(n, hidden, order, left, right, 0, store)


def tail_kernel(n, hidden, order, cuts, *refs):
    blocks = len(order)
    block_refs, refs = refs[:blocks], refs[blocks:]
    head_refs, (project_wide_ref, out_wide_ref, pick_ref, own_ref), middle_refs = refs[:8], refs[8:12], refs[12:20]
    x_early_ref, *refs = refs[20:]
    count_ref, gain_ref, bias_ref, project_ref, gate_ref, out_gain_ref, out_bias_ref = refs[:7]
    update_ref, pair_ref, project_grad_ref, gate_grad_ref, out_grad_ref = refs[7:12]
    tail_refs, (square_ref, dgo_ref, dp_ref, x_ref, x_late_ref, dx_ref) = refs[12:20], refs[20:]
    stages = (head_refs, middle_refs, tail_refs)
    f32, bf16 = jnp.float32, jnp.bfloat16
    per = LANES // hidden
    groups = n // per
    wide = n * hidden
    rows = n // blocks
    gain, gate_weight, project_t = gain_ref[...], gate_ref[...], project_ref[...]
    weights = gain, bias_ref[...], project_wide_ref[...], out_wide_ref[...], gate_weight
    stage(n, hidden, order, cuts[1], block_refs[cuts[1] * per // rows :], count_ref[0], *weights, tail_refs)

    spans = [(low * n, high * n) for low, high in zip((0, *cuts), (*cuts, groups))]
    half = per // 2

    def put(ref, q, column, value):
        for low, high in spans:
            ref[pl.ds(low * half + q * (high - low), high - low), pl.ds(column, LANES)] = value[low:high]

    def sum_pairs(ref):
        znt = [refs[7][...].reshape(2 * LANES, half * (high - low)) for refs, (low, high) in zip(stages, spans)]
        rows_of = [ref[pl.ds(low * half, (high - low) * half), :] for low, high in spans]
        return sum(dot(a, b) for a, b in zip(znt, rows_of))

    def all_rows(k):
        return jnp.concatenate([refs[k][...] for refs in stages], axis=0)


    def lanes(flat):
        return jnp.concatenate([flat[g * n : (g + 1) * n] for g in range(groups)], axis=1)

    def flatten(rowed):
        return jnp.concatenate([rowed[:, g * LANES : (g + 1) * LANES] for g in range(groups)], axis=0)

    left, right = lanes(all_rows(0)), lanes(all_rows(1))

    split = cuts[1] * LANES
    x_ref[...] = jnp.zeros_like(x_ref)

    def store_late(row, value):
        x_late_ref[row, :] = value

    def store_both(row, value):
        x_ref[row, :] = value[:, :split]
        x_late_ref[row, :] = value[:, split:]

    cross(n, hidden, order, left[:, split:], right[:, :split], 0, store_late)
    cross(n, hidden, order, left, right[:, split:], split // hidden, store_both)
    x = jnp.concatenate([x_early_ref[...] + x_ref[...], x_late_ref[...]], axis=1)
    x = flatten(x.astype(bf16).astype(f32))

    mean = jnp.where(iota((LANES, LANES), 0) // hidden == iota((LANES, LANES), 1) // hidden, 1.0 / hidden, 0.0)
    mean = mean.astype(bf16)
    mean_twice = jnp.concatenate([mean, mean], axis=0)
    out_gain = jnp.concatenate([out_gain_ref[...]] * per, axis=1)
    out_bias = jnp.concatenate([out_bias_ref[...]] * per, axis=1)
    centered = x - dot(x.astype(bf16), mean)
    xs = lax.rsqrt(dot_split(centered * centered, mean_twice) + 1e-05)
    xhat = centered * xs
    xn = (xhat * out_gain + out_bias).astype(bf16)

    u = out_gain * all_rows(6)
    dx = xs * (u - dot_split(u, mean_twice) - xhat * dot_split(u * xhat, mean_twice))
    dx_ref[...] = lanes(dx.astype(bf16)).astype(f32)

    same = iota((hidden, wide), 0) == iota((hidden, wide), 1) % hidden
    for t in range(n):
        row = dx_ref[pl.ds(row_of(order, rows, t), 1), :]
        row = jnp.broadcast_to(row, (hidden, wide)).astype(bf16)
        square_ref[pl.ds(t * hidden, hidden), :] = jnp.where(same, row, jnp.zeros_like(row))
    y_all = dot(xn, out_wide_ref[...])
    own_dgo = []
    for p in range(per):
        y = y_all[:, p * LANES : (p + 1) * LANES]
        dgo = (jnp.concatenate([refs[5][p] for refs in stages], axis=0) * y).astype(bf16)
        put(dgo_ref, p % half, p // half * LANES, dgo)
        if p < rows:
            update_ref[p] = (own_ref[p] * y[:n]).astype(bf16)
            own_dgo.append(dgo[:n])
    diagonal = square_ref[...]
    dleft = flatten(dot(right, diagonal).astype(bf16)).astype(f32)
    dright = flatten(dot(left, diagonal, NT).astype(bf16)).astype(f32)
    xnt, dy = xn.T, all_rows(4)
    out_grad = [dot(xnt[p * hidden : (p + 1) * hidden], dy[:, p * LANES : (p + 1) * LANES]) for p in range(per)]
    out_grad_ref[...] = sum(out_grad) / n
    gate_grad = sum_pairs(dgo_ref)
    gate_grad_ref[...] = (gate_grad[:LANES, :LANES] + gate_grad[LANES:, LANES:]) / n

    dp = []
    for side, grad in enumerate((dleft, dright)):
        masked = grad * jnp.concatenate([refs[2][side] for refs in stages], axis=0)
        dp += [masked, masked * jnp.concatenate([refs[3][side] for refs in stages], axis=0)]
    dp = jnp.concatenate([d.astype(bf16) for d in dp], axis=1)
    by_place = dot(dp, pick_ref[...]).astype(bf16)
    for q in range(half):
        put(dp_ref, q, 0, by_place[:, q * LANES : (q + 1) * LANES])
    tiled = [project_t[kind * hidden : (kind + 1) * hidden] for kind in range(KINDS) for _ in range(per)]
    place = iota((n, KINDS * LANES), 1) % LANES // hidden
    dp_rows = [jnp.where(place == r, dp[:n], jnp.zeros_like(dp[:n])) for r in range(rows)]
    dzn = dot(jnp.concatenate(dp_rows, axis=0), jnp.concatenate(tiled, axis=0))
    dzn += dot(jnp.concatenate(own_dgo, axis=0), gate_weight, NT)
    zhat, zs = normalize(block_refs[0][pl.ds(0, rows * n), :].astype(f32))
    u = gain * dzn
    first = jnp.mean(u, axis=-1, keepdims=True)
    second = jnp.mean(u * zhat, axis=-1, keepdims=True)
    pair_grad = zs * (u - first - zhat * second)
    for r in range(rows):
        pair_ref[r] = pair_grad[r * n : (r + 1) * n]

    project_grad = sum_pairs(dp_ref).T
    width = KINDS * hidden
    project_grad_ref[...] = (project_grad[:width, :LANES] + project_grad[width:, LANES:]) / n


def body_whole(
    devices,
    pair_acts,
    token_count,
    input_gain,
    input_bias,
    project_weight,
    gate_weight,
    output_norm_gain,
    output_shift_bias,
    output_weight,
    update_grad,
):
    rows, n, channels = pair_acts.shape
    hidden = output_weight.shape[0]
    f32, bf16 = jnp.float32, jnp.bfloat16
    half = rows * n
    vmem, anywhere = pl.BlockSpec(memory_space=pltpu.VMEM), pl.BlockSpec(memory_space=pl.ANY)
    shape = jax.ShapeDtypeStruct
    sources = [
        pair_acts.reshape(half, channels),
        update_grad.reshape(half, channels),
        input_gain[None],
        input_bias[None],
        project_weight.T,
        gate_weight,
        output_norm_gain[None],
        output_shift_bias[None],
        output_weight,
    ]
    send, gain, bias, project_t, gate_weight, out_gain, out_bias, out_weight = pl.pallas_call(
        load_kernel,
        out_shape=[pltpu.VMEM((2 * half, channels), bf16)] + [pltpu.VMEM(v.shape, v.dtype) for v in sources[2:]],
        in_specs=[anywhere] * len(sources),
        out_specs=[vmem] * (len(sources) - 1),
        scratch_shapes=[pltpu.SemaphoreType.DMA((len(sources),))],
        name="load",
    )(*sources)
    blocks = {0: send}
    core, x, *z = [1 << bit for bit in range(devices.bit_length() - 1)]

    def hop(step, sources):
        pairs = [(i, i ^ step) for i in range(devices)]
        for d in sources:
            blocks[d ^ step] = lax.ppermute(blocks[d], "row", pairs)

    for step in reversed(z):
        hop(step, [0])
        if step == z[-1]:
            hop(x, [0])
    for k, step in enumerate(z[:-1]):
        hop(step, [x])
        hop(step, [d for d in list(blocks) if 0 < d and d % (2 * step) == 0])
    hop(x, [d for d in list(blocks) if not d & x and d ^ x not in blocks])
    last = devices - 1 - core
    hop(core, [d for d in list(blocks) if d != last])
    order = sorted(range(devices), key=lambda d: (2 * d.bit_count() + (d & x) / x, -(d & core), -d))
    ordered = [blocks.get(d) for d in order]
    per = LANES // hidden
    groups = n // per
    cuts = (groups // 2, groups - 1)

    def stage_out(count):
        tall = count * n
        return (
            pltpu.VMEM((tall, LANES), bf16),
            pltpu.VMEM((tall, LANES), bf16),
            pltpu.VMEM((2, tall, LANES), f32),
            pltpu.VMEM((2, tall, LANES), f32),
            pltpu.VMEM((tall, per * channels), bf16),
            pltpu.VMEM((per, tall, channels), f32),
            pltpu.VMEM((tall, LANES), f32),
            pltpu.VMEM((2, channels, per // 2 * tall), bf16),
        )

    def span(first, last):
        return ordered[first * per // rows : -(-last * per // rows)]

    head_in = [*span(0, cuts[0]), token_count, gain, bias, project_t, gate_weight, out_weight]
    smem = pl.BlockSpec(memory_space=pltpu.SMEM)
    head_out = (
        *stage_out(cuts[0]),
        pltpu.VMEM((KINDS * LANES, per * channels), bf16),
        pltpu.VMEM((LANES, per * channels), bf16),
        pltpu.VMEM((KINDS * LANES, per // 2 * LANES), bf16),
        pltpu.VMEM((rows, n, channels), f32),
    )
    head = pl.pallas_call(
        functools.partial(head_kernel, n, hidden, order),
        out_shape=head_out,
        in_specs=[vmem] * (len(head_in) - 6) + [smem] + [vmem] * 5,
        out_specs=(vmem,) * len(head_out),
        compiler_params=pltpu.CompilerParams(vmem_limit_bytes=16 << 20),
        name="head",
    )(*head_in)
    blocks[last], head = lax.optimization_barrier((blocks[last], head))
    hop(core, [last])
    ordered = [blocks[d] for d in order]
    middle_in = [head[0], head[1], *span(*cuts), token_count, gain, bias, head[8], head[9], gate_weight]
    middle_out = (*stage_out(cuts[1] - cuts[0]), pltpu.VMEM((n, cuts[1] * LANES), f32))
    middle = pl.pallas_call(
        functools.partial(middle_kernel, n, hidden, order, cuts[0]),
        out_shape=middle_out,
        in_specs=[vmem] * (len(middle_in) - 6) + [smem] + [vmem] * 5,
        out_specs=(vmem,) * len(middle_out),
        compiler_params=pltpu.CompilerParams(vmem_limit_bytes=16 << 20),
        name="middle",
    )(*middle_in)
    tall = groups * n
    update, pair_grad, project_grad, gate_grad, output_grad = pl.pallas_call(
        functools.partial(tail_kernel, n, hidden, order, cuts),
        out_shape=(
            shape((rows, n, channels), bf16),
            shape((rows, n, channels), f32),
            shape((KINDS * hidden, channels), f32),
            shape((channels, channels), f32),
            shape((hidden, channels), f32),
        ),
        in_specs=[vmem] * (devices + len(head) + len(middle)) + [smem] + [vmem] * 6,
        out_specs=(vmem,) * 5,
        scratch_shapes=[
            *stage_out(groups - cuts[1]),
            pltpu.VMEM((n * hidden, n * hidden), bf16),
            pltpu.VMEM((per // 2 * tall, 2 * channels), bf16),
            pltpu.VMEM((per // 2 * tall, LANES), bf16),
            pltpu.VMEM((n, cuts[1] * LANES), f32),
            pltpu.VMEM((n, (groups - cuts[1]) * LANES), f32),
            pltpu.VMEM((n, n * hidden), f32),
        ],
        compiler_params=pltpu.CompilerParams(vmem_limit_bytes=32 << 20),
        name="tail",
    )(*ordered, *head, *middle, token_count, gain, bias, project_t, gate_weight, out_gain, out_bias)
    return update, pair_grad, project_grad.T, gate_grad, output_grad


def layer_normalize(values, norm_gain, norm_bias, reduce_axis):
    average = jnp.mean(values, axis=reduce_axis, keepdims=True)
    centered = values - average
    variance = jnp.mean(centered * centered, axis=reduce_axis, keepdims=True)
    inv_std = lax.rsqrt(variance + 1e-05)
    normed = centered * inv_std
    return (normed * norm_gain + norm_bias, normed, inv_std)


def norm_backward_pass(upstream, normed, inv_std, norm_gain, reduce_axis):
    scaled = upstream * norm_gain
    first = jnp.mean(scaled, axis=reduce_axis, keepdims=True)
    second = jnp.mean(scaled * normed, axis=reduce_axis, keepdims=True)
    return inv_std * (scaled - first - normed * second)


def body(
    pair_acts,
    token_count,
    input_gain,
    input_bias,
    project_weight,
    gate_weight,
    output_norm_gain,
    output_shift_bias,
    output_weight,
    update_grad,
):
    single_float_format = jnp.float32
    brain_float_sixteen = jnp.bfloat16
    row_count, length, channels = pair_acts.shape
    hidden = output_weight.shape[0]
    row_start = lax.axis_index("row") * row_count
    live_limit = token_count[0]
    row_live = (row_start + jnp.arange(row_count, dtype=jnp.int32) < live_limit).astype(
        single_float_format
    )
    col_live = (jnp.arange(length, dtype=jnp.int32) < live_limit).astype(single_float_format)
    live_mask = row_live[:, None] * col_live[None, :]
    zn32, zhat, zscale = layer_normalize(
        pair_acts.astype(single_float_format), input_gain, input_bias, -1
    )
    normed_pair = zn32.astype(brain_float_sixteen)
    projected = jnp.einsum(
        "rkd,de->erk", normed_pair, project_weight, preferred_element_type=single_float_format
    ).reshape(4, hidden, row_count, length)
    gate_left = jax.nn.sigmoid(projected[1])
    gate_right = jax.nn.sigmoid(projected[3])
    left_panel = (live_mask * gate_left * projected[0]).astype(brain_float_sixteen)
    right_panel = (live_mask * gate_right * projected[2]).astype(brain_float_sixteen)
    stacked = jnp.stack([left_panel, right_panel], axis=1)
    columns = lax.all_to_all(stacked, "row", split_axis=0, concat_axis=2, tiled=True)
    left_cols = columns[:, 0]
    right_cols = columns[:, 1]
    products = jnp.einsum(
        "cik,cjk->cij", left_cols, right_cols, preferred_element_type=single_float_format
    ).astype(brain_float_sixteen)
    triangle_product = lax.all_to_all(products, "row", split_axis=1, concat_axis=0, tiled=True)
    normed_input_single, standardized_input, input_inverse_scale = layer_normalize(
        triangle_product.astype(single_float_format),
        output_norm_gain[:, None, None],
        output_shift_bias[:, None, None],
        0,
    )
    normed_tri = normed_input_single.astype(brain_float_sixteen)
    mixed = jnp.einsum(
        "crk,cd->rkd", normed_tri, output_weight, preferred_element_type=single_float_format
    )
    gate_out = jax.nn.sigmoid(
        jnp.einsum(
            "rkd,de->rke", normed_pair, gate_weight, preferred_element_type=single_float_format
        )
    )
    update = (gate_out * mixed).astype(brain_float_sixteen)
    cotangent = update_grad.astype(single_float_format)
    mixed_grad = (cotangent * gate_out).astype(brain_float_sixteen)
    gate_logit_grad = (cotangent * mixed * gate_out * (1.0 - gate_out)).astype(brain_float_sixteen)
    output_terms = jnp.einsum(
        "crk,rkd->cd", normed_tri, mixed_grad, preferred_element_type=single_float_format
    )
    triangle_normed_gradient = jnp.einsum(
        "rkd,cd->crk", mixed_grad, output_weight, preferred_element_type=single_float_format
    )
    triangle_gradient = norm_backward_pass(
        triangle_normed_gradient,
        standardized_input,
        input_inverse_scale,
        output_norm_gain[:, None, None],
        0,
    ).astype(brain_float_sixteen)
    grad_cols = lax.all_to_all(triangle_gradient, "row", split_axis=0, concat_axis=1, tiled=True)
    left_col_grad = jnp.einsum(
        "cij,cjk->cik", grad_cols, right_cols, preferred_element_type=single_float_format
    ).astype(brain_float_sixteen)
    right_col_grad = jnp.einsum(
        "cij,cik->cjk", grad_cols, left_cols, preferred_element_type=single_float_format
    ).astype(brain_float_sixteen)
    returned = lax.all_to_all(
        jnp.stack([left_col_grad, right_col_grad], axis=1),
        "row",
        split_axis=2,
        concat_axis=0,
        tiled=True,
    )
    left_grad = returned[:, 0].astype(single_float_format)
    right_grad = returned[:, 1].astype(single_float_format)
    project_terms = jnp.stack(
        [
            left_grad * live_mask * gate_left,
            left_grad * live_mask * projected[0] * gate_left * (1.0 - gate_left),
            right_grad * live_mask * gate_right,
            right_grad * live_mask * projected[2] * gate_right * (1.0 - gate_right),
        ]
    )
    project_terms = project_terms.astype(brain_float_sixteen).reshape(4 * hidden, row_count, length)
    project_part = jnp.einsum(
        "rkd,erk->de", normed_pair, project_terms, preferred_element_type=single_float_format
    )
    gate_part = jnp.einsum(
        "rkd,rke->de", normed_pair, gate_logit_grad, preferred_element_type=single_float_format
    )
    totals = lax.psum((project_part, gate_part, output_terms), "row")
    project_grad = totals[0] / length
    gate_grad = totals[1] / length
    output_grad = totals[2] / length
    normed_grad = jnp.einsum(
        "erk,de->rkd", project_terms, project_weight, preferred_element_type=single_float_format
    ) + jnp.einsum(
        "rke,de->rkd", gate_logit_grad, gate_weight, preferred_element_type=single_float_format
    )
    pair_grad = norm_backward_pass(normed_grad, zhat, zscale, input_gain, -1)
    return (update, pair_grad, project_grad, gate_grad, output_grad)


def fits_whole(mesh, args):
    pair_acts, output_weight = args[0], args[8]
    devices = mesh.shape["row"]
    length, channels = pair_acts.shape[0] // mesh.shape["grp"], pair_acts.shape[2]
    hidden = output_weight.shape[0]
    return (
        channels == LANES
        and hidden % 16 == 0
        and LANES % hidden == 0
        and length % (LANES // hidden) == 0
        and (LANES // hidden) % 8 == 0
        and length % 16 == 0
        and length % devices == 0
        and length // devices <= LANES // hidden
        and devices in (8, 16)
        and 2 * KINDS * hidden == LANES
        and length // (LANES // hidden) >= 4
        and length // 2 % (LANES // hidden) == 0
        and 2 * pair_acts.dtype.itemsize * length * length * channels <= WHOLE_BYTES
    )


def solution(mesh):
    in_specs = (
        P(("grp", "row"), None, None),
        P("grp"),
        P(),
        P(),
        P(),
        P(),
        P(),
        P(),
        P(),
        P(("grp", "row"), None, None),
    )
    out_specs = (
        P(("grp", "row"), None, None),
        P(("grp", "row"), None, None),
        P("grp", None),
        P("grp", None),
        P("grp", None),
    )
    devices = mesh.shape["row"]

    def run(*args):
        crop = functools.partial(body_whole, devices) if fits_whole(mesh, args) else body
        return jax.shard_map(crop, mesh=mesh, in_specs=in_specs, out_specs=out_specs, check_vma=False)(*args)

    return run
```

```python
import functools

import jax
import jax.numpy as jnp
from jax import lax
from jax.experimental import pallas as pl
from jax.experimental.pallas import tpu as pltpu
from jax.sharding import PartitionSpec as P

LANES = 128
KINDS = 4
WHOLE_BYTES = 4 << 20

NN = (((1,), (0,)), ((), ()))
NT = (((1,), (1,)), ((), ()))
TN = (((0,), (0,)), ((), ()))


def dot(a, b, dims=NN):
    return lax.dot_general(a, b, dims, preferred_element_type=jnp.float32)


def dot_split(a, b_twice):
    high = a.astype(jnp.bfloat16)
    low = (a - high.astype(jnp.float32)).astype(jnp.bfloat16)
    return dot(jnp.concatenate([high, low], axis=1), b_twice)


def iota(shape, dim):
    return lax.broadcasted_iota(jnp.int32, shape, dim)


def zero_one(condition):
    return jnp.where(condition, 1.0, 0.0).astype(jnp.bfloat16)


def sigmoid(v):
    return 1.0 / (1.0 + jnp.exp(-v))


def normalize(v):
    centered = v - jnp.mean(v, axis=-1, keepdims=True)
    s = lax.rsqrt(jnp.mean(centered * centered, axis=-1, keepdims=True) + 1e-05)
    return centered * s, s


def row_of(order, rows, t):
    return (lax.axis_index("row") ^ order[t // rows]) * rows + t % rows


def rows_of_lanes(order, rows, hidden, group):
    per = LANES // hidden
    place = iota((1, LANES), 1) // hidden
    at = jnp.full((1, LANES), row_of(order, rows, group * per), jnp.int32)
    for p in range(1, per):
        at = jnp.where(place == p, row_of(order, rows, group * per + p), at)
    return at


def stage(n, hidden, order, first, block_refs, count, gain, bias, project_wide, out_wide, gate_weight, refs):
    left_ref, right_ref, mask_ref, slope_ref, dy_ref, dgo_part_ref, dxn_ref, znt_ref = refs
    f32, bf16 = jnp.float32, jnp.bfloat16
    per = LANES // hidden
    rows = n // len(order)
    tall = left_ref.shape[0]
    start = first * per
    zn, cotangent = {}, {}
    for t in range(start, start + per * (tall // n)):
        block, at = block_refs[t // rows - start // rows], t % rows * n
        zn[t] = (normalize(block[pl.ds(at, n), :].astype(f32))[0] * gain + bias).astype(bf16)
        cotangent[t] = block[pl.ds((rows + t % rows) * n, n), :]

    def place(tiles, p):
        return jnp.concatenate([tiles[t] for t in range(start + p, start + per * (tall // n), per)], axis=0)

    zn = [place(zn, p) for p in range(per)]
    projected = dot(jnp.concatenate(zn, axis=1), project_wide, NT)
    live_k = iota((n, LANES), 0) < count
    mask = [
        jnp.where(live_k & (rows_of_lanes(order, rows, hidden, first + g) < count), 1.0, 0.0) for g in range(tall // n)
    ]
    mask = jnp.concatenate(mask, axis=0)
    for side, ref in enumerate((left_ref, right_ref)):
        value = projected[:, 2 * side * LANES : (2 * side + 1) * LANES]
        gate = sigmoid(projected[:, (2 * side + 1) * LANES : (2 * side + 2) * LANES])
        ref[...] = (mask * gate * value).astype(bf16)
        mask_ref[side] = mask * gate
        slope_ref[side] = value * (1.0 - gate)
    own = []
    zn_tall = jnp.concatenate(zn, axis=0)
    gates = sigmoid(dot(zn_tall, gate_weight))
    for p in range(per):
        go = gates[p * tall : (p + 1) * tall]
        dy = place(cotangent, p).astype(f32) * go
        dy_ref[:, p * LANES : (p + 1) * LANES] = dy.astype(bf16)
        dgo_part_ref[p] = dy * (1.0 - go)
        own.append(go[:n])
    dxn_ref[...] = dot(dy_ref[...], out_wide, NT)
    half = per // 2 * tall
    znt_ref[0] = zn_tall[:half].T
    znt_ref[1] = zn_tall[half:].T
    return own


def wide_project(project_t, per):
    hidden, channels = project_t.shape[0] // KINDS, project_t.shape[1]
    columns = []
    for p in range(per):
        parts = []
        for kind in range(KINDS):
            before, after = p * hidden, (per - 1 - p) * hidden
            parts += [jnp.zeros((before, channels), project_t.dtype)] * (before > 0)
            parts += [project_t[kind * hidden : (kind + 1) * hidden]]
            parts += [jnp.zeros((after, channels), project_t.dtype)] * (after > 0)
        columns.append(jnp.concatenate(parts, axis=0))
    return jnp.concatenate(columns, axis=1)


def wide_out(out_weight, per):
    hidden, channels = out_weight.shape
    rows = []
    for p in range(per):
        before, after = p * channels, (per - 1 - p) * channels
        parts = [jnp.zeros((hidden, before), out_weight.dtype)] * (before > 0) + [out_weight]
        rows.append(jnp.concatenate(parts + [jnp.zeros((hidden, after), out_weight.dtype)] * (after > 0), axis=1))
    return jnp.concatenate(rows, axis=0)


def pick_place(per, hidden):
    half = per // 2
    rows = []
    for kind in range(KINDS):
        for p in range(per):
            column = (p // half * KINDS + kind) * hidden
            own = zero_one(iota((hidden, LANES), 1) == iota((hidden, LANES), 0) + column)
            before, after = p % half * LANES, (half - 1 - p % half) * LANES
            parts = [jnp.zeros((hidden, before), own.dtype)] * (before > 0) + [own]
            rows.append(jnp.concatenate(parts + [jnp.zeros((hidden, after), own.dtype)] * (after > 0), axis=1))
    return jnp.concatenate(rows, axis=0)


def load_kernel(*refs):
    count = len(refs) // 2
    sources, targets, sems = refs[:count], refs[count : 2 * count - 1], refs[-1]
    half = sources[0].shape[0]
    targets = [targets[0].at[pl.ds(0, half)], targets[0].at[pl.ds(half, half)], *targets[1:]]
    copies = [pltpu.make_async_copy(a, b, sems.at[k]) for k, (a, b) in enumerate(zip(sources, targets))]
    for copy in copies:
        copy.start()
    for copy in copies:
        copy.wait()


def cross(n, hidden, order, lefts, rights, first, store):
    wide = lefts.shape[1]
    same = iota((hidden, wide), 0) == iota((hidden, wide), 1) % hidden
    product = dot(rights, lefts, TN)
    for t in range(rights.shape[1] // hidden):
        own = jnp.where(same, product[t * hidden : (t + 1) * hidden], 0.0)
        store(pl.ds(row_of(order, n // len(order), first + t), 1), jnp.sum(own, axis=0, keepdims=True))


def side_by_side(ref, n):
    return jnp.concatenate([ref[pl.ds(g * n, n), :] for g in range(ref.shape[0] // n)], axis=1)


def head_kernel(n, hidden, order, *refs):
    *block_refs, count_ref, gain_ref, bias_ref, project_ref, gate_ref, out_weight_ref = refs[:-12]
    *stage_refs, project_wide_ref, out_wide_ref, pick_ref, own_ref = refs[-12:]
    per = LANES // hidden
    project_wide_ref[...] = wide_project(project_ref[...], per)
    out_wide_ref[...] = wide_out(out_weight_ref[...], per)
    pick_ref[...] = pick_place(per, hidden)
    weights = [ref[...] for ref in (gain_ref, bias_ref, project_wide_ref, out_wide_ref, gate_ref)]
    own = stage(n, hidden, order, 0, block_refs, count_ref[0], *weights, stage_refs)
    for r in range(own_ref.shape[0]):
        own_ref[r] = own[r]


def middle_kernel(n, hidden, order, first, *refs):
    left_head_ref, right_head_ref, *block_refs = refs[:-15]
    count_ref, gain_ref, bias_ref, project_wide_ref, out_wide_ref, gate_ref = refs[-15:-9]
    *stage_refs, x_ref = refs[-9:]
    weights = [ref[...] for ref in (gain_ref, bias_ref, project_wide_ref, out_wide_ref, gate_ref)]
    stage(n, hidden, order, first, block_refs, count_ref[0], *weights, stage_refs)
    left = jnp.concatenate([side_by_side(left_head_ref, n), side_by_side(stage_refs[0], n)], axis=1)
    right = jnp.concatenate([side_by_side(right_head_ref, n), side_by_side(stage_refs[1], n)], axis=1)
    x_ref[...] = jnp.zeros_like(x_ref)

    def store(row, value):
        x_ref[row, :] = value

    cross(n, hidden, order, left, right, 0, store)


def tail_kernel(n, hidden, order, cuts, *refs):
    blocks = len(order)
    block_refs, refs = refs[:blocks], refs[blocks:]
    head_refs, (project_wide_ref, out_wide_ref, pick_ref, own_ref), middle_refs = refs[:8], refs[8:12], refs[12:20]
    x_early_ref, *refs = refs[20:]
    count_ref, gain_ref, bias_ref, project_ref, gate_ref, out_gain_ref, out_bias_ref = refs[:7]
    update_ref, pair_ref, project_grad_ref, gate_grad_ref, out_grad_ref = refs[7:12]
    tail_refs, (square_ref, dgo_ref, dp_ref, x_ref, x_late_ref, dx_ref) = refs[12:20], refs[20:]
    stages = (head_refs, middle_refs, tail_refs)
    f32, bf16 = jnp.float32, jnp.bfloat16
    per = LANES // hidden
    groups = n // per
    wide = n * hidden
    rows = n // blocks
    gain, gate_weight, project_t = gain_ref[...], gate_ref[...], project_ref[...]
    weights = gain, bias_ref[...], project_wide_ref[...], out_wide_ref[...], gate_weight
    stage(n, hidden, order, cuts[1], block_refs[cuts[1] * per // rows :], count_ref[0], *weights, tail_refs)

    spans = [(low * n, high * n) for low, high in zip((0, *cuts), (*cuts, groups))]
    half = per // 2

    def put(ref, q, column, value):
        for low, high in spans:
            ref[pl.ds(low * half + q * (high - low), high - low), pl.ds(column, LANES)] = value[low:high]

    def sum_pairs(ref):
        znt = [refs[7][...].reshape(2 * LANES, half * (high - low)) for refs, (low, high) in zip(stages, spans)]
        rows_of = [ref[pl.ds(low * half, (high - low) * half), :] for low, high in spans]
        return sum(dot(a, b) for a, b in zip(znt, rows_of))

    def all_rows(k):
        return jnp.concatenate([refs[k][...] for refs in stages], axis=0)


    def lanes(flat):
        return jnp.concatenate([flat[g * n : (g + 1) * n] for g in range(groups)], axis=1)

    def flatten(rowed):
        return jnp.concatenate([rowed[:, g * LANES : (g + 1) * LANES] for g in range(groups)], axis=0)

    left, right = lanes(all_rows(0)), lanes(all_rows(1))

    split = cuts[1] * LANES
    x_ref[...] = jnp.zeros_like(x_ref)

    def store_late(row, value):
        x_late_ref[row, :] = value

    def store_both(row, value):
        x_ref[row, :] = value[:, :split]
        x_late_ref[row, :] = value[:, split:]

    cross(n, hidden, order, left[:, split:], right[:, :split], 0, store_late)
    cross(n, hidden, order, left, right[:, split:], split // hidden, store_both)
    x = jnp.concatenate([x_early_ref[...] + x_ref[...], x_late_ref[...]], axis=1)
    x = flatten(x.astype(bf16).astype(f32))

    zhat, zs = normalize(block_refs[0][pl.ds(0, rows * n), :].astype(f32))
    mean = jnp.where(iota((LANES, LANES), 0) // hidden == iota((LANES, LANES), 1) // hidden, 1.0 / hidden, 0.0)
    mean = mean.astype(bf16)
    mean_twice = jnp.concatenate([mean, mean], axis=0)
    out_gain = jnp.concatenate([out_gain_ref[...]] * per, axis=1)
    out_bias = jnp.concatenate([out_bias_ref[...]] * per, axis=1)
    centered = x - dot(x.astype(bf16), mean)
    xs = lax.rsqrt(dot_split(centered * centered, mean_twice) + 1e-05)
    xhat = centered * xs
    xn = (xhat * out_gain + out_bias).astype(bf16)

    u = out_gain * all_rows(6)
    dx = xs * (u - dot_split(u, mean_twice) - xhat * dot_split(u * xhat, mean_twice))
    dx_ref[...] = lanes(dx.astype(bf16)).astype(f32)

    same = iota((hidden, wide), 0) == iota((hidden, wide), 1) % hidden
    for t in range(n):
        row = dx_ref[pl.ds(row_of(order, rows, t), 1), :]
        row = jnp.broadcast_to(row, (hidden, wide)).astype(bf16)
        square_ref[pl.ds(t * hidden, hidden), :] = jnp.where(same, row, jnp.zeros_like(row))
    y_all = dot(xn, out_wide_ref[...])
    own_dgo = []
    for p in range(per):
        y = y_all[:, p * LANES : (p + 1) * LANES]
        dgo = (jnp.concatenate([refs[5][p] for refs in stages], axis=0) * y).astype(bf16)
        put(dgo_ref, p % half, p // half * LANES, dgo)
        if p < rows:
            update_ref[p] = (own_ref[p] * y[:n]).astype(bf16)
            own_dgo.append(dgo[:n])
    diagonal = square_ref[...]
    dleft = flatten(dot(right, diagonal).astype(bf16)).astype(f32)
    dright = flatten(dot(left, diagonal, NT).astype(bf16)).astype(f32)
    xnt, dy = xn.T, all_rows(4)
    out_grad = [dot(xnt[p * hidden : (p + 1) * hidden], dy[:, p * LANES : (p + 1) * LANES]) for p in range(per)]
    out_grad_ref[...] = sum(out_grad) / n
    gate_grad = sum_pairs(dgo_ref)
    gate_grad_ref[...] = (gate_grad[:LANES, :LANES] + gate_grad[LANES:, LANES:]) / n

    dp = []
    for side, grad in enumerate((dleft, dright)):
        masked = grad * jnp.concatenate([refs[2][side] for refs in stages], axis=0)
        dp += [masked, masked * jnp.concatenate([refs[3][side] for refs in stages], axis=0)]
    dp = jnp.concatenate([d.astype(bf16) for d in dp], axis=1)
    by_place = dot(dp, pick_ref[...]).astype(bf16)
    for q in range(half):
        put(dp_ref, q, 0, by_place[:, q * LANES : (q + 1) * LANES])
    tiled = [project_t[kind * hidden : (kind + 1) * hidden] for kind in range(KINDS) for _ in range(per)]
    place = iota((n, KINDS * LANES), 1) % LANES // hidden
    dp_rows = [jnp.where(place == r, dp[:n], jnp.zeros_like(dp[:n])) for r in range(rows)]
    dzn = dot(jnp.concatenate(dp_rows, axis=0), jnp.concatenate(tiled, axis=0))
    dzn += dot(jnp.concatenate(own_dgo, axis=0), gate_weight, NT)
    u = gain * dzn
    first = jnp.mean(u, axis=-1, keepdims=True)
    second = jnp.mean(u * zhat, axis=-1, keepdims=True)
    pair_grad = zs * (u - first - zhat * second)
    for r in range(rows):
        pair_ref[r] = pair_grad[r * n : (r + 1) * n]

    project_grad = sum_pairs(dp_ref).T
    width = KINDS * hidden
    project_grad_ref[...] = (project_grad[:width, :LANES] + project_grad[width:, LANES:]) / n


def body_whole(
    devices,
    pair_acts,
    token_count,
    input_gain,
    input_bias,
    project_weight,
    gate_weight,
    output_norm_gain,
    output_shift_bias,
    output_weight,
    update_grad,
):
    rows, n, channels = pair_acts.shape
    hidden = output_weight.shape[0]
    f32, bf16 = jnp.float32, jnp.bfloat16
    half = rows * n
    vmem, anywhere = pl.BlockSpec(memory_space=pltpu.VMEM), pl.BlockSpec(memory_space=pl.ANY)
    shape = jax.ShapeDtypeStruct
    sources = [
        pair_acts.reshape(half, channels),
        update_grad.reshape(half, channels),
        input_gain[None],
        input_bias[None],
        project_weight.T,
        gate_weight,
        output_norm_gain[None],
        output_shift_bias[None],
        output_weight,
    ]
    send, gain, bias, project_t, gate_weight, out_gain, out_bias, out_weight = pl.pallas_call(
        load_kernel,
        out_shape=[pltpu.VMEM((2 * half, channels), bf16)] + [pltpu.VMEM(v.shape, v.dtype) for v in sources[2:]],
        in_specs=[anywhere] * len(sources),
        out_specs=[vmem] * (len(sources) - 1),
        scratch_shapes=[pltpu.SemaphoreType.DMA((len(sources),))],
        name="load",
    )(*sources)
    blocks = {0: send}
    core, x, *z = [1 << bit for bit in range(devices.bit_length() - 1)]

    def hop(step, sources):
        pairs = [(i, i ^ step) for i in range(devices)]
        for d in sources:
            blocks[d ^ step] = lax.ppermute(blocks[d], "row", pairs)

    for step in reversed(z):
        hop(step, [0])
        if step == z[-1]:
            hop(x, [0])
    for k, step in enumerate(z[:-1]):
        hop(step, [x])
        hop(step, [d for d in list(blocks) if 0 < d and d % (2 * step) == 0])
    hop(x, [d for d in list(blocks) if not d & x and d ^ x not in blocks])
    last = devices - 1 - core
    hop(core, [d for d in list(blocks) if d != last])
    order = sorted(range(devices), key=lambda d: (2 * d.bit_count() + (d & x) / x, -(d & core), -d))
    ordered = [blocks.get(d) for d in order]
    per = LANES // hidden
    groups = n // per
    cuts = (groups // 2, groups - 1)

    def stage_out(count):
        tall = count * n
        return (
            pltpu.VMEM((tall, LANES), bf16),
            pltpu.VMEM((tall, LANES), bf16),
            pltpu.VMEM((2, tall, LANES), f32),
            pltpu.VMEM((2, tall, LANES), f32),
            pltpu.VMEM((tall, per * channels), bf16),
            pltpu.VMEM((per, tall, channels), f32),
            pltpu.VMEM((tall, LANES), f32),
            pltpu.VMEM((2, channels, per // 2 * tall), bf16),
        )

    def span(first, last):
        return ordered[first * per // rows : -(-last * per // rows)]

    head_in = [*span(0, cuts[0]), token_count, gain, bias, project_t, gate_weight, out_weight]
    smem = pl.BlockSpec(memory_space=pltpu.SMEM)
    head_out = (
        *stage_out(cuts[0]),
        pltpu.VMEM((KINDS * LANES, per * channels), bf16),
        pltpu.VMEM((LANES, per * channels), bf16),
        pltpu.VMEM((KINDS * LANES, per // 2 * LANES), bf16),
        pltpu.VMEM((rows, n, channels), f32),
    )
    head = pl.pallas_call(
        functools.partial(head_kernel, n, hidden, order),
        out_shape=head_out,
        in_specs=[vmem] * (len(head_in) - 6) + [smem] + [vmem] * 5,
        out_specs=(vmem,) * len(head_out),
        compiler_params=pltpu.CompilerParams(vmem_limit_bytes=16 << 20),
        name="head",
    )(*head_in)
    blocks[last], head = lax.optimization_barrier((blocks[last], head))
    hop(core, [last])
    ordered = [blocks[d] for d in order]
    middle_in = [head[0], head[1], *span(*cuts), token_count, gain, bias, head[8], head[9], gate_weight]
    middle_out = (*stage_out(cuts[1] - cuts[0]), pltpu.VMEM((n, cuts[1] * LANES), f32))
    middle = pl.pallas_call(
        functools.partial(middle_kernel, n, hidden, order, cuts[0]),
        out_shape=middle_out,
        in_specs=[vmem] * (len(middle_in) - 6) + [smem] + [vmem] * 5,
        out_specs=(vmem,) * len(middle_out),
        compiler_params=pltpu.CompilerParams(vmem_limit_bytes=16 << 20),
        name="middle",
    )(*middle_in)
    tall = groups * n
    update, pair_grad, project_grad, gate_grad, output_grad = pl.pallas_call(
        functools.partial(tail_kernel, n, hidden, order, cuts),
        out_shape=(
            shape((rows, n, channels), bf16),
            shape((rows, n, channels), f32),
            shape((KINDS * hidden, channels), f32),
            shape((channels, channels), f32),
            shape((hidden, channels), f32),
        ),
        in_specs=[vmem] * (devices + len(head) + len(middle)) + [smem] + [vmem] * 6,
        out_specs=(vmem,) * 5,
        scratch_shapes=[
            *stage_out(groups - cuts[1]),
            pltpu.VMEM((n * hidden, n * hidden), bf16),
            pltpu.VMEM((per // 2 * tall, 2 * channels), bf16),
            pltpu.VMEM((per // 2 * tall, LANES), bf16),
            pltpu.VMEM((n, cuts[1] * LANES), f32),
            pltpu.VMEM((n, (groups - cuts[1]) * LANES), f32),
            pltpu.VMEM((n, n * hidden), f32),
        ],
        compiler_params=pltpu.CompilerParams(vmem_limit_bytes=32 << 20),
        name="tail",
    )(*ordered, *head, *middle, token_count, gain, bias, project_t, gate_weight, out_gain, out_bias)
    return update, pair_grad, project_grad.T, gate_grad, output_grad


def layer_normalize(values, norm_gain, norm_bias, reduce_axis):
    average = jnp.mean(values, axis=reduce_axis, keepdims=True)
    centered = values - average
    variance = jnp.mean(centered * centered, axis=reduce_axis, keepdims=True)
    inv_std = lax.rsqrt(variance + 1e-05)
    normed = centered * inv_std
    return (normed * norm_gain + norm_bias, normed, inv_std)


def norm_backward_pass(upstream, normed, inv_std, norm_gain, reduce_axis):
    scaled = upstream * norm_gain
    first = jnp.mean(scaled, axis=reduce_axis, keepdims=True)
    second = jnp.mean(scaled * normed, axis=reduce_axis, keepdims=True)
    return inv_std * (scaled - first - normed * second)


def body(
    pair_acts,
    token_count,
    input_gain,
    input_bias,
    project_weight,
    gate_weight,
    output_norm_gain,
    output_shift_bias,
    output_weight,
    update_grad,
):
    single_float_format = jnp.float32
    brain_float_sixteen = jnp.bfloat16
    row_count, length, channels = pair_acts.shape
    hidden = output_weight.shape[0]
    row_start = lax.axis_index("row") * row_count
    live_limit = token_count[0]
    row_live = (row_start + jnp.arange(row_count, dtype=jnp.int32) < live_limit).astype(
        single_float_format
    )
    col_live = (jnp.arange(length, dtype=jnp.int32) < live_limit).astype(single_float_format)
    live_mask = row_live[:, None] * col_live[None, :]
    zn32, zhat, zscale = layer_normalize(
        pair_acts.astype(single_float_format), input_gain, input_bias, -1
    )
    normed_pair = zn32.astype(brain_float_sixteen)
    projected = jnp.einsum(
        "rkd,de->erk", normed_pair, project_weight, preferred_element_type=single_float_format
    ).reshape(4, hidden, row_count, length)
    gate_left = jax.nn.sigmoid(projected[1])
    gate_right = jax.nn.sigmoid(projected[3])
    left_panel = (live_mask * gate_left * projected[0]).astype(brain_float_sixteen)
    right_panel = (live_mask * gate_right * projected[2]).astype(brain_float_sixteen)
    stacked = jnp.stack([left_panel, right_panel], axis=1)
    columns = lax.all_to_all(stacked, "row", split_axis=0, concat_axis=2, tiled=True)
    left_cols = columns[:, 0]
    right_cols = columns[:, 1]
    products = jnp.einsum(
        "cik,cjk->cij", left_cols, right_cols, preferred_element_type=single_float_format
    ).astype(brain_float_sixteen)
    triangle_product = lax.all_to_all(products, "row", split_axis=1, concat_axis=0, tiled=True)
    normed_input_single, standardized_input, input_inverse_scale = layer_normalize(
        triangle_product.astype(single_float_format),
        output_norm_gain[:, None, None],
        output_shift_bias[:, None, None],
        0,
    )
    normed_tri = normed_input_single.astype(brain_float_sixteen)
    mixed = jnp.einsum(
        "crk,cd->rkd", normed_tri, output_weight, preferred_element_type=single_float_format
    )
    gate_out = jax.nn.sigmoid(
        jnp.einsum(
            "rkd,de->rke", normed_pair, gate_weight, preferred_element_type=single_float_format
        )
    )
    update = (gate_out * mixed).astype(brain_float_sixteen)
    cotangent = update_grad.astype(single_float_format)
    mixed_grad = (cotangent * gate_out).astype(brain_float_sixteen)
    gate_logit_grad = (cotangent * mixed * gate_out * (1.0 - gate_out)).astype(brain_float_sixteen)
    output_terms = jnp.einsum(
        "crk,rkd->cd", normed_tri, mixed_grad, preferred_element_type=single_float_format
    )
    triangle_normed_gradient = jnp.einsum(
        "rkd,cd->crk", mixed_grad, output_weight, preferred_element_type=single_float_format
    )
    triangle_gradient = norm_backward_pass(
        triangle_normed_gradient,
        standardized_input,
        input_inverse_scale,
        output_norm_gain[:, None, None],
        0,
    ).astype(brain_float_sixteen)
    grad_cols = lax.all_to_all(triangle_gradient, "row", split_axis=0, concat_axis=1, tiled=True)
    left_col_grad = jnp.einsum(
        "cij,cjk->cik", grad_cols, right_cols, preferred_element_type=single_float_format
    ).astype(brain_float_sixteen)
    right_col_grad = jnp.einsum(
        "cij,cik->cjk", grad_cols, left_cols, preferred_element_type=single_float_format
    ).astype(brain_float_sixteen)
    returned = lax.all_to_all(
        jnp.stack([left_col_grad, right_col_grad], axis=1),
        "row",
        split_axis=2,
        concat_axis=0,
        tiled=True,
    )
    left_grad = returned[:, 0].astype(single_float_format)
    right_grad = returned[:, 1].astype(single_float_format)
    project_terms = jnp.stack(
        [
            left_grad * live_mask * gate_left,
            left_grad * live_mask * projected[0] * gate_left * (1.0 - gate_left),
            right_grad * live_mask * gate_right,
            right_grad * live_mask * projected[2] * gate_right * (1.0 - gate_right),
        ]
    )
    project_terms = project_terms.astype(brain_float_sixteen).reshape(4 * hidden, row_count, length)
    project_part = jnp.einsum(
        "rkd,erk->de", normed_pair, project_terms, preferred_element_type=single_float_format
    )
    gate_part = jnp.einsum(
        "rkd,rke->de", normed_pair, gate_logit_grad, preferred_element_type=single_float_format
    )
    totals = lax.psum((project_part, gate_part, output_terms), "row")
    project_grad = totals[0] / length
    gate_grad = totals[1] / length
    output_grad = totals[2] / length
    normed_grad = jnp.einsum(
        "erk,de->rkd", project_terms, project_weight, preferred_element_type=single_float_format
    ) + jnp.einsum(
        "rke,de->rkd", gate_logit_grad, gate_weight, preferred_element_type=single_float_format
    )
    pair_grad = norm_backward_pass(normed_grad, zhat, zscale, input_gain, -1)
    return (update, pair_grad, project_grad, gate_grad, output_grad)


def fits_whole(mesh, args):
    pair_acts, output_weight = args[0], args[8]
    devices = mesh.shape["row"]
    length, channels = pair_acts.shape[0] // mesh.shape["grp"], pair_acts.shape[2]
    hidden = output_weight.shape[0]
    return (
        channels == LANES
        and hidden % 16 == 0
        and LANES % hidden == 0
        and length % (LANES // hidden) == 0
        and (LANES // hidden) % 8 == 0
        and length % 16 == 0
        and length % devices == 0
        and length // devices <= LANES // hidden
        and devices in (8, 16)
        and 2 * KINDS * hidden == LANES
        and length // (LANES // hidden) >= 4
        and length // 2 % (LANES // hidden) == 0
        and 2 * pair_acts.dtype.itemsize * length * length * channels <= WHOLE_BYTES
    )


def solution(mesh):
    in_specs = (
        P(("grp", "row"), None, None),
        P("grp"),
        P(),
        P(),
        P(),
        P(),
        P(),
        P(),
        P(),
        P(("grp", "row"), None, None),
    )
    out_specs = (
        P(("grp", "row"), None, None),
        P(("grp", "row"), None, None),
        P("grp", None),
        P("grp", None),
        P("grp", None),
    )
    devices = mesh.shape["row"]

    def run(*args):
        crop = functools.partial(body_whole, devices) if fits_whole(mesh, args) else body
        return jax.shard_map(crop, mesh=mesh, in_specs=in_specs, out_specs=out_specs, check_vma=False)(*args)

    return run
```

```python
import functools

import jax
import jax.numpy as jnp
from jax import lax
from jax.experimental import pallas as pl
from jax.experimental.pallas import tpu as pltpu
from jax.sharding import PartitionSpec as P

LANES = 128
KINDS = 4
WHOLE_BYTES = 4 << 20

NN = (((1,), (0,)), ((), ()))
NT = (((1,), (1,)), ((), ()))
TN = (((0,), (0,)), ((), ()))


def dot(a, b, dims=NN):
    return lax.dot_general(a, b, dims, preferred_element_type=jnp.float32)


def dot_split(a, b_twice):
    high = a.astype(jnp.bfloat16)
    low = (a - high.astype(jnp.float32)).astype(jnp.bfloat16)
    return dot(jnp.concatenate([high, low], axis=1), b_twice)


def iota(shape, dim):
    return lax.broadcasted_iota(jnp.int32, shape, dim)


def zero_one(condition):
    return jnp.where(condition, 1.0, 0.0).astype(jnp.bfloat16)


def sigmoid(v):
    return 1.0 / (1.0 + jnp.exp(-v))


def normalize(v):
    centered = v - jnp.mean(v, axis=-1, keepdims=True)
    s = lax.rsqrt(jnp.mean(centered * centered, axis=-1, keepdims=True) + 1e-05)
    return centered * s, s


def row_of(order, rows, t):
    return (lax.axis_index("row") ^ order[t // rows]) * rows + t % rows


def rows_of_lanes(order, rows, hidden, group):
    per = LANES // hidden
    place = iota((1, LANES), 1) // hidden
    at = jnp.full((1, LANES), row_of(order, rows, group * per), jnp.int32)
    for p in range(1, per):
        at = jnp.where(place == p, row_of(order, rows, group * per + p), at)
    return at


def stage(n, hidden, order, first, block_refs, count, gain, bias, project_wide, out_wide, gate_weight, refs):
    left_ref, right_ref, mask_ref, slope_ref, dy_ref, dgo_part_ref, dxn_ref, znt_ref = refs
    f32, bf16 = jnp.float32, jnp.bfloat16
    per = LANES // hidden
    rows = n // len(order)
    tall = left_ref.shape[0]
    start = first * per
    zn, cotangent = {}, {}
    for t in range(start, start + per * (tall // n)):
        block, at = block_refs[t // rows - start // rows], t % rows * n
        zn[t] = (normalize(block[pl.ds(at, n), :].astype(f32))[0] * gain + bias).astype(bf16)
        cotangent[t] = block[pl.ds((rows + t % rows) * n, n), :]

    def place(tiles, p):
        return jnp.concatenate([tiles[t] for t in range(start + p, start + per * (tall // n), per)], axis=0)

    zn = [place(zn, p) for p in range(per)]
    projected = dot(jnp.concatenate(zn, axis=1), project_wide, NT)
    live_k = iota((n, LANES), 0) < count
    mask = [
        jnp.where(live_k & (rows_of_lanes(order, rows, hidden, first + g) < count), 1.0, 0.0) for g in range(tall // n)
    ]
    mask = jnp.concatenate(mask, axis=0)
    for side, ref in enumerate((left_ref, right_ref)):
        value = projected[:, 2 * side * LANES : (2 * side + 1) * LANES]
        gate = sigmoid(projected[:, (2 * side + 1) * LANES : (2 * side + 2) * LANES])
        ref[...] = (mask * gate * value).astype(bf16)
        mask_ref[side] = mask * gate
        slope_ref[side] = value * (1.0 - gate)
    own = []
    zn_tall = jnp.concatenate(zn, axis=0)
    gates = sigmoid(dot(zn_tall, gate_weight))
    for p in range(per):
        go = gates[p * tall : (p + 1) * tall]
        dy = place(cotangent, p).astype(f32) * go
        dy_ref[:, p * LANES : (p + 1) * LANES] = dy.astype(bf16)
        dgo_part_ref[p] = dy * (1.0 - go)
        own.append(go[:n])
    dxn_ref[...] = dot(dy_ref[...], out_wide, NT)
    half = per // 2 * tall
    znt_ref[0] = zn_tall[:half].T
    znt_ref[1] = zn_tall[half:].T
    return own


def wide_project(project_t, per):
    hidden, channels = project_t.shape[0] // KINDS, project_t.shape[1]
    columns = []
    for p in range(per):
        parts = []
        for kind in range(KINDS):
            before, after = p * hidden, (per - 1 - p) * hidden
            parts += [jnp.zeros((before, channels), project_t.dtype)] * (before > 0)
            parts += [project_t[kind * hidden : (kind + 1) * hidden]]
            parts += [jnp.zeros((after, channels), project_t.dtype)] * (after > 0)
        columns.append(jnp.concatenate(parts, axis=0))
    return jnp.concatenate(columns, axis=1)


def wide_out(out_weight, per):
    hidden, channels = out_weight.shape
    rows = []
    for p in range(per):
        before, after = p * channels, (per - 1 - p) * channels
        parts = [jnp.zeros((hidden, before), out_weight.dtype)] * (before > 0) + [out_weight]
        rows.append(jnp.concatenate(parts + [jnp.zeros((hidden, after), out_weight.dtype)] * (after > 0), axis=1))
    return jnp.concatenate(rows, axis=0)


def pick_place(per, hidden):
    half = per // 2
    rows = []
    for kind in range(KINDS):
        for p in range(per):
            column = (p // half * KINDS + kind) * hidden
            own = zero_one(iota((hidden, LANES), 1) == iota((hidden, LANES), 0) + column)
            before, after = p % half * LANES, (half - 1 - p % half) * LANES
            parts = [jnp.zeros((hidden, before), own.dtype)] * (before > 0) + [own]
            rows.append(jnp.concatenate(parts + [jnp.zeros((hidden, after), own.dtype)] * (after > 0), axis=1))
    return jnp.concatenate(rows, axis=0)


def load_kernel(*refs):
    count = len(refs) // 2
    sources, targets, sems = refs[:count], refs[count : 2 * count - 1], refs[-1]
    half = sources[0].shape[0]
    targets = [targets[0].at[pl.ds(0, half)], targets[0].at[pl.ds(half, half)], *targets[1:]]
    copies = [pltpu.make_async_copy(a, b, sems.at[k]) for k, (a, b) in enumerate(zip(sources, targets))]
    for copy in copies:
        copy.start()
    for copy in copies:
        copy.wait()


def cross(n, hidden, order, lefts, rights, first, store):
    wide = lefts.shape[1]
    same = iota((hidden, wide), 0) == iota((hidden, wide), 1) % hidden
    product = dot(rights, lefts, TN)
    for t in range(rights.shape[1] // hidden):
        own = jnp.where(same, product[t * hidden : (t + 1) * hidden], 0.0)
        store(pl.ds(row_of(order, n // len(order), first + t), 1), jnp.sum(own, axis=0, keepdims=True))


def side_by_side(ref, n):
    return jnp.concatenate([ref[pl.ds(g * n, n), :] for g in range(ref.shape[0] // n)], axis=1)


def head_kernel(n, hidden, order, *refs):
    *block_refs, count_ref, gain_ref, bias_ref, project_ref, gate_ref, out_weight_ref = refs[:-12]
    *stage_refs, project_wide_ref, out_wide_ref, pick_ref, own_ref = refs[-12:]
    per = LANES // hidden
    project_wide_ref[...] = wide_project(project_ref[...], per)
    out_wide_ref[...] = wide_out(out_weight_ref[...], per)
    pick_ref[...] = pick_place(per, hidden)
    weights = [ref[...] for ref in (gain_ref, bias_ref, project_wide_ref, out_wide_ref, gate_ref)]
    own = stage(n, hidden, order, 0, block_refs, count_ref[0], *weights, stage_refs)
    for r in range(own_ref.shape[0]):
        own_ref[r] = own[r]


def middle_kernel(n, hidden, order, first, *refs):
    left_head_ref, right_head_ref, *block_refs = refs[:-15]
    count_ref, gain_ref, bias_ref, project_wide_ref, out_wide_ref, gate_ref = refs[-15:-9]
    *stage_refs, x_ref = refs[-9:]
    weights = [ref[...] for ref in (gain_ref, bias_ref, project_wide_ref, out_wide_ref, gate_ref)]
    stage(n, hidden, order, first, block_refs, count_ref[0], *weights, stage_refs)
    left = jnp.concatenate([side_by_side(left_head_ref, n), side_by_side(stage_refs[0], n)], axis=1)
    right = jnp.concatenate([side_by_side(right_head_ref, n), side_by_side(stage_refs[1], n)], axis=1)
    x_ref[...] = jnp.zeros_like(x_ref)

    def store(row, value):
        x_ref[row, :] = value

    cross(n, hidden, order, left, right, 0, store)


def tail_kernel(n, hidden, order, cuts, *refs):
    blocks = len(order)
    block_refs, refs = refs[:blocks], refs[blocks:]
    head_refs, (project_wide_ref, out_wide_ref, pick_ref, own_ref), middle_refs = refs[:8], refs[8:12], refs[12:20]
    x_early_ref, *refs = refs[20:]
    count_ref, gain_ref, bias_ref, project_ref, gate_ref, out_gain_ref, out_bias_ref = refs[:7]
    update_ref, pair_ref, project_grad_ref, gate_grad_ref, out_grad_ref = refs[7:12]
    tail_refs, (square_ref, dgo_ref, dp_ref, x_ref, x_late_ref, dx_ref) = refs[12:20], refs[20:]
    stages = (head_refs, middle_refs, tail_refs)
    f32, bf16 = jnp.float32, jnp.bfloat16
    per = LANES // hidden
    groups = n // per
    wide = n * hidden
    rows = n // blocks
    gain, gate_weight, project_t = gain_ref[...], gate_ref[...], project_ref[...]
    weights = gain, bias_ref[...], project_wide_ref[...], out_wide_ref[...], gate_weight
    stage(n, hidden, order, cuts[1], block_refs[cuts[1] * per // rows :], count_ref[0], *weights, tail_refs)

    spans = [(low * n, high * n) for low, high in zip((0, *cuts), (*cuts, groups))]
    half = per // 2

    def put(ref, q, column, value):
        for low, high in spans:
            ref[pl.ds(low * half + q * (high - low), high - low), pl.ds(column, LANES)] = value[low:high]

    def sum_pairs(ref):
        znt = [refs[7][...].reshape(2 * LANES, half * (high - low)) for refs, (low, high) in zip(stages, spans)]
        rows_of = [ref[pl.ds(low * half, (high - low) * half), :] for low, high in spans]
        return sum(dot(a, b) for a, b in zip(znt, rows_of))

    def all_rows(k):
        return jnp.concatenate([refs[k][...] for refs in stages], axis=0)


    def lanes(flat):
        return jnp.concatenate([flat[g * n : (g + 1) * n] for g in range(groups)], axis=1)

    def flatten(rowed):
        return jnp.concatenate([rowed[:, g * LANES : (g + 1) * LANES] for g in range(groups)], axis=0)

    left, right = lanes(all_rows(0)), lanes(all_rows(1))

    split = cuts[1] * LANES
    x_ref[...] = jnp.zeros_like(x_ref)

    def store_late(row, value):
        x_late_ref[row, :] = value

    def store_both(row, value):
        x_ref[row, :] = value[:, :split]
        x_late_ref[row, :] = value[:, split:]

    cross(n, hidden, order, left[:, split:], right[:, :split], 0, store_late)
    cross(n, hidden, order, left, right[:, split:], split // hidden, store_both)
    x = jnp.concatenate([x_early_ref[...] + x_ref[...], x_late_ref[...]], axis=1)
    x = flatten(x.astype(bf16).astype(f32))

    mean = jnp.where(iota((LANES, LANES), 0) // hidden == iota((LANES, LANES), 1) // hidden, 1.0 / hidden, 0.0)
    mean = mean.astype(bf16)
    mean_twice = jnp.concatenate([mean, mean], axis=0)
    out_gain = jnp.concatenate([out_gain_ref[...]] * per, axis=1)
    out_bias = jnp.concatenate([out_bias_ref[...]] * per, axis=1)
    centered = x - dot(x.astype(bf16), mean)
    xs = lax.rsqrt(dot_split(centered * centered, mean_twice) + 1e-05)
    xhat = centered * xs
    xn = (xhat * out_gain + out_bias).astype(bf16)

    u = out_gain * all_rows(6)
    dx = xs * (u - dot_split(u, mean_twice) - xhat * dot_split(u * xhat, mean_twice))
    dx_ref[...] = lanes(dx.astype(bf16)).astype(f32)

    same = iota((hidden, wide), 0) == iota((hidden, wide), 1) % hidden
    for t in range(n):
        row = dx_ref[pl.ds(row_of(order, rows, t), 1), :]
        row = jnp.broadcast_to(row, (hidden, wide)).astype(bf16)
        square_ref[pl.ds(t * hidden, hidden), :] = jnp.where(same, row, jnp.zeros_like(row))
    y_all = dot(xn, out_wide_ref[...])
    own_dgo = []
    for p in range(per):
        y = y_all[:, p * LANES : (p + 1) * LANES]
        dgo = (jnp.concatenate([refs[5][p] for refs in stages], axis=0) * y).astype(bf16)
        put(dgo_ref, p % half, p // half * LANES, dgo)
        if p < rows:
            update_ref[p] = (own_ref[p] * y[:n]).astype(bf16)
            own_dgo.append(dgo[:n])
    diagonal = square_ref[...]
    dleft = flatten(dot(right, diagonal).astype(bf16)).astype(f32)
    dright = flatten(dot(left, diagonal, NT).astype(bf16)).astype(f32)
    xnt, dy = xn.T, all_rows(4)
    out_grad = [dot(xnt[p * hidden : (p + 1) * hidden], dy[:, p * LANES : (p + 1) * LANES]) for p in range(per)]
    out_grad_ref[...] = sum(out_grad) / n
    gate_grad = sum_pairs(dgo_ref)
    gate_grad_ref[...] = (gate_grad[:LANES, :LANES] + gate_grad[LANES:, LANES:]) / n

    dp = []
    for side, grad in enumerate((dleft, dright)):
        masked = grad * jnp.concatenate([refs[2][side] for refs in stages], axis=0)
        dp += [masked, masked * jnp.concatenate([refs[3][side] for refs in stages], axis=0)]
    dp = jnp.concatenate([d.astype(bf16) for d in dp], axis=1)
    by_place = dot(dp, pick_ref[...]).astype(bf16)
    for q in range(half):
        put(dp_ref, q, 0, by_place[:, q * LANES : (q + 1) * LANES])
    tiled = [project_t[kind * hidden : (kind + 1) * hidden] for kind in range(KINDS) for _ in range(per)]
    place = iota((n, KINDS * LANES), 1) % LANES // hidden
    dp_rows = [jnp.where(place == r, dp[:n], jnp.zeros_like(dp[:n])) for r in range(rows)]
    dzn = dot(jnp.concatenate(dp_rows, axis=0), jnp.concatenate(tiled, axis=0))
    dzn += dot(jnp.concatenate(own_dgo, axis=0), gate_weight, NT)
    zhat, zs = normalize(block_refs[0][pl.ds(0, rows * n), :].astype(f32))
    u = gain * dzn
    first = jnp.mean(u, axis=-1, keepdims=True)
    second = jnp.mean(u * zhat, axis=-1, keepdims=True)
    pair_grad = zs * (u - first - zhat * second)
    for r in range(rows):
        pair_ref[r] = pair_grad[r * n : (r + 1) * n]

    project_grad = sum_pairs(dp_ref).T
    width = KINDS * hidden
    project_grad_ref[...] = (project_grad[:width, :LANES] + project_grad[width:, LANES:]) / n


def body_whole(
    devices,
    pair_acts,
    token_count,
    input_gain,
    input_bias,
    project_weight,
    gate_weight,
    output_norm_gain,
    output_shift_bias,
    output_weight,
    update_grad,
):
    rows, n, channels = pair_acts.shape
    hidden = output_weight.shape[0]
    f32, bf16 = jnp.float32, jnp.bfloat16
    half = rows * n
    vmem, anywhere = pl.BlockSpec(memory_space=pltpu.VMEM), pl.BlockSpec(memory_space=pl.ANY)
    shape = jax.ShapeDtypeStruct
    sources = [
        pair_acts.reshape(half, channels),
        update_grad.reshape(half, channels),
        input_gain[None],
        input_bias[None],
        project_weight.T,
        gate_weight,
        output_norm_gain[None],
        output_shift_bias[None],
        output_weight,
    ]
    send, gain, bias, project_t, gate_weight, out_gain, out_bias, out_weight = pl.pallas_call(
        load_kernel,
        out_shape=[pltpu.VMEM((2 * half, channels), bf16)] + [pltpu.VMEM(v.shape, v.dtype) for v in sources[2:]],
        in_specs=[anywhere] * len(sources),
        out_specs=[vmem] * (len(sources) - 1),
        scratch_shapes=[pltpu.SemaphoreType.DMA((len(sources),))],
        name="load",
    )(*sources)
    blocks = {0: send}
    core, x, *z = [1 << bit for bit in range(devices.bit_length() - 1)]

    def hop(step, sources):
        pairs = [(i, i ^ step) for i in range(devices)]
        for d in sources:
            blocks[d ^ step] = lax.ppermute(blocks[d], "row", pairs)

    for step in reversed(z):
        hop(step, [0])
        if step == z[-1]:
            hop(x, [0])
    for k, step in enumerate(z[:-1]):
        hop(step, [d for d in list(blocks) if 0 < d and d % (2 * step) == 0])
    hop(x, [d for d in list(blocks) if not d & x and d ^ x not in blocks])
    last = devices - 1 - core
    hop(core, [d for d in list(blocks) if d != last])
    order = sorted(range(devices), key=lambda d: (2 * d.bit_count() + (d & x) / x, -(d & core), -d))
    ordered = [blocks.get(d) for d in order]
    per = LANES // hidden
    groups = n // per
    cuts = (groups // 2, groups - 1)

    def stage_out(count):
        tall = count * n
        return (
            pltpu.VMEM((tall, LANES), bf16),
            pltpu.VMEM((tall, LANES), bf16),
            pltpu.VMEM((2, tall, LANES), f32),
            pltpu.VMEM((2, tall, LANES), f32),
            pltpu.VMEM((tall, per * channels), bf16),
            pltpu.VMEM((per, tall, channels), f32),
            pltpu.VMEM((tall, LANES), f32),
            pltpu.VMEM((2, channels, per // 2 * tall), bf16),
        )

    def span(first, last):
        return ordered[first * per // rows : -(-last * per // rows)]

    head_in = [*span(0, cuts[0]), token_count, gain, bias, project_t, gate_weight, out_weight]
    smem = pl.BlockSpec(memory_space=pltpu.SMEM)
    head_out = (
        *stage_out(cuts[0]),
        pltpu.VMEM((KINDS * LANES, per * channels), bf16),
        pltpu.VMEM((LANES, per * channels), bf16),
        pltpu.VMEM((KINDS * LANES, per // 2 * LANES), bf16),
        pltpu.VMEM((rows, n, channels), f32),
    )
    head = pl.pallas_call(
        functools.partial(head_kernel, n, hidden, order),
        out_shape=head_out,
        in_specs=[vmem] * (len(head_in) - 6) + [smem] + [vmem] * 5,
        out_specs=(vmem,) * len(head_out),
        compiler_params=pltpu.CompilerParams(vmem_limit_bytes=16 << 20),
        name="head",
    )(*head_in)
    blocks[last], head = lax.optimization_barrier((blocks[last], head))
    hop(core, [last])
    ordered = [blocks[d] for d in order]
    middle_in = [head[0], head[1], *span(*cuts), token_count, gain, bias, head[8], head[9], gate_weight]
    middle_out = (*stage_out(cuts[1] - cuts[0]), pltpu.VMEM((n, cuts[1] * LANES), f32))
    middle = pl.pallas_call(
        functools.partial(middle_kernel, n, hidden, order, cuts[0]),
        out_shape=middle_out,
        in_specs=[vmem] * (len(middle_in) - 6) + [smem] + [vmem] * 5,
        out_specs=(vmem,) * len(middle_out),
        compiler_params=pltpu.CompilerParams(vmem_limit_bytes=16 << 20),
        name="middle",
    )(*middle_in)
    tall = groups * n
    update, pair_grad, project_grad, gate_grad, output_grad = pl.pallas_call(
        functools.partial(tail_kernel, n, hidden, order, cuts),
        out_shape=(
            shape((rows, n, channels), bf16),
            shape((rows, n, channels), f32),
            shape((KINDS * hidden, channels), f32),
            shape((channels, channels), f32),
            shape((hidden, channels), f32),
        ),
        in_specs=[vmem] * (devices + len(head) + len(middle)) + [smem] + [vmem] * 6,
        out_specs=(vmem,) * 5,
        scratch_shapes=[
            *stage_out(groups - cuts[1]),
            pltpu.VMEM((n * hidden, n * hidden), bf16),
            pltpu.VMEM((per // 2 * tall, 2 * channels), bf16),
            pltpu.VMEM((per // 2 * tall, LANES), bf16),
            pltpu.VMEM((n, cuts[1] * LANES), f32),
            pltpu.VMEM((n, (groups - cuts[1]) * LANES), f32),
            pltpu.VMEM((n, n * hidden), f32),
        ],
        compiler_params=pltpu.CompilerParams(vmem_limit_bytes=32 << 20),
        name="tail",
    )(*ordered, *head, *middle, token_count, gain, bias, project_t, gate_weight, out_gain, out_bias)
    return update, pair_grad, project_grad.T, gate_grad, output_grad


def layer_normalize(values, norm_gain, norm_bias, reduce_axis):
    average = jnp.mean(values, axis=reduce_axis, keepdims=True)
    centered = values - average
    variance = jnp.mean(centered * centered, axis=reduce_axis, keepdims=True)
    inv_std = lax.rsqrt(variance + 1e-05)
    normed = centered * inv_std
    return (normed * norm_gain + norm_bias, normed, inv_std)


def norm_backward_pass(upstream, normed, inv_std, norm_gain, reduce_axis):
    scaled = upstream * norm_gain
    first = jnp.mean(scaled, axis=reduce_axis, keepdims=True)
    second = jnp.mean(scaled * normed, axis=reduce_axis, keepdims=True)
    return inv_std * (scaled - first - normed * second)


def body(
    pair_acts,
    token_count,
    input_gain,
    input_bias,
    project_weight,
    gate_weight,
    output_norm_gain,
    output_shift_bias,
    output_weight,
    update_grad,
):
    single_float_format = jnp.float32
    brain_float_sixteen = jnp.bfloat16
    row_count, length, channels = pair_acts.shape
    hidden = output_weight.shape[0]
    row_start = lax.axis_index("row") * row_count
    live_limit = token_count[0]
    row_live = (row_start + jnp.arange(row_count, dtype=jnp.int32) < live_limit).astype(
        single_float_format
    )
    col_live = (jnp.arange(length, dtype=jnp.int32) < live_limit).astype(single_float_format)
    live_mask = row_live[:, None] * col_live[None, :]
    zn32, zhat, zscale = layer_normalize(
        pair_acts.astype(single_float_format), input_gain, input_bias, -1
    )
    normed_pair = zn32.astype(brain_float_sixteen)
    projected = jnp.einsum(
        "rkd,de->erk", normed_pair, project_weight, preferred_element_type=single_float_format
    ).reshape(4, hidden, row_count, length)
    gate_left = jax.nn.sigmoid(projected[1])
    gate_right = jax.nn.sigmoid(projected[3])
    left_panel = (live_mask * gate_left * projected[0]).astype(brain_float_sixteen)
    right_panel = (live_mask * gate_right * projected[2]).astype(brain_float_sixteen)
    stacked = jnp.stack([left_panel, right_panel], axis=1)
    columns = lax.all_to_all(stacked, "row", split_axis=0, concat_axis=2, tiled=True)
    left_cols = columns[:, 0]
    right_cols = columns[:, 1]
    products = jnp.einsum(
        "cik,cjk->cij", left_cols, right_cols, preferred_element_type=single_float_format
    ).astype(brain_float_sixteen)
    triangle_product = lax.all_to_all(products, "row", split_axis=1, concat_axis=0, tiled=True)
    normed_input_single, standardized_input, input_inverse_scale = layer_normalize(
        triangle_product.astype(single_float_format),
        output_norm_gain[:, None, None],
        output_shift_bias[:, None, None],
        0,
    )
    normed_tri = normed_input_single.astype(brain_float_sixteen)
    mixed = jnp.einsum(
        "crk,cd->rkd", normed_tri, output_weight, preferred_element_type=single_float_format
    )
    gate_out = jax.nn.sigmoid(
        jnp.einsum(
            "rkd,de->rke", normed_pair, gate_weight, preferred_element_type=single_float_format
        )
    )
    update = (gate_out * mixed).astype(brain_float_sixteen)
    cotangent = update_grad.astype(single_float_format)
    mixed_grad = (cotangent * gate_out).astype(brain_float_sixteen)
    gate_logit_grad = (cotangent * mixed * gate_out * (1.0 - gate_out)).astype(brain_float_sixteen)
    output_terms = jnp.einsum(
        "crk,rkd->cd", normed_tri, mixed_grad, preferred_element_type=single_float_format
    )
    triangle_normed_gradient = jnp.einsum(
        "rkd,cd->crk", mixed_grad, output_weight, preferred_element_type=single_float_format
    )
    triangle_gradient = norm_backward_pass(
        triangle_normed_gradient,
        standardized_input,
        input_inverse_scale,
        output_norm_gain[:, None, None],
        0,
    ).astype(brain_float_sixteen)
    grad_cols = lax.all_to_all(triangle_gradient, "row", split_axis=0, concat_axis=1, tiled=True)
    left_col_grad = jnp.einsum(
        "cij,cjk->cik", grad_cols, right_cols, preferred_element_type=single_float_format
    ).astype(brain_float_sixteen)
    right_col_grad = jnp.einsum(
        "cij,cik->cjk", grad_cols, left_cols, preferred_element_type=single_float_format
    ).astype(brain_float_sixteen)
    returned = lax.all_to_all(
        jnp.stack([left_col_grad, right_col_grad], axis=1),
        "row",
        split_axis=2,
        concat_axis=0,
        tiled=True,
    )
    left_grad = returned[:, 0].astype(single_float_format)
    right_grad = returned[:, 1].astype(single_float_format)
    project_terms = jnp.stack(
        [
            left_grad * live_mask * gate_left,
            left_grad * live_mask * projected[0] * gate_left * (1.0 - gate_left),
            right_grad * live_mask * gate_right,
            right_grad * live_mask * projected[2] * gate_right * (1.0 - gate_right),
        ]
    )
    project_terms = project_terms.astype(brain_float_sixteen).reshape(4 * hidden, row_count, length)
    project_part = jnp.einsum(
        "rkd,erk->de", normed_pair, project_terms, preferred_element_type=single_float_format
    )
    gate_part = jnp.einsum(
        "rkd,rke->de", normed_pair, gate_logit_grad, preferred_element_type=single_float_format
    )
    totals = lax.psum((project_part, gate_part, output_terms), "row")
    project_grad = totals[0] / length
    gate_grad = totals[1] / length
    output_grad = totals[2] / length
    normed_grad = jnp.einsum(
        "erk,de->rkd", project_terms, project_weight, preferred_element_type=single_float_format
    ) + jnp.einsum(
        "rke,de->rkd", gate_logit_grad, gate_weight, preferred_element_type=single_float_format
    )
    pair_grad = norm_backward_pass(normed_grad, zhat, zscale, input_gain, -1)
    return (update, pair_grad, project_grad, gate_grad, output_grad)


def fits_whole(mesh, args):
    pair_acts, output_weight = args[0], args[8]
    devices = mesh.shape["row"]
    length, channels = pair_acts.shape[0] // mesh.shape["grp"], pair_acts.shape[2]
    hidden = output_weight.shape[0]
    return (
        channels == LANES
        and hidden % 16 == 0
        and LANES % hidden == 0
        and length % (LANES // hidden) == 0
        and (LANES // hidden) % 8 == 0
        and length % 16 == 0
        and length % devices == 0
        and length // devices <= LANES // hidden
        and devices in (8, 16)
        and 2 * KINDS * hidden == LANES
        and length // (LANES // hidden) >= 4
        and length // 2 % (LANES // hidden) == 0
        and 2 * pair_acts.dtype.itemsize * length * length * channels <= WHOLE_BYTES
    )


def solution(mesh):
    in_specs = (
        P(("grp", "row"), None, None),
        P("grp"),
        P(),
        P(),
        P(),
        P(),
        P(),
        P(),
        P(),
        P(("grp", "row"), None, None),
    )
    out_specs = (
        P(("grp", "row"), None, None),
        P(("grp", "row"), None, None),
        P("grp", None),
        P("grp", None),
        P("grp", None),
    )
    devices = mesh.shape["row"]

    def run(*args):
        crop = functools.partial(body_whole, devices) if fits_whole(mesh, args) else body
        return jax.shard_map(crop, mesh=mesh, in_specs=in_specs, out_specs=out_specs, check_vma=False)(*args)

    return run
```
